512 devices in a mesh: dp: 16 (over z), latent: 8 (over y, core), section: 4 (over x).
Axes of the slice: x: 4, y: 4, z: 16, core: 2. Of those that a mesh axis runs over, the one named last changes fastest.
Arguments:
- activations: bfloat16 [16384, 4608], P(('latent', 'section'), 'dp'), may hold values from -6 to 6
- bias_dec: bfloat16 [4608], P('dp'), may hold values from -4 to 4
- encoder: bfloat16 [4608, 65536], P('dp', ('latent', 'section')), may hold values from -0.09375 to 0.09375
- decoder: bfloat16 [65536, 4608], P(('latent', 'section'), 'dp'), may hold values from -0.375 to 0.375
- active_blocks: int32 [16384, 4], P(('latent', 'section')), may hold values from 0 to 1023, all different within a row; in each aligned block of 512 rows (0 to 511, 512 to 1023, ...) at most 4 rows name the same one
Outputs:
- grad_decoder: bfloat16 [65536, 4608], P(('latent', 'section'), 'dp')
- row_loss: float32 [16384], P(('latent', 'section'))
The draws below stay inside these ranges and needn't reach their ends.
Inputs may be any that keep to these rules, and one draw needn't show every extreme that they name: `active_blocks`: each row names 4 different blocks; among the 512 rows of one device no block is named by more than 4 rows, and some block is named by exactly 4 of them.
All inputs are finite; a program needn't handle non-finite values.
Results may differ from the reference program's by a relative error of at most 0.0034.
Values may be sent and summed in bfloat16 or wider, within the bound.
No kernel may reach another device: no remote copies, remote signals or barrier semaphores. Data moves between devices by JAX's collectives and lax.ppermute only.
A program may use at most 64 MiB of HBM per device.

```python
import math
import jax
import jax.numpy as jnp
import numpy as np
from jax import lax

D = 4608
BLOCK = 64
BPG = 32
K_ACT = 4
ROW_DEV = 512
LATENTS = 65536
ROWS = 16384
MOST = 4
N_LATENT = 8
N_SECTION = 4


def block_scale(key, shape, pieces, least, top_value):
    def one(dim, parts):
        heights = jax.random.uniform(jax.random.fold_in(jax.random.fold_in(key, 6), dim), (parts,), jnp.float32, least / len(pieces), top_value / len(pieces))
        return jnp.repeat(jnp.exp(heights), shape[dim] // parts).reshape((-1,) + (1,) * (len(shape) - dim - 1))

    loudness = one(*pieces[0])
    for cut in pieces[1:]:
        loudness = loudness * one(*cut)
    return loudness


def assign_block(key, own, number, rows, number_of, top, limit, skew):
    ranking = jax.random.permutation(key, number_of)
    heavy_load, usual = load_shares(number_of, rows * top, limit, skew, True), load_shares(number_of, rows * top, limit, skew, False)
    places = jnp.arange(number_of)

    def named(sizes, rotation):
        used = int((sizes > 0).sum())
        fixed = max(1, used // 4)
        moved = fixed + (places - fixed + rotation * (used - fixed)) % max(1, number_of - fixed)
        return jnp.zeros((number_of,), jnp.int32).at[ranking[jnp.where(places < fixed, places, moved)]].set(jnp.asarray(sizes, jnp.int32))

    sizes = jnp.where(number % 4 == 0, named(heavy_load, number // 4), named(usual, number - number // 4 - 1))
    mixed = jax.random.permutation(jax.random.fold_in(own, 3), number_of)
    donor, receiver = mixed[0:number_of // 2 * 2:2], mixed[1:number_of // 2 * 2:2]
    margin = jnp.minimum(sizes[donor] - 1, limit - sizes[receiver]) // 2
    margin = jnp.where((donor == ranking[0]) | (receiver == ranking[0]) | (sizes[receiver] == 0), 0, jnp.maximum(margin, 0))
    moved = jax.random.randint(jax.random.fold_in(own, 4), (number_of // 2,), 0, 1 << 20) % (margin + 1)
    sizes = sizes.at[donor].add(-moved).at[receiver].add(moved)
    items = jnp.searchsorted(jnp.cumsum(sizes), jnp.arange(rows * top), side="right").astype(jnp.int32)
    grid = items.reshape(top, rows).T
    grid = grid[jax.random.permutation(jax.random.fold_in(own, 1), rows)]
    rotation = jax.random.randint(jax.random.fold_in(own, 2), (rows, 1), 0, top)
    return jnp.take_along_axis(grid, (jnp.arange(top)[None, :] + rotation) % top, axis=1)


def load_shares(count, total, reach, lean, full):
    weights = [(1 << 20) // math.isqrt(standing ** lean) + 1 for standing in range(1, count + 1)]
    largest = reach if full else min(reach, max(-(-total // count), total * weights[0] // sum(weights)))
    least = 1 if total - largest >= count - 1 else 0
    given, surplus = [largest] + [least] * (count - 1), total - largest - least * (count - 1)
    while surplus > 0:
        free = [i for i in range(1, count) if given[i] < largest] or [i for i in range(1, count) if given[i] < reach]
        whole, remaining = sum([weights[i] for i in free]), surplus
        for i in free:
            addition = min(reach - given[i], max(1, remaining * weights[i] // whole), surplus)
            given[i] = given[i] + addition
            surplus = surplus - addition
    return np.array(given)


def centred(rng, shape, spread, limit, split=(), kind=jnp.bfloat16):
    gain = block_scale(rng, shape, split, -0.22, 0.18) if split else 1.0
    values = jax.random.normal(rng, shape, jnp.float32) * spread * gain
    return jnp.minimum(jnp.maximum(values, -limit), limit).astype(kind)


def setup_inputs(seed: int = 0) -> dict:
    streams_of = jax.random.split(jax.random.key(seed), 6)
    activations = centred(streams_of[0], (ROWS, D), 1.0, 6.0, ((0, 32), (1, 16)))
    bias_dec = centred(streams_of[1], (D,), 1.0, 4.0, ((0, 16),))
    encoder = centred(streams_of[2], (D, LATENTS), D ** -0.5, 0.09375, ((0, 16), (1, 32)))
    decoder = centred(streams_of[3], (LATENTS, D), (K_ACT * BLOCK) ** -0.5, 0.375, ((0, 32), (1, 16)))
    active_blocks_keys = jax.random.split(jax.random.fold_in(streams_of[4], 1), ROWS // ROW_DEV)
    active_blocks_turns = jax.random.permutation(jax.random.fold_in(streams_of[4], 3), ROWS // ROW_DEV)
    active_blocks = jax.vmap(lambda own, number: assign_block(jax.random.fold_in(streams_of[4], 2), own, number, ROW_DEV, BPG * N_LATENT * N_SECTION, K_ACT, MOST, 2))(active_blocks_keys, active_blocks_turns).reshape((ROWS, K_ACT))
    return {"activations": activations, "bias_dec": bias_dec, "encoder": encoder, "decoder": decoder, "active_blocks": active_blocks}


def reference(activations, bias_dec, encoder, decoder, active_blocks):
    total_blocks = BPG * N_LATENT * N_SECTION
    capacity = MOST * N_LATENT * N_SECTION
    bias_wide = bias_dec.astype(jnp.float32)[None, :]
    shifted = (activations.astype(jnp.float32) - bias_wide).astype(jnp.bfloat16)
    pair_blocks = active_blocks.reshape(-1).astype(jnp.int32)
    total_pairs = pair_blocks.shape[0]
    sort_order = jnp.argsort(pair_blocks, stable=True).astype(jnp.int32)
    sorted_blocks = pair_blocks[sort_order]
    starts = jnp.searchsorted(sorted_blocks, jnp.arange(total_blocks + 1, dtype=jnp.int32), side="left").astype(jnp.int32)

    def block_rows(block_id):
        positions = starts[block_id] + jnp.arange(capacity, dtype=jnp.int32)
        in_use = positions < starts[block_id + 1]
        clipped = jnp.minimum(positions, total_pairs - 1)
        row_ids = (sort_order[clipped] // K_ACT).astype(jnp.int32)
        return row_ids, in_use

    def forward(rebuilt, block_id):
        row_ids, in_use = block_rows(block_id)
        enc_cols = lax.dynamic_slice_in_dim(encoder, block_id * BLOCK, BLOCK, 1)
        dec_rows = lax.dynamic_slice_in_dim(decoder, block_id * BLOCK, BLOCK, 0)
        preact = jnp.dot(shifted[row_ids], enc_cols, preferred_element_type=jnp.float32)
        latent_codes = jnp.where(in_use[:, None], jnp.maximum(preact, 0.0), 0.0).astype(jnp.bfloat16)
        contribution = jnp.dot(latent_codes, dec_rows, preferred_element_type=jnp.float32).astype(jnp.bfloat16)
        rebuilt = rebuilt.at[row_ids].add(contribution.astype(jnp.float32))
        return rebuilt, latent_codes

    block_list = jnp.arange(total_blocks, dtype=jnp.int32)
    start_sum = jnp.zeros((ROWS, D), jnp.float32)
    rebuilt, all_codes = lax.scan(forward, start_sum, block_list)
    rebuilt = rebuilt + bias_wide
    error = rebuilt - activations.astype(jnp.float32)
    row_loss = jnp.sum(error * error, axis=1)
    error_b = error.astype(jnp.bfloat16)

    def backward(carry, inputs):
        block_id, latent_codes = inputs
        row_ids, in_use = block_rows(block_id)
        gradient = jnp.dot(latent_codes.T, error_b[row_ids], preferred_element_type=jnp.float32).astype(jnp.bfloat16)
        return carry, gradient

    unused, gradients = lax.scan(backward, jnp.int32(0), (block_list, all_codes))
    return gradients.reshape(total_blocks * BLOCK, D), row_loss
```

```python
import jax
import jax.numpy as jnp
from jax import lax
from jax.experimental import pallas as pl
from jax.experimental.pallas import tpu as pltpu
from jax.sharding import PartitionSpec as P

BLOCK = 64
PLANE = ("latent", "section")
GROUPS = 32
SHARDS = 16
LOCAL = 32
ROWS = 512
FEATURES = 288
HALF = FEATURES // 2
NAMED = 4
MAIN = 64
EXTRA = 16
MAIN_SLOTS = GROUPS * MAIN
EXTRA_SLOTS = GROUPS * EXTRA
SLOTS = MAIN_SLOTS + EXTRA_SLOTS
PACKED = HALF + 3 * EXTRA
PAIRS = GROUPS // 2
LANE_TILES = SLOTS // 128
CHUNK_TILES = 5
CHUNK_ROWS = 16 * CHUNK_TILES

NT = (((1,), (1,)), ((), ()))
F32 = jnp.float32
BF16 = jnp.bfloat16


def mm(a, b):
    return jnp.dot(a, b, preferred_element_type=F32)


def mm_nt(a, b):
    return lax.dot_general(a, b, NT, preferred_element_type=F32)


def identity(n):
    rows = lax.broadcasted_iota(jnp.int32, (n, n), 0)
    return jnp.where(rows == lax.broadcasted_iota(jnp.int32, (n, n), 1), 1.0, 0.0).astype(BF16)


def lane_offset(tile, width=128):
    return pl.ds(pl.multiple_of(tile * width, width), width)


def store_pair(out_ref, pair, values):
    top, bottom = values[:HALF], values[HALF:]
    low = lax.broadcasted_iota(jnp.int32, (HALF, 128), 1) < MAIN
    first = jnp.where(low, top, pltpu.roll(bottom, MAIN, 1))
    second = jnp.where(low, pltpu.roll(top, MAIN, 1), bottom)
    out_ref[pair, 0:HALF, :] = first.astype(BF16)
    out_ref[pair + PAIRS, 0:HALF, :] = second.astype(BF16)


def store_extra(out_ref, values):
    for part in range(3):
        piece = values[:, part * 128 : (part + 1) * 128].astype(BF16)
        out_ref[:, HALF + part * EXTRA : HALF + (part + 1) * EXTRA, :] = piece.reshape(GROUPS, EXTRA, 128)


def unpack(in_ref, full_ref):
    def one(pair, carry):
        first = in_ref[pair, 0:HALF, :].astype(F32)
        second = in_ref[pair + PAIRS, 0:HALF, :].astype(F32)
        low = lax.broadcasted_iota(jnp.int32, (HALF, 128), 1) < MAIN
        full_ref[0:HALF, lane_offset(pair)] = jnp.where(low, first, pltpu.roll(second, MAIN, 1)).astype(BF16)
        full_ref[HALF:, lane_offset(pair)] = jnp.where(low, pltpu.roll(first, MAIN, 1), second).astype(BF16)
        return carry

    lax.fori_loop(0, PAIRS, one, 0, unroll=2)
    eye = identity(128)
    turned, last = None, None
    for part in range(3):
        last = in_ref[:, HALF + part * EXTRA : HALF + (part + 1) * EXTRA, :].reshape(EXTRA_SLOTS, 128)
        turned = mm_nt(eye, last)
        height = min(128, FEATURES - part * 128)
        full_ref[part * 128 : part * 128 + height, MAIN_SLOTS:] = turned[:height].astype(BF16)
    return last, turned


def prepare_kernel(act_ref, bias_ref, blocks_ref, send_ref, place_ref, extra_ref):
    blocks = blocks_ref[...]
    target = lax.shift_right_logical(blocks, 5)
    local = jnp.bitwise_and(blocks, LOCAL - 1)
    groups = lax.broadcasted_iota(jnp.int32, (GROUPS, ROWS), 0)
    hits = [groups == target[k : k + 1, :] for k in range(NAMED)]
    counts = sum(jnp.where(hit, 1.0, 0.0) for hit in hits).astype(BF16)
    before = lax.broadcasted_iota(jnp.int32, (ROWS, ROWS), 0) < lax.broadcasted_iota(jnp.int32, (ROWS, ROWS), 1)
    earlier = mm(counts, jnp.where(before, 1.0, 0.0).astype(BF16))
    slots, names, most = [], [], jnp.zeros((1, ROWS), jnp.int32)
    for k in range(NAMED):
        mine = target[k : k + 1, :]
        rank = jnp.sum(jnp.where(hits[k], earlier, 0.0), axis=0, keepdims=True).astype(jnp.int32)
        for other in range(k):
            rank = rank + jnp.where(target[other : other + 1, :] == mine, 1, 0)
        main = (jnp.bitwise_and(mine, PAIRS - 1) * 2 + lax.shift_right_logical(mine, 4)) * MAIN + rank
        extra = MAIN_SLOTS + mine * EXTRA + (rank - MAIN)
        slots.append(jnp.where(rank < MAIN, main, jnp.where(rank < MAIN + EXTRA, extra, -1)))
        names.append((local[k : k + 1, :] + 1).astype(F32))
        most = jnp.maximum(most, rank)
    over = jnp.where(jnp.max(most, axis=1, keepdims=True) >= MAIN + EXTRA, 1.0, 0.0)
    shifted = (act_ref[...].astype(F32) - bias_ref[...]).astype(BF16)

    def placed(start, count):
        index = lax.broadcasted_iota(jnp.int32, (count, ROWS), 0) + start
        named = jnp.zeros((count, ROWS), F32)
        for k in range(NAMED):
            named = jnp.where(index == slots[k], names[k], named)
        return named.astype(BF16), jnp.where(named > 0.0, 1.0, 0.0).astype(BF16)

    named, place = placed(MAIN_SLOTS, EXTRA_SLOTS)
    place_ref[MAIN_SLOTS:, :] = place
    padded = jnp.concatenate([shifted, jnp.zeros((96, ROWS), BF16)], axis=0)
    values = mm_nt(place, padded)
    lane = lax.broadcasted_iota(jnp.int32, (EXTRA_SLOTS, 128), 1)
    ids = mm(named, jnp.ones((ROWS, 128), BF16))
    store_extra(send_ref, values)
    extra_ref[...] = jnp.where(lane == 32, ids, values[:, 256:])
    row = lax.broadcasted_iota(jnp.int32, (EXTRA, 128), 0)
    high = lax.broadcasted_iota(jnp.int32, (EXTRA, 128), 1) >= MAIN

    def one(pair, carry):
        named, place = placed(pair * 128, 128)
        place_ref[pl.ds(pl.multiple_of(pair * 128, 128), 128), :] = place
        store_pair(send_ref, pair, mm_nt(shifted, place))
        ids = mm_nt(jnp.ones((EXTRA, ROWS), BF16), named)
        for half in range(2):
            device = pair + half * PAIRS
            mine = ids if half else pltpu.roll(ids, MAIN, 1)
            tile = extra_ref[pl.ds(pl.multiple_of(device * EXTRA, EXTRA), EXTRA), :]
            tile = jnp.where(high & (row == 0), mine, tile)
            tile = jnp.where(high & (row == 1), jnp.broadcast_to(over, (EXTRA, 128)), tile)
            send_ref[device, HALF + 2 * EXTRA :, :] = tile.astype(BF16)
        return carry

    lax.fori_loop(0, PAIRS, one, 0, unroll=2)


def encode_kernel(recv_ref, enc_ref, out_ref, ids_ref, over_ref, full_ref):
    last, turned = unpack(recv_ref, full_ref)
    pick = lax.broadcasted_iota(jnp.int32, (2 * GROUPS, EXTRA_SLOTS), 0)
    column = lax.broadcasted_iota(jnp.int32, (2 * GROUPS, EXTRA_SLOTS), 1)
    wanted = jnp.where(pick < GROUPS, pick * EXTRA, (pick - GROUPS) * EXTRA + 1)
    rows = mm(jnp.where(column == wanted, 1.0, 0.0).astype(BF16), last)
    first, second = rows[:PAIRS], rows[PAIRS:GROUPS]
    low = lax.broadcasted_iota(jnp.int32, (PAIRS, 128), 1) < MAIN
    ids_ref[0:PAIRS, :] = jnp.where(low, pltpu.roll(first, MAIN, 1), second)
    for part in range(EXTRA_SLOTS // 128):
        ids_ref[PAIRS + part : PAIRS + part + 1, :] = turned[32:33, part * 128 : (part + 1) * 128]
    ids_ref[LANE_TILES:, :] = jnp.zeros((24 - LANE_TILES, 128), F32)
    flags = jnp.where(lax.broadcasted_iota(jnp.int32, (GROUPS, 128), 1) == MAIN, rows[GROUPS:], 0.0)
    flag = jnp.max(jnp.max(flags, axis=1, keepdims=True), axis=0, keepdims=True)
    over_ref[...] = jnp.broadcast_to(flag, (8, 128)).astype(jnp.int32)

    def one(tile, carry):
        values = full_ref[:, lane_offset(tile, 256)]
        ids = jnp.concatenate([ids_ref[pl.ds(2 * tile, 1), :], ids_ref[pl.ds(2 * tile + 1, 1), :]], axis=1)
        total = jnp.zeros((BLOCK, 256), F32)
        for group in range(LOCAL // 4):
            part = mm(enc_ref[group * 256 : (group + 1) * 256, :], values)
            for b in range(4):
                total = jnp.where(ids == float(group * 4 + b + 1), part[b * BLOCK : (b + 1) * BLOCK], total)
        for half in range(2):
            lane_tile = 2 * tile + half
            for quarter in range(4):
                piece = total[quarter * 16 : (quarter + 1) * 16, half * 128 : (half + 1) * 128]
                out_ref[
                    quarter + 4 * (lane_tile // CHUNK_TILES),
                    pl.ds(pl.multiple_of((lane_tile % CHUNK_TILES) * 16, 16), 16),
                    :,
                ] = piece.astype(BF16)
        return carry

    lax.fori_loop(0, LANE_TILES // 2, one, 0)


def load_codes(codes_ref, full_ref):
    for tile in range(LANE_TILES):
        for quarter in range(4):
            full_ref[quarter * 16 : (quarter + 1) * 16, tile * 128 : (tile + 1) * 128] = codes_ref[
                quarter + 4 * (tile // CHUNK_TILES),
                (tile % CHUNK_TILES) * 16 : (tile % CHUNK_TILES + 1) * 16,
                :,
            ]


def decode_kernel(codes_ref, ids_ref, dec_ref, send_ref, full_ref, spread_ref, extra_ref):
    load_codes(codes_ref, full_ref)

    def contribution(tile):
        codes = full_ref[:, lane_offset(tile, 256)]
        ids = jnp.concatenate([ids_ref[pl.ds(2 * tile, 1), :], ids_ref[pl.ds(2 * tile + 1, 1), :]], axis=1)
        ids = jnp.broadcast_to(ids, (BLOCK, 256)).astype(BF16)
        for b in range(LOCAL):
            spread_ref[b * BLOCK : (b + 1) * BLOCK, :] = jnp.where(ids == BF16(b + 1), codes, BF16(0))
        return mm(dec_ref[...], spread_ref[...])

    def one(tile, carry):
        values = contribution(tile)
        store_pair(send_ref, 2 * tile, values[:, :128])
        store_pair(send_ref, 2 * tile + 1, values[:, 128:])
        return carry

    lax.fori_loop(0, PAIRS // 2, one, 0)
    extra_ref[FEATURES:, :] = jnp.zeros((384 - FEATURES, EXTRA_SLOTS), BF16)
    for tile in range(PAIRS // 2, LANE_TILES // 2):
        start = tile * 256 - MAIN_SLOTS
        extra_ref[0:FEATURES, start : start + 256] = contribution(tile).astype(BF16)
    store_extra(send_ref, mm_nt(identity(EXTRA_SLOTS), extra_ref[...]))


def combine_kernel(recv_ref, place_ref, act_ref, bias_ref, send_ref, loss_ref, full_ref):
    unpack(recv_ref, full_ref)
    error = mm(full_ref[...], place_ref[...]) + bias_ref[...] - act_ref[...].astype(F32)
    loss_ref[...] = jnp.broadcast_to(jnp.sum(error * error, axis=0, keepdims=True), (8, ROWS))
    sent = error.astype(BF16)

    def one(pair, carry):
        place = place_ref[pl.ds(pl.multiple_of(pair * 128, 128), 128), :]
        store_pair(send_ref, pair, mm_nt(sent, place))
        return carry

    lax.fori_loop(0, PAIRS, one, 0, unroll=2)
    padded = jnp.concatenate([sent, jnp.zeros((96, ROWS), BF16)], axis=0)
    store_extra(send_ref, mm_nt(place_ref[MAIN_SLOTS:, :], padded))


def gradient_kernel(recv_ref, codes_ref, ids_ref, grad_ref, full_ref, code_ref, spread_ref):
    unpack(recv_ref, full_ref)
    load_codes(codes_ref, code_ref)

    def one(group, carry):
        for b in range(4):
            wanted = (group * 4 + b + 1).astype(F32)
            for tile in range(LANE_TILES):
                ids = jnp.broadcast_to(ids_ref[tile : tile + 1, :], (BLOCK, 128)).astype(BF16)
                codes = code_ref[:, tile * 128 : (tile + 1) * 128]
                mask = ids == wanted.astype(BF16)
                spread_ref[b * BLOCK : (b + 1) * BLOCK, tile * 128 : (tile + 1) * 128] = jnp.where(
                    mask, codes, BF16(0)
                )
        grad_ref[:, lane_offset(group, 256)] = mm_nt(full_ref[...], spread_ref[...]).astype(BF16)
        return carry

    lax.fori_loop(0, LOCAL // 4, one, 0)


def call(kernel, out_shape, scratch, flops, name):
    return pl.pallas_call(
        kernel,
        out_shape=out_shape,
        scratch_shapes=scratch,
        name=name,
        compiler_params=pltpu.CompilerParams(vmem_limit_bytes=40 * 1024 * 1024),
        cost_estimate=pl.CostEstimate(flops=flops, bytes_accessed=6_000_000, transcendentals=0),
    )


def shape(dims, dtype=BF16):
    return jax.ShapeDtypeStruct(dims, dtype)


def route(buffer):
    return lax.all_to_all(buffer, PLANE, split_axis=0, concat_axis=0, tiled=True)


def sum_codes(partial):
    received = lax.all_to_all(partial, "dp", split_axis=0, concat_axis=0, tiled=True)
    total = jnp.sum(received.astype(F32), axis=0)
    codes = jnp.maximum(total, 0.0).astype(BF16)
    copies = jnp.broadcast_to(codes[None], (SHARDS,) + codes.shape)
    return lax.all_to_all(copies, "dp", split_axis=0, concat_axis=0, tiled=True)


def sum_loss(part):
    copies = jnp.broadcast_to(part.reshape(1, 4, 128), (SHARDS, 4, 128))
    received = lax.all_to_all(copies, "dp", split_axis=0, concat_axis=0, tiled=True)
    return jnp.sum(received, axis=0).reshape(ROWS)


def padded_plan(activations, bias_dec, encoder, decoder, active_blocks):
    row_count, shard_width = activations.shape
    per_row = active_blocks.shape[1]
    groups = lax.axis_size(PLANE)
    local_blocks = encoder.shape[1] // BLOCK
    total_blocks = local_blocks * groups
    capacity = max(2, 2 * row_count * per_row // total_blocks)
    slot_count = total_blocks * capacity
    pair_blocks = active_blocks.reshape(-1)
    pair_iota = jnp.arange(pair_blocks.shape[0], dtype=jnp.int32)
    same_block = pair_blocks[:, None] == pair_blocks[None, :]
    earlier = pair_iota[None, :] < pair_iota[:, None]
    block_rank = jnp.sum((same_block & earlier).astype(jnp.int32), axis=1)
    slot_index = (pair_blocks * capacity + block_rank).reshape(row_count, per_row)
    slot_iota = jnp.arange(slot_count, dtype=jnp.int32)
    placement = jnp.zeros((slot_count, row_count), BF16)
    for which in range(per_row):
        placement = placement + (slot_index[:, which][None, :] == slot_iota[:, None]).astype(BF16)
    slot_shape = (groups, local_blocks, capacity, shard_width)

    def scatter_rows(values):
        filled = jnp.dot(placement, values, preferred_element_type=F32).astype(values.dtype)
        return filled.reshape(slot_shape)

    bias_wide = bias_dec.astype(F32)[None, :]
    shifted = (activations.astype(F32) - bias_wide).astype(BF16)
    received = route(scatter_rows(shifted))
    enc_local = encoder.reshape(shard_width, local_blocks, BLOCK)
    partial_pre = jnp.einsum("sbkd,dbl->sbkl", received, enc_local, preferred_element_type=F32)
    pre_total = lax.psum(partial_pre, "dp")
    latent_codes = jnp.maximum(pre_total, 0.0).astype(BF16)
    dec_local = decoder.reshape(local_blocks, BLOCK, shard_width)
    contrib = jnp.einsum("sbkl,bld->sbkd", latent_codes, dec_local, preferred_element_type=F32).astype(BF16)
    returned = route(contrib).reshape(slot_count, shard_width)
    summed_rows = jnp.einsum("sr,sd->rd", placement, returned, preferred_element_type=F32)
    error = summed_rows + bias_wide - activations.astype(F32)
    row_loss = lax.psum(jnp.sum(error * error, axis=1), "dp")
    error_sent = route(scatter_rows(error.astype(BF16)))
    gradient = jnp.einsum("sbkl,sbkd->bld", latent_codes, error_sent, preferred_element_type=F32)
    return gradient.reshape(local_blocks * BLOCK, shard_width).astype(BF16), row_loss


def on_device(activations, bias_dec, encoder, decoder, active_blocks):
    act = activations.T
    bias = bias_dec.astype(F32).reshape(FEATURES, 1)
    packed = shape((GROUPS, PACKED, 128))
    full = pltpu.VMEM((FEATURES, SLOTS), BF16)
    spread = pltpu.VMEM((LOCAL * BLOCK, 256), BF16)
    sent, place = call(
        prepare_kernel,
        (packed, shape((SLOTS, ROWS))),
        [pltpu.VMEM((EXTRA_SLOTS, 128), F32)],
        2 * FEATURES * SLOTS * ROWS,
        "prepare",
    )(act, bias, active_blocks.T)
    received = route(sent)
    partial, ids, over = call(
        encode_kernel,
        (shape((SHARDS, CHUNK_ROWS, 128)), shape((24, 128), F32), shape((8, 128), jnp.int32)),
        [full],
        2 * FEATURES * SLOTS * LOCAL * BLOCK,
        "encode",
    )(received, encoder.T)
    codes = sum_codes(partial)
    sent = call(
        decode_kernel,
        packed,
        [
            pltpu.VMEM((BLOCK, SLOTS), BF16),
            spread,
            pltpu.VMEM((384, EXTRA_SLOTS), BF16),
        ],
        2 * FEATURES * SLOTS * LOCAL * BLOCK,
        "decode",
    )(codes, ids, decoder.T)
    received = route(sent)
    sent, loss = call(
        combine_kernel,
        (packed, shape((8, ROWS), F32)),
        [full],
        4 * FEATURES * SLOTS * ROWS,
        "combine",
    )(received, place, act, bias)
    received = route(sent)
    row_loss = sum_loss(loss[0])

    def packed_plan():
        gradient = call(
            gradient_kernel,
            shape((FEATURES, LOCAL * BLOCK)),
            [full, pltpu.VMEM((BLOCK, SLOTS), BF16), pltpu.VMEM((4 * BLOCK, SLOTS), BF16)],
            2 * FEATURES * SLOTS * LOCAL * BLOCK,
            "gradient",
        )(received, codes, ids)
        return gradient.T, row_loss

    return lax.cond(
        over[0, 0] > 0,
        lambda: padded_plan(activations, bias_dec, encoder, decoder, active_blocks),
        packed_plan,
    )


def solution(mesh):
    placed = (
        P(PLANE, "dp"),
        P("dp"),
        P("dp", PLANE),
        P(PLANE, "dp"),
        P(PLANE, None),
    )
    return jax.shard_map(
        on_device,
        mesh=mesh,
        in_specs=placed,
        out_specs=(P(PLANE, "dp"), P(PLANE)),
        check_vma=False,
    )
```

```python
import jax
import jax.numpy as jnp
from jax import lax
from jax.experimental import pallas as pl
from jax.experimental.pallas import tpu as pltpu
from jax.sharding import PartitionSpec as P

BLOCK = 64
PLANE = ("latent", "section")
GROUPS = 32
SHARDS = 16
LOCAL = 32
ROWS = 512
FEATURES = 288
HALF = FEATURES // 2
NAMED = 4
MAIN = 64
EXTRA = 16
MAIN_SLOTS = GROUPS * MAIN
EXTRA_SLOTS = GROUPS * EXTRA
SLOTS = MAIN_SLOTS + EXTRA_SLOTS
PACKED = HALF + 3 * EXTRA
PAIRS = GROUPS // 2
LANE_TILES = SLOTS // 128
CHUNK_TILES = 5
CHUNK_ROWS = 16 * CHUNK_TILES

NT = (((1,), (1,)), ((), ()))
F32 = jnp.float32
BF16 = jnp.bfloat16


def mm(a, b):
    return jnp.dot(a, b, preferred_element_type=F32)


def mm_nt(a, b):
    return lax.dot_general(a, b, NT, preferred_element_type=F32)


def identity(n):
    rows = lax.broadcasted_iota(jnp.int32, (n, n), 0)
    return jnp.where(rows == lax.broadcasted_iota(jnp.int32, (n, n), 1), 1.0, 0.0).astype(BF16)


def lane_offset(tile, width=128):
    return pl.ds(pl.multiple_of(tile * width, width), width)


def store_pair(out_ref, pair, values):
    top, bottom = values[:HALF], values[HALF:]
    low = lax.broadcasted_iota(jnp.int32, (HALF, 128), 1) < MAIN
    first = jnp.where(low, top, pltpu.roll(bottom, MAIN, 1))
    second = jnp.where(low, pltpu.roll(top, MAIN, 1), bottom)
    out_ref[pair, 0:HALF, :] = first.astype(BF16)
    out_ref[pair + PAIRS, 0:HALF, :] = second.astype(BF16)


def store_extra(out_ref, values):
    for part in range(3):
        piece = values[:, part * 128 : (part + 1) * 128].astype(BF16)
        out_ref[:, HALF + part * EXTRA : HALF + (part + 1) * EXTRA, :] = piece.reshape(GROUPS, EXTRA, 128)


def unpack(in_ref, full_ref):
    def one(pair):
        lanes = slice(pair * 128, (pair + 1) * 128)
        first = in_ref[pair, 0:HALF, :].astype(F32)
        second = in_ref[pair + PAIRS, 0:HALF, :].astype(F32)
        low = lax.broadcasted_iota(jnp.int32, (HALF, 128), 1) < MAIN
        full_ref[0:HALF, lanes] = jnp.where(low, first, pltpu.roll(second, MAIN, 1)).astype(BF16)
        full_ref[HALF:, lanes] = jnp.where(low, pltpu.roll(first, MAIN, 1), second).astype(BF16)

    for pair in range(PAIRS):
        one(pair)
    eye = identity(128)
    turned, last = None, None
    for part in range(3):
        last = in_ref[:, HALF + part * EXTRA : HALF + (part + 1) * EXTRA, :].reshape(EXTRA_SLOTS, 128)
        turned = mm_nt(eye, last)
        height = min(128, FEATURES - part * 128)
        full_ref[part * 128 : part * 128 + height, MAIN_SLOTS:] = turned[:height].astype(BF16)
    return last, turned


def placed(slots, names, start, count):
    index = lax.broadcasted_iota(jnp.int32, (count, ROWS), 0) + start
    named = jnp.zeros((count, ROWS), F32)
    for k in range(NAMED):
        named = jnp.where(index == slots[k], names[k], named)
    named = named.astype(BF16)
    return named, jnp.minimum(named, BF16(1))


def prepare_kernel(act_ref, bias_ref, blocks_ref, send_ref, slots_ref):
    blocks = blocks_ref[...]
    target = lax.shift_right_logical(blocks, 5)
    local = jnp.bitwise_and(blocks, LOCAL - 1)
    groups = lax.broadcasted_iota(jnp.int32, (GROUPS, ROWS), 0)
    hits = [groups == target[k : k + 1, :] for k in range(NAMED)]
    counts = sum(jnp.where(hit, 1.0, 0.0) for hit in hits).astype(BF16)
    before = lax.broadcasted_iota(jnp.int32, (ROWS, ROWS), 0) < lax.broadcasted_iota(jnp.int32, (ROWS, ROWS), 1)
    earlier = mm(counts, jnp.where(before, 1.0, 0.0).astype(BF16))
    slots, names, most = [], [], jnp.zeros((1, ROWS), jnp.int32)
    for k in range(NAMED):
        mine = target[k : k + 1, :]
        rank = jnp.sum(jnp.where(hits[k], earlier, 0.0), axis=0, keepdims=True).astype(jnp.int32)
        for other in range(k):
            rank = rank + jnp.where(target[other : other + 1, :] == mine, 1, 0)
        main = (jnp.bitwise_and(mine, PAIRS - 1) * 2 + lax.shift_right_logical(mine, 4)) * MAIN + rank
        extra = MAIN_SLOTS + mine * EXTRA + (rank - MAIN)
        slots.append(jnp.where(rank < MAIN, main, jnp.where(rank < MAIN + EXTRA, extra, -1)))
        names.append((local[k : k + 1, :] + 1).astype(F32))
        most = jnp.maximum(most, rank)
    over = jnp.where(jnp.max(most, axis=1, keepdims=True) >= MAIN + EXTRA, 1.0, 0.0)
    shifted = (act_ref[...].astype(F32) - bias_ref[...]).astype(BF16)

    for k in range(NAMED):
        slots_ref[k : k + 1, :] = slots[k]
    slots_ref[NAMED:, :] = jnp.zeros((8 - NAMED, ROWS), jnp.int32)
    named, place = placed(slots, names, MAIN_SLOTS, EXTRA_SLOTS)
    padded = jnp.concatenate([shifted, jnp.zeros((96, ROWS), BF16)], axis=0)
    values = mm_nt(place, padded)
    store_extra(send_ref, values)
    lane = lax.broadcasted_iota(jnp.int32, (EXTRA_SLOTS, 128), 1)
    ids = mm(named, jnp.ones((ROWS, 128), BF16))
    last = jnp.where(lane == 32, ids, values[:, 256:])
    row = lax.broadcasted_iota(jnp.int32, (EXTRA, 128), 0)
    high = lax.broadcasted_iota(jnp.int32, (EXTRA, 128), 1) >= MAIN
    flag = jnp.broadcast_to(over, (EXTRA, 128))
    for double in range(PAIRS // 2):
        named, place = placed(slots, names, double * 256, 256)
        values = mm_nt(shifted, place)
        ids = mm_nt(jnp.ones((EXTRA, ROWS), BF16), named)
        for side in range(2):
            pair = 2 * double + side
            store_pair(send_ref, pair, values[:, side * 128 : (side + 1) * 128])
            for half in range(2):
                device = pair + half * PAIRS
                mine = ids[:, side * 128 : (side + 1) * 128]
                mine = mine if half else pltpu.roll(mine, MAIN, 1)
                tile = last[device * EXTRA : (device + 1) * EXTRA]
                tile = jnp.where(high & (row == 0), mine, tile)
                tile = jnp.where(high & (row == 1), flag, tile)
                send_ref[device, HALF + 2 * EXTRA :, :] = tile.astype(BF16)


def place_kernel(slots_ref, place_ref):
    slots = [slots_ref[k : k + 1, :] for k in range(NAMED)]
    ones = [jnp.ones((1, ROWS), F32)] * NAMED
    for start in range(0, SLOTS, 256):
        place_ref[start : start + 256, :] = placed(slots, ones, start, 256)[0]


def encode_kernel(recv_ref, enc_ref, rest_ref, out_ref, ids_ref, over_ref, full_ref):
    last, turned = unpack(recv_ref, full_ref)
    pick = lax.broadcasted_iota(jnp.int32, (2 * GROUPS, EXTRA_SLOTS), 0)
    column = lax.broadcasted_iota(jnp.int32, (2 * GROUPS, EXTRA_SLOTS), 1)
    wanted = jnp.where(pick < GROUPS, pick * EXTRA, (pick - GROUPS) * EXTRA + 1)
    rows = mm(jnp.where(column == wanted, 1.0, 0.0).astype(BF16), last)
    first, second = rows[:PAIRS], rows[PAIRS:GROUPS]
    low = lax.broadcasted_iota(jnp.int32, (PAIRS, 128), 1) < MAIN
    ids_ref[0:PAIRS, :] = jnp.where(low, pltpu.roll(first, MAIN, 1), second)
    for part in range(EXTRA_SLOTS // 128):
        ids_ref[PAIRS + part : PAIRS + part + 1, :] = turned[32:33, part * 128 : (part + 1) * 128]
    ids_ref[LANE_TILES:, :] = jnp.zeros((24 - LANE_TILES, 128), F32)
    flags = jnp.where(lax.broadcasted_iota(jnp.int32, (GROUPS, 128), 1) == MAIN, rows[GROUPS:], 0.0)
    flag = jnp.max(jnp.max(flags, axis=1, keepdims=True), axis=0, keepdims=True)
    over_ref[...] = jnp.broadcast_to(flag, (8, 128)).astype(jnp.int32)

    for tile in range(LANE_TILES // 2):
        lanes = slice(tile * 256, (tile + 1) * 256)
        ids = jnp.concatenate([ids_ref[2 * tile : 2 * tile + 1, :], ids_ref[2 * tile + 1 : 2 * tile + 2, :]], axis=1)
        code = ids.astype(jnp.int32) - 1
        part = mm(enc_ref[...], full_ref[0:256, lanes])
        total = jnp.zeros((BLOCK, 256), F32)
        for b in range(LOCAL):
            total = jnp.where(code == b, part[b * BLOCK : (b + 1) * BLOCK], total)
        rest = full_ref[256:, lanes]
        member = jnp.broadcast_to(jnp.bitwise_and(code, 7), (32, 256))
        spread = [jnp.where(member == m, rest, BF16(0)) for m in range(8)]
        part = mm(rest_ref[...], jnp.concatenate(spread, axis=0))
        group = lax.shift_right_arithmetic(code, 3)
        more = jnp.zeros((BLOCK, 256), F32)
        for g in range(4):
            more = jnp.where(group == g, part[g * BLOCK : (g + 1) * BLOCK], more)
        total = total + more
        for half in range(2):
            lane_tile = 2 * tile + half
            slot_row = (lane_tile % CHUNK_TILES) * 16
            for quarter in range(4):
                piece = total[quarter * 16 : (quarter + 1) * 16, half * 128 : (half + 1) * 128]
                out_ref[quarter + 4 * (lane_tile // CHUNK_TILES), slot_row : slot_row + 16, :] = piece.astype(BF16)


def load_codes(codes_ref, full_ref):
    for tile in range(LANE_TILES):
        for quarter in range(4):
            full_ref[quarter * 16 : (quarter + 1) * 16, tile * 128 : (tile + 1) * 128] = codes_ref[
                quarter + 4 * (tile // CHUNK_TILES),
                (tile % CHUNK_TILES) * 16 : (tile % CHUNK_TILES + 1) * 16,
                :,
            ]


def decode_kernel(codes_ref, ids_ref, dec_ref, send_ref, full_ref, spread_ref, extra_ref):
    load_codes(codes_ref, full_ref)

    def contribution(tile):
        spread = spread_ref.at[tile % 2]
        codes = full_ref[:, tile * 256 : (tile + 1) * 256]
        ids = jnp.concatenate([ids_ref[2 * tile : 2 * tile + 1, :], ids_ref[2 * tile + 1 : 2 * tile + 2, :]], axis=1)
        ids = jnp.broadcast_to(ids, (BLOCK, 256)).astype(BF16)
        for b in range(LOCAL):
            spread[b * BLOCK : (b + 1) * BLOCK, :] = jnp.where(ids == BF16(b + 1), codes, BF16(0))
        return mm(dec_ref[...], spread[...])

    extra_ref[FEATURES:, :] = jnp.zeros((384 - FEATURES, EXTRA_SLOTS), BF16)
    for tile in range(PAIRS // 2, LANE_TILES // 2):
        start = tile * 256 - MAIN_SLOTS
        extra_ref[0:FEATURES, start : start + 256] = contribution(tile).astype(BF16)
    store_extra(send_ref, mm_nt(identity(EXTRA_SLOTS), extra_ref[...]))
    for tile in range(PAIRS // 2):
        values = contribution(tile)
        store_pair(send_ref, 2 * tile, values[:, :128])
        store_pair(send_ref, 2 * tile + 1, values[:, 128:])


def spread_kernel(codes_ref, ids_ref, spread_ref):
    for tile in range(LANE_TILES):
        pieces = []
        for quarter in range(4):
            row = (tile % CHUNK_TILES) * 16
            pieces.append(codes_ref[quarter + 4 * (tile // CHUNK_TILES), row : row + 16, :])
        codes = jnp.concatenate(pieces, axis=0)
        ids = jnp.broadcast_to(ids_ref[tile : tile + 1, :], (BLOCK, 128)).astype(BF16)
        for b in range(LOCAL):
            spread_ref[b * BLOCK : (b + 1) * BLOCK, tile * 128 : (tile + 1) * 128] = jnp.where(
                ids == BF16(b + 1), codes, BF16(0)
            )


def combine_kernel(recv_ref, place_ref, act_ref, bias_ref, send_ref, loss_ref, full_ref):
    unpack(recv_ref, full_ref)
    error = mm(full_ref[...], place_ref[...]) + bias_ref[...] - act_ref[...].astype(F32)
    loss_ref[...] = jnp.broadcast_to(jnp.sum(error * error, axis=0, keepdims=True), (8, ROWS))
    sent = error.astype(BF16)

    for double in range(PAIRS // 2):
        values = mm_nt(sent, place_ref[double * 256 : (double + 1) * 256, :])
        store_pair(send_ref, 2 * double, values[:, :128])
        store_pair(send_ref, 2 * double + 1, values[:, 128:])
    padded = jnp.concatenate([sent, jnp.zeros((96, ROWS), BF16)], axis=0)
    store_extra(send_ref, mm_nt(place_ref[MAIN_SLOTS:, :], padded))


def gradient_kernel(recv_ref, spread_ref, grad_ref, full_ref):
    unpack(recv_ref, full_ref)
    for start in range(0, LOCAL * BLOCK, 256):
        part = mm_nt(full_ref[...], spread_ref[start : start + 256, :])
        grad_ref[:, start : start + 256] = part.astype(BF16)


def call(kernel, out_shape, scratch, flops, name):
    return pl.pallas_call(
        kernel,
        out_shape=out_shape,
        scratch_shapes=scratch,
        name=name,
        compiler_params=pltpu.CompilerParams(vmem_limit_bytes=40 * 1024 * 1024),
        cost_estimate=pl.CostEstimate(flops=flops, bytes_accessed=6_000_000, transcendentals=0),
    )


def shape(dims, dtype=BF16):
    return jax.ShapeDtypeStruct(dims, dtype)


def route(buffer):
    return lax.all_to_all(buffer, PLANE, split_axis=0, concat_axis=0, tiled=True)


def sum_codes(partial):
    received = lax.all_to_all(partial, "dp", split_axis=0, concat_axis=0, tiled=True)
    total = jnp.sum(received.astype(F32), axis=0)
    codes = jnp.maximum(total, 0.0).astype(BF16)
    copies = jnp.broadcast_to(codes[None], (SHARDS,) + codes.shape)
    return lax.all_to_all(copies, "dp", split_axis=0, concat_axis=0, tiled=True)


def sum_loss(part):
    return lax.psum(part, "dp")


def padded_plan(activations, bias_dec, encoder, decoder, active_blocks):
    row_count, shard_width = activations.shape
    per_row = active_blocks.shape[1]
    groups = lax.axis_size(PLANE)
    local_blocks = encoder.shape[1] // BLOCK
    total_blocks = local_blocks * groups
    capacity = max(2, 2 * row_count * per_row // total_blocks)
    slot_count = total_blocks * capacity
    pair_blocks = active_blocks.reshape(-1)
    pair_iota = jnp.arange(pair_blocks.shape[0], dtype=jnp.int32)
    same_block = pair_blocks[:, None] == pair_blocks[None, :]
    earlier = pair_iota[None, :] < pair_iota[:, None]
    block_rank = jnp.sum((same_block & earlier).astype(jnp.int32), axis=1)
    slot_index = (pair_blocks * capacity + block_rank).reshape(row_count, per_row)
    slot_iota = jnp.arange(slot_count, dtype=jnp.int32)
    placement = jnp.zeros((slot_count, row_count), BF16)
    for which in range(per_row):
        placement = placement + (slot_index[:, which][None, :] == slot_iota[:, None]).astype(BF16)
    slot_shape = (groups, local_blocks, capacity, shard_width)

    def scatter_rows(values):
        filled = jnp.dot(placement, values, preferred_element_type=F32).astype(values.dtype)
        return filled.reshape(slot_shape)

    bias_wide = bias_dec.astype(F32)[None, :]
    shifted = (activations.astype(F32) - bias_wide).astype(BF16)
    received = route(scatter_rows(shifted))
    enc_local = encoder.reshape(shard_width, local_blocks, BLOCK)
    partial_pre = jnp.einsum("sbkd,dbl->sbkl", received, enc_local, preferred_element_type=F32)
    pre_total = lax.psum(partial_pre, "dp")
    latent_codes = jnp.maximum(pre_total, 0.0).astype(BF16)
    dec_local = decoder.reshape(local_blocks, BLOCK, shard_width)
    contrib = jnp.einsum("sbkl,bld->sbkd", latent_codes, dec_local, preferred_element_type=F32).astype(BF16)
    returned = route(contrib).reshape(slot_count, shard_width)
    summed_rows = jnp.einsum("sr,sd->rd", placement, returned, preferred_element_type=F32)
    error = summed_rows + bias_wide - activations.astype(F32)
    row_loss = lax.psum(jnp.sum(error * error, axis=1), "dp")
    error_sent = route(scatter_rows(error.astype(BF16)))
    gradient = jnp.einsum("sbkl,sbkd->bld", latent_codes, error_sent, preferred_element_type=F32)
    return gradient.reshape(local_blocks * BLOCK, shard_width).astype(BF16), row_loss


def on_device(activations, bias_dec, encoder, decoder, active_blocks):
    act = activations.T
    bias = bias_dec.astype(F32).reshape(FEATURES, 1)
    packed = shape((GROUPS, PACKED, 128))
    full = pltpu.VMEM((FEATURES, SLOTS), BF16)
    spread = pltpu.VMEM((2, LOCAL * BLOCK, 256), BF16)
    sent, slots = call(
        prepare_kernel,
        (packed, shape((8, ROWS), jnp.int32)),
        [],
        2 * FEATURES * SLOTS * ROWS,
        "prepare",
    )(act, bias, active_blocks.T)
    received = route(sent)
    place = call(place_kernel, shape((SLOTS, ROWS)), [], 0, "place")(slots)
    turned = encoder.T
    rest = turned[:, 256:].reshape(4, 8, BLOCK, 32).transpose(0, 2, 1, 3).reshape(4 * BLOCK, 256)
    partial, ids, over = call(
        encode_kernel,
        (shape((SHARDS, CHUNK_ROWS, 128)), shape((24, 128), F32), shape((8, 128), jnp.int32)),
        [full],
        2 * FEATURES * SLOTS * LOCAL * BLOCK,
        "encode",
    )(received, turned[:, :256], rest)
    codes = sum_codes(partial)
    sent = call(
        decode_kernel,
        packed,
        [
            pltpu.VMEM((BLOCK, SLOTS), BF16),
            spread,
            pltpu.VMEM((384, EXTRA_SLOTS), BF16),
        ],
        2 * FEATURES * SLOTS * LOCAL * BLOCK,
        "decode",
    )(codes, ids, decoder.T)
    received = route(sent)
    sent, loss = call(
        combine_kernel,
        (packed, shape((8, ROWS), F32)),
        [full],
        4 * FEATURES * SLOTS * ROWS,
        "combine",
    )(received, place, act, bias)
    received = route(sent)
    row_loss = sum_loss(loss[0])
    spread = call(spread_kernel, shape((LOCAL * BLOCK, SLOTS)), [], 0, "spread")(codes, ids)

    def packed_plan():
        gradient = call(
            gradient_kernel,
            shape((FEATURES, LOCAL * BLOCK)),
            [full],
            2 * FEATURES * SLOTS * LOCAL * BLOCK,
            "gradient",
        )(received, spread)
        return gradient.T, row_loss

    return lax.cond(
        over[0, 0] > 0,
        lambda: padded_plan(activations, bias_dec, encoder, decoder, active_blocks),
        packed_plan,
    )


def solution(mesh):
    placed = (
        P(PLANE, "dp"),
        P("dp"),
        P("dp", PLANE),
        P(PLANE, "dp"),
        P(PLANE, None),
    )
    return jax.shard_map(
        on_device,
        mesh=mesh,
        in_specs=placed,
        out_specs=(P(PLANE, "dp"), P(PLANE)),
        check_vma=False,
    )
```

```python
import jax
import jax.numpy as jnp
from jax import lax
from jax.experimental import pallas as pl
from jax.experimental.pallas import tpu as pltpu
from jax.sharding import PartitionSpec as P

BLOCK = 64
PLANE = ("latent", "section")
OUTER, INNER = "dp_outer", "dp_inner"
DP = (OUTER, INNER)
GROUPS = 32
SHARDS = 16
LOCAL = 32
ROWS = 512
FEATURES = 288
HALF = FEATURES // 2
NAMED = 4
MAIN = 64
EXTRA = 16
MAIN_SLOTS = GROUPS * MAIN
EXTRA_SLOTS = GROUPS * EXTRA
SLOTS = MAIN_SLOTS + EXTRA_SLOTS
PACKED = HALF + 3 * EXTRA
PAIRS = GROUPS // 2
EARLY = 12
LANE_TILES = SLOTS // 128
CHUNK_TILES = 5
CHUNK_ROWS = 16 * CHUNK_TILES

NT = (((1,), (1,)), ((), ()))
F32 = jnp.float32
BF16 = jnp.bfloat16


def mm(a, b):
    return jnp.dot(a, b, preferred_element_type=F32)


def mm_nt(a, b):
    return lax.dot_general(a, b, NT, preferred_element_type=F32)


def identity(n):
    rows = lax.broadcasted_iota(jnp.int32, (n, n), 0)
    return jnp.where(rows == lax.broadcasted_iota(jnp.int32, (n, n), 1), 1.0, 0.0).astype(BF16)


def lane_offset(tile, width=128):
    return pl.ds(pl.multiple_of(tile * width, width), width)


def store_pair(out_ref, pair, values):
    top, bottom = values[:HALF], values[HALF:]
    low = lax.broadcasted_iota(jnp.int32, (HALF, 128), 1) < MAIN
    first = jnp.where(low, top, pltpu.roll(bottom, MAIN, 1))
    second = jnp.where(low, pltpu.roll(top, MAIN, 1), bottom)
    out_ref[pair, 0:HALF, :] = first.astype(BF16)
    out_ref[pair + PAIRS, 0:HALF, :] = second.astype(BF16)


def stage_copies(buffer_ref, out_ref, sems, stage):
    first, count = (0, EARLY) if stage == 0 else (EARLY, PAIRS - EARLY)
    copies = []
    for side in range(2):
        devices = pl.ds(side * PAIRS + first, count)
        copies.append(
            pltpu.make_async_copy(buffer_ref.at[devices], out_ref.at[devices], sems.at[2 * stage + side])
        )
    return copies


def start_stage(buffer_ref, out_ref, sems, done):
    if done in (EARLY, PAIRS):
        for copy in stage_copies(buffer_ref, out_ref, sems, 0 if done == EARLY else 1):
            copy.start()


def wait_stages(buffer_ref, out_ref, sems):
    for stage in range(2):
        for copy in stage_copies(buffer_ref, out_ref, sems, stage):
            copy.wait()


def bias_column(bias_ref):
    rows = lax.broadcasted_iota(jnp.int32, (FEATURES, FEATURES), 0)
    lanes = lax.broadcasted_iota(jnp.int32, (FEATURES, FEATURES), 1)
    wide = jnp.broadcast_to(bias_ref[...].astype(F32).reshape(1, FEATURES), (FEATURES, FEATURES))
    return jnp.sum(jnp.where(rows == lanes, wide, 0.0), axis=1, keepdims=True)


def store_extra(out_ref, values):
    for part in range(3):
        piece = values[:, part * 128 : (part + 1) * 128].astype(BF16)
        out_ref[:, HALF + part * EXTRA : HALF + (part + 1) * EXTRA, :] = piece.reshape(GROUPS, EXTRA, 128)


def unpack(in_ref, full_ref):
    def one(pair):
        lanes = slice(pair * 128, (pair + 1) * 128)
        first = in_ref[pair, 0:HALF, :].astype(F32)
        second = in_ref[pair + PAIRS, 0:HALF, :].astype(F32)
        low = lax.broadcasted_iota(jnp.int32, (HALF, 128), 1) < MAIN
        full_ref[0:HALF, lanes] = jnp.where(low, first, pltpu.roll(second, MAIN, 1)).astype(BF16)
        full_ref[HALF:, lanes] = jnp.where(low, pltpu.roll(first, MAIN, 1), second).astype(BF16)

    for pair in range(PAIRS):
        one(pair)
    eye = identity(128)
    turned, last = None, None
    for part in range(3):
        last = in_ref[:, HALF + part * EXTRA : HALF + (part + 1) * EXTRA, :].reshape(EXTRA_SLOTS, 128)
        turned = mm_nt(eye, last)
        height = min(128, FEATURES - part * 128)
        full_ref[part * 128 : part * 128 + height, MAIN_SLOTS:] = turned[:height].astype(BF16)
    return last, turned


def placed(slots, names, start, count):
    index = lax.broadcasted_iota(jnp.int32, (count, ROWS), 0) + start
    named = jnp.zeros((count, ROWS), F32)
    for k in range(NAMED):
        named = jnp.where(index == slots[k], names[k], named)
    named = named.astype(BF16)
    return named, jnp.minimum(named, BF16(1))


def prepare_kernel(act_ref, bias_ref, blocks_ref, out_ref, slots_ref, send_ref, sems):
    blocks = blocks_ref[...]
    target = lax.shift_right_logical(blocks, 5)
    local = jnp.bitwise_and(blocks, LOCAL - 1)
    groups = lax.broadcasted_iota(jnp.int32, (GROUPS, ROWS), 0)
    hits = [groups == target[k : k + 1, :] for k in range(NAMED)]
    counts = sum(jnp.where(hit, 1.0, 0.0) for hit in hits).astype(BF16)
    before = lax.broadcasted_iota(jnp.int32, (ROWS, ROWS), 0) < lax.broadcasted_iota(jnp.int32, (ROWS, ROWS), 1)
    earlier = mm(counts, jnp.where(before, 1.0, 0.0).astype(BF16))
    slots, names, most = [], [], jnp.zeros((1, ROWS), jnp.int32)
    for k in range(NAMED):
        mine = target[k : k + 1, :]
        rank = jnp.sum(jnp.where(hits[k], earlier, 0.0), axis=0, keepdims=True).astype(jnp.int32)
        for other in range(k):
            rank = rank + jnp.where(target[other : other + 1, :] == mine, 1, 0)
        main = (jnp.bitwise_and(mine, PAIRS - 1) * 2 + lax.shift_right_logical(mine, 4)) * MAIN + rank
        extra = MAIN_SLOTS + mine * EXTRA + (rank - MAIN)
        slots.append(jnp.where(rank < MAIN, main, jnp.where(rank < MAIN + EXTRA, extra, -1)))
        names.append((local[k : k + 1, :] + 1).astype(F32))
        most = jnp.maximum(most, rank)
    over = jnp.where(jnp.max(most, axis=1, keepdims=True) >= MAIN + EXTRA, 1.0, 0.0)
    shifted = (act_ref[...].astype(F32) - bias_column(bias_ref)).astype(BF16)

    for k in range(NAMED):
        slots_ref[k : k + 1, :] = slots[k]
    slots_ref[NAMED:, :] = jnp.zeros((8 - NAMED, ROWS), jnp.int32)
    named, place = placed(slots, names, MAIN_SLOTS, EXTRA_SLOTS)
    padded = jnp.concatenate([shifted, jnp.zeros((96, ROWS), BF16)], axis=0)
    values = mm_nt(place, padded)
    store_extra(send_ref, values)
    lane = lax.broadcasted_iota(jnp.int32, (EXTRA_SLOTS, 128), 1)
    ids = mm(named, jnp.ones((ROWS, 128), BF16))
    last = jnp.where(lane == 32, ids, values[:, 256:])
    row = lax.broadcasted_iota(jnp.int32, (EXTRA, 128), 0)
    high = lax.broadcasted_iota(jnp.int32, (EXTRA, 128), 1) >= MAIN
    flag = jnp.broadcast_to(over, (EXTRA, 128))
    for double in range(PAIRS // 2):
        named, place = placed(slots, names, double * 256, 256)
        values = mm_nt(shifted, place)
        ids = mm_nt(jnp.ones((EXTRA, ROWS), BF16), named)
        for side in range(2):
            pair = 2 * double + side
            store_pair(send_ref, pair, values[:, side * 128 : (side + 1) * 128])
            for half in range(2):
                device = pair + half * PAIRS
                mine = ids[:, side * 128 : (side + 1) * 128]
                mine = mine if half else pltpu.roll(mine, MAIN, 1)
                tile = last[device * EXTRA : (device + 1) * EXTRA]
                tile = jnp.where(high & (row == 0), mine, tile)
                tile = jnp.where(high & (row == 1), flag, tile)
                send_ref[device, HALF + 2 * EXTRA :, :] = tile.astype(BF16)
        start_stage(send_ref, out_ref, sems, 2 * double + 2)
    wait_stages(send_ref, out_ref, sems)


def place_kernel(slots_ref, place_ref):
    slots = [slots_ref[k : k + 1, :] for k in range(NAMED)]
    ones = [jnp.ones((1, ROWS), F32)] * NAMED
    for start in range(0, SLOTS, 256):
        place_ref[start : start + 256, :] = placed(slots, ones, start, 256)[0]


def encode_kernel(recv_ref, enc_ref, rest_ref, out_ref, ids_ref, over_ref, full_ref):
    last, turned = unpack(recv_ref, full_ref)
    pick = lax.broadcasted_iota(jnp.int32, (2 * GROUPS, EXTRA_SLOTS), 0)
    column = lax.broadcasted_iota(jnp.int32, (2 * GROUPS, EXTRA_SLOTS), 1)
    wanted = jnp.where(pick < GROUPS, pick * EXTRA, (pick - GROUPS) * EXTRA + 1)
    rows = mm(jnp.where(column == wanted, 1.0, 0.0).astype(BF16), last)
    first, second = rows[:PAIRS], rows[PAIRS:GROUPS]
    low = lax.broadcasted_iota(jnp.int32, (PAIRS, 128), 1) < MAIN
    ids_ref[0:PAIRS, :] = jnp.where(low, pltpu.roll(first, MAIN, 1), second)
    for part in range(EXTRA_SLOTS // 128):
        ids_ref[PAIRS + part : PAIRS + part + 1, :] = turned[32:33, part * 128 : (part + 1) * 128]
    ids_ref[LANE_TILES:, :] = jnp.zeros((24 - LANE_TILES, 128), F32)
    flags = jnp.where(lax.broadcasted_iota(jnp.int32, (GROUPS, 128), 1) == MAIN, rows[GROUPS:], 0.0)
    flag = jnp.max(jnp.max(flags, axis=1, keepdims=True), axis=0, keepdims=True)
    over_ref[...] = jnp.broadcast_to(flag, (8, 128)).astype(jnp.int32)

    for tile in range(LANE_TILES // 2):
        lanes = slice(tile * 256, (tile + 1) * 256)
        ids = jnp.concatenate([ids_ref[2 * tile : 2 * tile + 1, :], ids_ref[2 * tile + 1 : 2 * tile + 2, :]], axis=1)
        code = ids.astype(jnp.int32) - 1
        part = mm(enc_ref[...], full_ref[0:256, lanes])
        total = jnp.zeros((BLOCK, 256), F32)
        for b in range(LOCAL):
            total = jnp.where(code == b, part[b * BLOCK : (b + 1) * BLOCK], total)
        rest = full_ref[256:, lanes]
        member = jnp.broadcast_to(jnp.bitwise_and(code, 7), (32, 256))
        spread = [jnp.where(member == m, rest, BF16(0)) for m in range(8)]
        part = mm(rest_ref[...], jnp.concatenate(spread, axis=0))
        group = lax.shift_right_arithmetic(code, 3)
        more = jnp.zeros((BLOCK, 256), F32)
        for g in range(4):
            more = jnp.where(group == g, part[g * BLOCK : (g + 1) * BLOCK], more)
        total = total + more
        for half in range(2):
            lane_tile = 2 * tile + half
            slot_row = (lane_tile % CHUNK_TILES) * 16
            for quarter in range(4):
                piece = total[quarter * 16 : (quarter + 1) * 16, half * 128 : (half + 1) * 128]
                out_ref[quarter + 4 * (lane_tile // CHUNK_TILES), slot_row : slot_row + 16, :] = piece.astype(BF16)


def load_codes(codes_ref, full_ref):
    for tile in range(LANE_TILES):
        for quarter in range(4):
            full_ref[quarter * 16 : (quarter + 1) * 16, tile * 128 : (tile + 1) * 128] = codes_ref[
                quarter + 4 * (tile // CHUNK_TILES),
                (tile % CHUNK_TILES) * 16 : (tile % CHUNK_TILES + 1) * 16,
                :,
            ]


def decode_kernel(codes_ref, ids_ref, dec_ref, out_ref, full_ref, extra_ref, send_ref, sems):
    load_codes(codes_ref, full_ref)

    def contribution(tile):
        codes = full_ref[:, tile * 256 : (tile + 1) * 256]
        ids = jnp.concatenate([ids_ref[2 * tile : 2 * tile + 1, :], ids_ref[2 * tile + 1 : 2 * tile + 2, :]], axis=1)
        ids = jnp.broadcast_to(ids, (BLOCK, 256)).astype(BF16)
        spread = [jnp.where(ids == BF16(b + 1), codes, BF16(0)) for b in range(LOCAL)]
        return mm(dec_ref[...], jnp.concatenate(spread, axis=0))

    extra_ref[FEATURES:, :] = jnp.zeros((384 - FEATURES, EXTRA_SLOTS), BF16)
    for tile in range(PAIRS // 2, LANE_TILES // 2):
        start = tile * 256 - MAIN_SLOTS
        extra_ref[0:FEATURES, start : start + 256] = contribution(tile).astype(BF16)
    store_extra(send_ref, mm_nt(identity(EXTRA_SLOTS), extra_ref[...]))
    for tile in range(PAIRS // 2):
        values = contribution(tile)
        store_pair(send_ref, 2 * tile, values[:, :128])
        store_pair(send_ref, 2 * tile + 1, values[:, 128:])
        start_stage(send_ref, out_ref, sems, 2 * tile + 2)
    wait_stages(send_ref, out_ref, sems)


def combine_kernel(recv_ref, place_ref, act_ref, bias_ref, out_ref, loss_ref, full_ref, send_ref, sems):
    unpack(recv_ref, full_ref)
    error = mm(full_ref[...], place_ref[...]) + bias_column(bias_ref) - act_ref[...].astype(F32)
    sent = error.astype(BF16)
    padded = jnp.concatenate([sent, jnp.zeros((96, ROWS), BF16)], axis=0)
    store_extra(send_ref, mm_nt(place_ref[MAIN_SLOTS:, :], padded))
    for double in range(PAIRS // 2):
        values = mm_nt(sent, place_ref[double * 256 : (double + 1) * 256, :])
        store_pair(send_ref, 2 * double, values[:, :128])
        store_pair(send_ref, 2 * double + 1, values[:, 128:])
        start_stage(send_ref, out_ref, sems, 2 * double + 2)
    loss = jnp.sum(error * error, axis=0, keepdims=True)
    for part in range(ROWS // 128):
        loss_ref[part : part + 1, :] = loss[:, part * 128 : (part + 1) * 128]
    wait_stages(send_ref, out_ref, sems)


def gradient_kernel(
    recv_ref, codes_ref, ids_ref, loss_ref, out_ref, out_loss_ref, full_ref, code_ref, grad_ref, sems
):
    out_loss_ref[...] = loss_ref[...]
    unpack(recv_ref, full_ref)
    load_codes(codes_ref, code_ref)
    ids = jnp.concatenate([ids_ref[tile : tile + 1, :] for tile in range(LANE_TILES)], axis=1)
    ids = jnp.broadcast_to(ids, (BLOCK, SLOTS)).astype(BF16)
    copies, begin = [], 0
    for start in range(0, LOCAL * BLOCK, 256):
        stop = start + 256
        spread = [
            jnp.where(ids == BF16(b + 1), code_ref[...], BF16(0)) for b in range(start // BLOCK, stop // BLOCK)
        ]
        grad_ref[:, start:stop] = mm_nt(full_ref[...], jnp.concatenate(spread, axis=0)).astype(BF16)
        if stop in (LOCAL * BLOCK * 3 // 4, LOCAL * BLOCK):
            lanes = pl.ds(begin, stop - begin)
            copy = pltpu.make_async_copy(grad_ref.at[:, lanes], out_ref.at[:, lanes], sems.at[len(copies)])
            copy.start()
            copies.append(copy)
            begin = stop
    for copy in copies:
        copy.wait()


def call(kernel, out_shape, scratch, flops, name, megabytes, **specs):
    return pl.pallas_call(
        kernel,
        out_shape=out_shape,
        scratch_shapes=scratch,
        name=name,
        **specs,
        compiler_params=pltpu.CompilerParams(vmem_limit_bytes=megabytes * 1024 * 1024),
        cost_estimate=pl.CostEstimate(flops=flops, bytes_accessed=6_000_000, transcendentals=0),
    )


def shape(dims, dtype=BF16):
    return jax.ShapeDtypeStruct(dims, dtype)


def in_hbm(dims, dtype=BF16):
    return pltpu.HBM(dims, dtype)


def route(buffer):
    return lax.all_to_all(buffer, PLANE, split_axis=0, concat_axis=0, tiled=True)


def sum_codes(partial):
    received = lax.all_to_all(partial, DP, split_axis=0, concat_axis=0, tiled=True)
    total = jnp.sum(received.astype(F32), axis=0)
    codes = jnp.maximum(total, 0.0).astype(BF16)
    copies = jnp.broadcast_to(codes[None], (SHARDS,) + codes.shape)
    return lax.all_to_all(copies, DP, split_axis=0, concat_axis=0, tiled=True)


def sum_loss(part):
    return lax.psum(lax.psum(part, INNER), OUTER)


def padded_plan(activations, bias_dec, encoder, decoder, active_blocks):
    row_count, shard_width = activations.shape
    per_row = active_blocks.shape[1]
    groups = lax.axis_size(PLANE)
    local_blocks = encoder.shape[1] // BLOCK
    total_blocks = local_blocks * groups
    capacity = max(2, 2 * row_count * per_row // total_blocks)
    slot_count = total_blocks * capacity
    pair_blocks = active_blocks.reshape(-1)
    pair_iota = jnp.arange(pair_blocks.shape[0], dtype=jnp.int32)
    same_block = pair_blocks[:, None] == pair_blocks[None, :]
    earlier = pair_iota[None, :] < pair_iota[:, None]
    block_rank = jnp.sum((same_block & earlier).astype(jnp.int32), axis=1)
    slot_index = (pair_blocks * capacity + block_rank).reshape(row_count, per_row)
    slot_iota = jnp.arange(slot_count, dtype=jnp.int32)
    placement = jnp.zeros((slot_count, row_count), BF16)
    for which in range(per_row):
        placement = placement + (slot_index[:, which][None, :] == slot_iota[:, None]).astype(BF16)
    slot_shape = (groups, local_blocks, capacity, shard_width)

    def scatter_rows(values):
        filled = jnp.dot(placement, values, preferred_element_type=F32).astype(values.dtype)
        return filled.reshape(slot_shape)

    bias_wide = bias_dec.astype(F32)[None, :]
    shifted = (activations.astype(F32) - bias_wide).astype(BF16)
    received = route(scatter_rows(shifted))
    enc_local = encoder.reshape(shard_width, local_blocks, BLOCK)
    partial_pre = jnp.einsum("sbkd,dbl->sbkl", received, enc_local, preferred_element_type=F32)
    pre_total = lax.psum(partial_pre, DP)
    latent_codes = jnp.maximum(pre_total, 0.0).astype(BF16)
    dec_local = decoder.reshape(local_blocks, BLOCK, shard_width)
    contrib = jnp.einsum("sbkl,bld->sbkd", latent_codes, dec_local, preferred_element_type=F32).astype(BF16)
    returned = route(contrib).reshape(slot_count, shard_width)
    summed_rows = jnp.einsum("sr,sd->rd", placement, returned, preferred_element_type=F32)
    error = summed_rows + bias_wide - activations.astype(F32)
    row_loss = lax.psum(jnp.sum(error * error, axis=1), DP)
    error_sent = route(scatter_rows(error.astype(BF16)))
    gradient = jnp.einsum("sbkl,sbkd->bld", latent_codes, error_sent, preferred_element_type=F32)
    return gradient.reshape(local_blocks * BLOCK, shard_width).astype(BF16), row_loss


def on_device(activations, bias_dec, encoder, decoder, active_blocks):
    act = activations.T
    bias = bias_dec
    packed = in_hbm((GROUPS, PACKED, 128))
    full = pltpu.VMEM((FEATURES, SLOTS), BF16)
    sending = [pltpu.VMEM((GROUPS, PACKED, 128), BF16), pltpu.SemaphoreType.DMA((4,))]
    vmem, hbm = pl.BlockSpec(memory_space=pltpu.VMEM), pl.BlockSpec(memory_space=pltpu.HBM)
    spread_flops = 2 * FEATURES * SLOTS * LOCAL * BLOCK
    sent, slots = call(
        prepare_kernel,
        (packed, shape((8, ROWS), jnp.int32)),
        sending,
        2 * FEATURES * SLOTS * ROWS,
        "prepare",
        20,
        out_specs=(hbm, vmem),
    )(act, bias, active_blocks.T)
    received = route(sent)
    place = call(place_kernel, shape((SLOTS, ROWS)), [], 0, "place", 16)(slots)
    turned = encoder.T
    rest = turned[:, 256:].reshape(4, 8, BLOCK, 32).transpose(0, 2, 1, 3).reshape(4 * BLOCK, 256)
    partial, ids, over = call(
        encode_kernel,
        (shape((SHARDS, CHUNK_ROWS, 128)), shape((24, 128), F32), shape((8, 128), jnp.int32)),
        [full],
        spread_flops,
        "encode",
        20,
    )(received, turned[:, :256], rest)
    codes = sum_codes(partial)
    sent = call(
        decode_kernel,
        packed,
        [
            pltpu.VMEM((BLOCK, SLOTS), BF16),
            pltpu.VMEM((384, EXTRA_SLOTS), BF16),
        ]
        + sending,
        spread_flops,
        "decode",
        20,
        out_specs=hbm,
    )(codes, ids, decoder.T)
    received = route(sent)
    heavy = over[0, 0] > 0
    received, heavy = lax.optimization_barrier((received, heavy))
    sent, loss = call(
        combine_kernel,
        (packed, shape((ROWS // 128, 128), F32)),
        [full] + sending,
        4 * FEATURES * SLOTS * ROWS,
        "combine",
        20,
        out_specs=(hbm, vmem),
    )(received, place, act, bias)
    received = route(sent)
    loss = sum_loss(loss)

    def packed_plan():
        gradient, row_loss = call(
            gradient_kernel,
            (in_hbm((FEATURES, LOCAL * BLOCK)), in_hbm((ROWS // 128, 128), F32)),
            [
                full,
                pltpu.VMEM((BLOCK, SLOTS), BF16),
                pltpu.VMEM((FEATURES, LOCAL * BLOCK), BF16),
                pltpu.SemaphoreType.DMA((2,)),
            ],
            spread_flops,
            "gradient",
            24,
            out_specs=(hbm, vmem),
        )(received, codes, ids, loss)
        return gradient.T, row_loss.reshape(ROWS)

    return lax.cond(
        heavy,
        lambda: padded_plan(activations, bias_dec, encoder, decoder, active_blocks),
        packed_plan,
    )


def solution(mesh):
    split = jax.sharding.Mesh(mesh.devices.reshape(4, 4, 8, 4), (OUTER, INNER) + PLANE)
    placed = (
        P(PLANE, DP),
        P(DP),
        P(DP, PLANE),
        P(PLANE, DP),
        P(PLANE, None),
    )
    return jax.shard_map(
        on_device,
        mesh=split,
        in_specs=placed,
        out_specs=(P(PLANE, DP), P(PLANE)),
        check_vma=False,
    )
```

```python
import jax
import jax.numpy as jnp
from jax import lax
from jax.experimental import pallas as pl
from jax.experimental.pallas import tpu as pltpu
from jax.sharding import PartitionSpec as P

BLOCK = 64
PLANE = ("latent", "section")
OUTER, INNER = "dp_outer", "dp_inner"
DP = (OUTER, INNER)
GROUPS = 32
SHARDS = 16
LOCAL = 32
ROWS = 512
FEATURES = 288
HALF = FEATURES // 2
NAMED = 4
QUARTERS = 4
SHARE = 16
MAIN = QUARTERS * SHARE
EXTRA = 16
MAIN_SLOTS = GROUPS * MAIN
EXTRA_SLOTS = GROUPS * EXTRA
SLOTS = MAIN_SLOTS + EXTRA_SLOTS
PACKED = HALF + 3 * EXTRA
PAIRS = GROUPS // 2
EARLY = 12
LANE_TILES = SLOTS // 128
CHUNK_TILES = 5
CHUNK_ROWS = 16 * CHUNK_TILES

NT = (((1,), (1,)), ((), ()))
F32 = jnp.float32
BF16 = jnp.bfloat16


def mm(a, b):
    return jnp.dot(a, b, preferred_element_type=F32)


def mm_nt(a, b):
    return lax.dot_general(a, b, NT, preferred_element_type=F32)


def identity(n):
    rows = lax.broadcasted_iota(jnp.int32, (n, n), 0)
    return jnp.where(rows == lax.broadcasted_iota(jnp.int32, (n, n), 1), 1.0, 0.0).astype(BF16)


def lane_offset(tile, width=128):
    return pl.ds(pl.multiple_of(tile * width, width), width)


def exchange(a, b, width):
    kind = jnp.int16 if a.dtype == BF16 else jnp.int32
    lane = lax.broadcasted_iota(kind, a.shape, 1)
    even = jnp.bitwise_and(lane, jnp.full((), 2 * width - 1, kind)) < jnp.full((), width, kind)
    return jnp.where(even, a, pltpu.roll(b, width, 1)), jnp.where(even, pltpu.roll(a, 128 - width, 1), b)


def regroup(tiles):
    a0, a1 = exchange(tiles[0], tiles[1], 32)
    b0, b1 = exchange(tiles[2], tiles[3], 32)
    return *exchange(a0, b0, 16), *exchange(a1, b1, 16)


def ungroup(tiles):
    a0, b0 = exchange(tiles[0], tiles[1], 16)
    a1, b1 = exchange(tiles[2], tiles[3], 16)
    return *exchange(a0, a1, 32), *exchange(b0, b1, 32)


def store_pair(out_ref, pair, values):
    values = values.astype(BF16)
    first, second = exchange(values[:HALF], values[HALF:], MAIN)
    out_ref[pair, 0:HALF, :] = first
    out_ref[pair + PAIRS, 0:HALF, :] = second


def stage_copies(buffer_ref, out_ref, sems, stage, early):
    first, count = (0, early) if stage == 0 else (early, PAIRS - early)
    copies = []
    for side in range(2):
        devices = pl.ds(side * PAIRS + first, count)
        copies.append(
            pltpu.make_async_copy(buffer_ref.at[devices], out_ref.at[devices], sems.at[2 * stage + side])
        )
    return copies


def start_stage(buffer_ref, out_ref, sems, done, early=EARLY):
    if done in (early, PAIRS):
        for copy in stage_copies(buffer_ref, out_ref, sems, 0 if done == early else 1, early):
            copy.start()


def wait_stages(buffer_ref, out_ref, sems, early=EARLY):
    for stage in range(2):
        for copy in stage_copies(buffer_ref, out_ref, sems, stage, early):
            copy.wait()


def bias_column(bias_ref):
    rows = lax.broadcasted_iota(jnp.int32, (FEATURES, FEATURES), 0)
    lanes = lax.broadcasted_iota(jnp.int32, (FEATURES, FEATURES), 1)
    wide = jnp.broadcast_to(bias_ref[...].astype(F32).reshape(1, FEATURES), (FEATURES, FEATURES))
    return jnp.sum(jnp.where(rows == lanes, wide, 0.0), axis=1, keepdims=True)


def store_extra(out_ref, values):
    for part in range(3):
        piece = values[:, part * 128 : (part + 1) * 128].astype(BF16)
        out_ref[:, HALF + part * EXTRA : HALF + (part + 1) * EXTRA, :] = piece.reshape(GROUPS, EXTRA, 128)


def load_pair(in_ref, pair):
    return exchange(in_ref[pair, 0:HALF, :], in_ref[pair + PAIRS, 0:HALF, :], MAIN)


def unpack(in_ref, full_ref):
    for pair in range(PAIRS):
        top, bottom = load_pair(in_ref, pair)
        full_ref[0:HALF, pair * 128 : (pair + 1) * 128] = top
        full_ref[HALF:, pair * 128 : (pair + 1) * 128] = bottom
    unpack_extra(in_ref, full_ref)


def unpack_grouped(in_ref, full_ref):
    for quad in range(4):
        pairs = [load_pair(in_ref, 4 * quad + j) for j in range(4)]
        for half in range(2):
            tiles = regroup([pair[half] for pair in pairs])
            for quarter in range(QUARTERS):
                tile = 4 * quarter + quad
                full_ref[half * HALF : (half + 1) * HALF, tile * 128 : (tile + 1) * 128] = tiles[quarter]
    return unpack_extra(in_ref, full_ref)


def unpack_extra(in_ref, full_ref):
    eye = identity(128)
    turned, last = None, None
    for part in range(3):
        last = in_ref[:, HALF + part * EXTRA : HALF + (part + 1) * EXTRA, :].reshape(EXTRA_SLOTS, 128)
        turned = mm_nt(eye, last)
        height = min(128, FEATURES - part * 128)
        full_ref[part * 128 : part * 128 + height, MAIN_SLOTS:] = turned[:height].astype(BF16)
    return last, turned


def placed(slots, names, start, count):
    index = lax.broadcasted_iota(jnp.int16, (count, ROWS), 0) + jnp.int16(start)
    named = jnp.zeros((count, ROWS), BF16)
    for k in range(NAMED):
        named = jnp.where(index == jnp.broadcast_to(slots[k], index.shape), names[k], named)
    return named, jnp.minimum(named, BF16(1))


def prepare_kernel(act_ref, bias_ref, blocks_ref, out_ref, slots_ref, send_ref, sems):
    blocks = blocks_ref[...]
    group = lax.shift_right_logical(blocks, 3)
    local = jnp.bitwise_and(blocks, LOCAL - 1)
    count = GROUPS * QUARTERS
    groups = lax.broadcasted_iota(jnp.int32, (count, ROWS), 0)
    hits = [groups == group[k : k + 1, :] for k in range(NAMED)]
    counts = sum(jnp.where(hit, 1.0, 0.0) for hit in hits).astype(BF16)
    before = lax.broadcasted_iota(jnp.int32, (ROWS, ROWS), 0) < lax.broadcasted_iota(jnp.int32, (ROWS, ROWS), 1)
    earlier = mm(counts, jnp.where(before, 1.0, 0.0).astype(BF16))
    beyond = jnp.maximum(mm(counts, jnp.ones((ROWS, 128), BF16)) - SHARE, 0.0).astype(BF16)
    one = lax.broadcasted_iota(jnp.int32, (count, count), 0)
    other = lax.broadcasted_iota(jnp.int32, (count, count), 1)
    same = lax.shift_right_logical(one, 2) == lax.shift_right_logical(other, 2)
    offset = mm(jnp.where(same & (other < one), 1.0, 0.0).astype(BF16), beyond)
    table = earlier + 1024.0 * jnp.concatenate([offset] * (ROWS // 128), axis=1)
    slots, names, most = [], [], jnp.zeros((1, ROWS), jnp.int32)
    for k in range(NAMED):
        mine = group[k : k + 1, :]
        found = jnp.sum(jnp.where(hits[k], table, 0.0), axis=0, keepdims=True).astype(jnp.int32)
        rank = jnp.bitwise_and(found, 1023)
        for previous in range(k):
            rank = rank + jnp.where(group[previous : previous + 1, :] == mine, 1, 0)
        target = lax.shift_right_logical(mine, 2)
        place = (jnp.bitwise_and(target, PAIRS - 1) * 2 + lax.shift_right_logical(target, 4)) * MAIN
        main = place + jnp.bitwise_and(mine, QUARTERS - 1) * SHARE + rank
        extra = lax.shift_right_logical(found, 10) + rank - SHARE
        late = jnp.where(extra < EXTRA, MAIN_SLOTS + target * EXTRA + extra, -1)
        slots.append(jnp.where(rank < SHARE, main, late))
        names.append((local[k : k + 1, :] + 1).astype(F32).astype(BF16))
        most = jnp.maximum(most, jnp.where(rank < SHARE, 0, extra))
    over = jnp.where(jnp.max(most, axis=1, keepdims=True) >= EXTRA, 1.0, 0.0)
    shifted = (act_ref[...].astype(F32) - bias_column(bias_ref)).astype(BF16)

    for k in range(NAMED):
        slots_ref[k : k + 1, :] = slots[k]
    slots_ref[NAMED:, :] = jnp.zeros((8 - NAMED, ROWS), jnp.int32)
    slots = [slot.astype(jnp.int16) for slot in slots]
    named, place = placed(slots, names, MAIN_SLOTS, EXTRA_SLOTS)
    padded = jnp.concatenate([shifted, jnp.zeros((96, ROWS), BF16)], axis=0)
    values = mm_nt(place, padded)
    store_extra(send_ref, values)
    lane = lax.broadcasted_iota(jnp.int32, (EXTRA_SLOTS, 128), 1)
    ids = mm(named, jnp.ones((ROWS, 128), BF16))
    last = jnp.where(lane == 32, ids, values[:, 256:])
    row = lax.broadcasted_iota(jnp.int32, (EXTRA, 128), 0)
    high = lax.broadcasted_iota(jnp.int32, (EXTRA, 128), 1) >= MAIN
    flag = jnp.broadcast_to(over, (EXTRA, 128))
    for double in range(PAIRS // 2):
        named, place = placed(slots, names, double * 256, 256)
        values = mm_nt(shifted, place)
        ids = mm_nt(jnp.ones((EXTRA, ROWS), BF16), named)
        for side in range(2):
            pair = 2 * double + side
            store_pair(send_ref, pair, values[:, side * 128 : (side + 1) * 128])
            for half in range(2):
                device = pair + half * PAIRS
                mine = ids[:, side * 128 : (side + 1) * 128]
                mine = mine if half else pltpu.roll(mine, MAIN, 1)
                tile = last[device * EXTRA : (device + 1) * EXTRA]
                tile = jnp.where(high & (row == 0), mine, tile)
                tile = jnp.where(high & (row == 1), flag, tile)
                send_ref[device, HALF + 2 * EXTRA :, :] = tile.astype(BF16)
        start_stage(send_ref, out_ref, sems, 2 * double + 2)
    wait_stages(send_ref, out_ref, sems)


def place_kernel(slots_ref, place_ref):
    slots = [slots_ref[k : k + 1, :].astype(jnp.int16) for k in range(NAMED)]
    ones = [jnp.ones((1, ROWS), BF16)] * NAMED
    for start in range(0, SLOTS, 256):
        place_ref[start : start + 256, :] = placed(slots, ones, start, 256)[0]


def encode_kernel(recv_ref, enc_ref, rest_ref, out_ref, ids_ref, over_ref, full_ref):
    last, turned = unpack_grouped(recv_ref, full_ref)
    pick = lax.broadcasted_iota(jnp.int32, (2 * GROUPS, EXTRA_SLOTS), 0)
    column = lax.broadcasted_iota(jnp.int32, (2 * GROUPS, EXTRA_SLOTS), 1)
    wanted = jnp.where(pick < GROUPS, pick * EXTRA, (pick - GROUPS) * EXTRA + 1)
    rows = mm(jnp.where(column == wanted, 1.0, 0.0).astype(BF16), last)
    first, second = rows[:PAIRS], rows[PAIRS:GROUPS]
    low = lax.broadcasted_iota(jnp.int32, (PAIRS, 128), 1) < MAIN
    named = jnp.where(low, pltpu.roll(first, MAIN, 1), second)
    picked = [[named[4 * quad + j : 4 * quad + j + 1] for quad in range(4)] for j in range(4)]
    tiles = regroup([jnp.concatenate(some, axis=0) for some in picked])
    for quarter in range(QUARTERS):
        ids_ref[4 * quarter : 4 * quarter + 4, :] = tiles[quarter]
    for part in range(EXTRA_SLOTS // 128):
        ids_ref[PAIRS + part : PAIRS + part + 1, :] = turned[32:33, part * 128 : (part + 1) * 128]
    ids_ref[LANE_TILES:, :] = jnp.zeros((24 - LANE_TILES, 128), F32)
    flags = jnp.where(lax.broadcasted_iota(jnp.int32, (GROUPS, 128), 1) == MAIN, rows[GROUPS:], 0.0)
    flag = jnp.max(jnp.max(flags, axis=1, keepdims=True), axis=0, keepdims=True)
    over_ref[...] = jnp.broadcast_to(flag, (8, 128)).astype(jnp.int32)

    for tile in range(LANE_TILES // 2):
        lanes = slice(tile * 256, (tile + 1) * 256)
        ids = jnp.concatenate([ids_ref[2 * tile : 2 * tile + 1, :], ids_ref[2 * tile + 1 : 2 * tile + 2, :]], axis=1)
        code = ids.astype(jnp.int32) - 1
        main = tile < PAIRS // 2
        quarter = tile // 2 if main else 0
        first, held = (8 * quarter, 8) if main else (0, LOCAL)
        part = mm(enc_ref[first * BLOCK : (first + held) * BLOCK, :], full_ref[0:256, lanes])
        total = jnp.zeros((BLOCK, 256), F32)
        for b in range(held):
            total = jnp.where(code == first + b, part[b * BLOCK : (b + 1) * BLOCK], total)
        rest = full_ref[256:, lanes]
        member = jnp.broadcast_to(jnp.bitwise_and(code, 7), (32, 256))
        spread = jnp.concatenate([jnp.where(member == m, rest, BF16(0)) for m in range(8)], axis=0)
        if main:
            more = mm(rest_ref[quarter * BLOCK : (quarter + 1) * BLOCK, :], spread)
        else:
            part = mm(rest_ref[...], spread)
            more = jnp.zeros((BLOCK, 256), F32)
            for g in range(QUARTERS):
                wanted = lax.shift_right_arithmetic(code, 3) == g
                more = jnp.where(wanted, part[g * BLOCK : (g + 1) * BLOCK], more)
        total = total + more
        for half in range(2):
            lane_tile = 2 * tile + half
            slot_row = (lane_tile % CHUNK_TILES) * 16
            for quarter in range(4):
                piece = total[quarter * 16 : (quarter + 1) * 16, half * 128 : (half + 1) * 128]
                out_ref[quarter + 4 * (lane_tile // CHUNK_TILES), slot_row : slot_row + 16, :] = piece.astype(BF16)


def load_codes(codes_ref, full_ref):
    for tile in range(LANE_TILES):
        for quarter in range(4):
            full_ref[quarter * 16 : (quarter + 1) * 16, tile * 128 : (tile + 1) * 128] = codes_ref[
                quarter + 4 * (tile // CHUNK_TILES),
                (tile % CHUNK_TILES) * 16 : (tile % CHUNK_TILES + 1) * 16,
                :,
            ]


def decode_kernel(codes_ref, ids_ref, dec_ref, out_ref, full_ref, extra_ref, send_ref, sems):
    load_codes(codes_ref, full_ref)

    def contribution(tile):
        codes = full_ref[:, tile * 256 : (tile + 1) * 256]
        ids = jnp.concatenate([ids_ref[2 * tile : 2 * tile + 1, :], ids_ref[2 * tile + 1 : 2 * tile + 2, :]], axis=1)
        ids = jnp.broadcast_to(ids, (BLOCK, 256)).astype(BF16)
        main = tile < PAIRS // 2
        first, held = (8 * (tile // 2), 8) if main else (0, LOCAL)
        spread = [jnp.where(ids == BF16(b + 1), codes, BF16(0)) for b in range(first, first + held)]
        weights = dec_ref[:, first * BLOCK : (first + held) * BLOCK]
        return mm(weights, jnp.concatenate(spread, axis=0)).astype(BF16)

    extra_ref[FEATURES:, :] = jnp.zeros((384 - FEATURES, EXTRA_SLOTS), BF16)
    for tile in range(PAIRS // 2, LANE_TILES // 2):
        start = tile * 256 - MAIN_SLOTS
        extra_ref[0:FEATURES, start : start + 256] = contribution(tile)
    store_extra(send_ref, mm_nt(identity(EXTRA_SLOTS), extra_ref[...]))
    for double in range(2):
        values = [contribution(2 * quarter + double) for quarter in range(QUARTERS)]
        for side in range(2):
            lanes = slice(side * 128, (side + 1) * 128)
            tops = ungroup([value[:HALF, lanes] for value in values])
            bottoms = ungroup([value[HALF:, lanes] for value in values])
            for j in range(4):
                pair = 8 * double + 4 * side + j
                first, second = exchange(tops[j], bottoms[j], MAIN)
                send_ref[pair, 0:HALF, :] = first
                send_ref[pair + PAIRS, 0:HALF, :] = second
        start_stage(send_ref, out_ref, sems, 8 * double + 8, 8)
    wait_stages(send_ref, out_ref, sems, 8)


def combine_kernel(recv_ref, place_ref, act_ref, bias_ref, out_ref, loss_ref, full_ref, send_ref, sems):
    unpack(recv_ref, full_ref)
    error = mm(full_ref[...], place_ref[...]) + bias_column(bias_ref) - act_ref[...].astype(F32)
    sent = error.astype(BF16)
    padded = jnp.concatenate([sent, jnp.zeros((96, ROWS), BF16)], axis=0)
    store_extra(send_ref, mm_nt(place_ref[MAIN_SLOTS:, :], padded))
    for double in range(PAIRS // 2):
        values = mm_nt(sent, place_ref[double * 256 : (double + 1) * 256, :])
        store_pair(send_ref, 2 * double, values[:, :128])
        store_pair(send_ref, 2 * double + 1, values[:, 128:])
        start_stage(send_ref, out_ref, sems, 2 * double + 2)
    loss = jnp.sum(error * error, axis=0, keepdims=True)
    for part in range(ROWS // 128):
        loss_ref[part : part + 1, :] = loss[:, part * 128 : (part + 1) * 128]
    wait_stages(send_ref, out_ref, sems)


def gradient_kernel(
    recv_ref, codes_ref, ids_ref, loss_ref, out_ref, out_loss_ref, full_ref, code_ref, grad_ref, sems
):
    out_loss_ref[...] = loss_ref[...]
    unpack_grouped(recv_ref, full_ref)
    load_codes(codes_ref, code_ref)
    ids = jnp.concatenate([ids_ref[tile : tile + 1, :] for tile in range(LANE_TILES)], axis=1)
    ids = jnp.broadcast_to(ids, (BLOCK, SLOTS)).astype(BF16)
    copies, begin = [], 0
    for start in range(0, LOCAL * BLOCK, 256):
        stop = start + 256
        width = MAIN_SLOTS // QUARTERS
        lanes = slice(start // 512 * width, (start // 512 + 1) * width)

        def both(values):
            return jnp.concatenate([values[:, lanes], values[:, MAIN_SLOTS:]], axis=1)

        near, codes = both(ids), both(code_ref)
        spread = [jnp.where(near == BF16(b + 1), codes, BF16(0)) for b in range(start // BLOCK, stop // BLOCK)]
        grad_ref[:, start:stop] = mm_nt(both(full_ref), jnp.concatenate(spread, axis=0)).astype(BF16)
        if stop in (LOCAL * BLOCK * 3 // 4, LOCAL * BLOCK):
            lanes = pl.ds(begin, stop - begin)
            copy = pltpu.make_async_copy(grad_ref.at[:, lanes], out_ref.at[:, lanes], sems.at[len(copies)])
            copy.start()
            copies.append(copy)
            begin = stop
    for copy in copies:
        copy.wait()


def call(kernel, out_shape, scratch, flops, name, megabytes, **specs):
    return pl.pallas_call(
        kernel,
        out_shape=out_shape,
        scratch_shapes=scratch,
        name=name,
        **specs,
        compiler_params=pltpu.CompilerParams(vmem_limit_bytes=megabytes * 1024 * 1024),
        cost_estimate=pl.CostEstimate(flops=flops, bytes_accessed=6_000_000, transcendentals=0),
    )


def shape(dims, dtype=BF16):
    return jax.ShapeDtypeStruct(dims, dtype)


def in_hbm(dims, dtype=BF16):
    return pltpu.HBM(dims, dtype)


def route(buffer):
    return lax.all_to_all(buffer, PLANE, split_axis=0, concat_axis=0, tiled=True)


def sum_codes(partial):
    received = lax.all_to_all(partial, DP, split_axis=0, concat_axis=0, tiled=True)
    total = jnp.sum(received.astype(F32), axis=0)
    codes = jnp.maximum(total, 0.0).astype(BF16)
    copies = jnp.broadcast_to(codes[None], (SHARDS,) + codes.shape)
    return lax.all_to_all(copies, DP, split_axis=0, concat_axis=0, tiled=True)


def sum_loss(part):
    return lax.psum(lax.psum(part, INNER), OUTER)


def padded_plan(activations, bias_dec, encoder, decoder, active_blocks):
    row_count, shard_width = activations.shape
    per_row = active_blocks.shape[1]
    groups = lax.axis_size(PLANE)
    local_blocks = encoder.shape[1] // BLOCK
    total_blocks = local_blocks * groups
    capacity = max(2, 2 * row_count * per_row // total_blocks)
    slot_count = total_blocks * capacity
    pair_blocks = active_blocks.reshape(-1)
    pair_iota = jnp.arange(pair_blocks.shape[0], dtype=jnp.int32)
    same_block = pair_blocks[:, None] == pair_blocks[None, :]
    earlier = pair_iota[None, :] < pair_iota[:, None]
    block_rank = jnp.sum((same_block & earlier).astype(jnp.int32), axis=1)
    slot_index = (pair_blocks * capacity + block_rank).reshape(row_count, per_row)
    slot_iota = jnp.arange(slot_count, dtype=jnp.int32)
    placement = jnp.zeros((slot_count, row_count), BF16)
    for which in range(per_row):
        placement = placement + (slot_index[:, which][None, :] == slot_iota[:, None]).astype(BF16)
    slot_shape = (groups, local_blocks, capacity, shard_width)

    def scatter_rows(values):
        filled = jnp.dot(placement, values, preferred_element_type=F32).astype(values.dtype)
        return filled.reshape(slot_shape)

    bias_wide = bias_dec.astype(F32)[None, :]
    shifted = (activations.astype(F32) - bias_wide).astype(BF16)
    received = route(scatter_rows(shifted))
    enc_local = encoder.reshape(shard_width, local_blocks, BLOCK)
    partial_pre = jnp.einsum("sbkd,dbl->sbkl", received, enc_local, preferred_element_type=F32)
    pre_total = lax.psum(partial_pre, DP)
    latent_codes = jnp.maximum(pre_total, 0.0).astype(BF16)
    dec_local = decoder.reshape(local_blocks, BLOCK, shard_width)
    contrib = jnp.einsum("sbkl,bld->sbkd", latent_codes, dec_local, preferred_element_type=F32).astype(BF16)
    returned = route(contrib).reshape(slot_count, shard_width)
    summed_rows = jnp.einsum("sr,sd->rd", placement, returned, preferred_element_type=F32)
    error = summed_rows + bias_wide - activations.astype(F32)
    row_loss = lax.psum(jnp.sum(error * error, axis=1), DP)
    error_sent = route(scatter_rows(error.astype(BF16)))
    gradient = jnp.einsum("sbkl,sbkd->bld", latent_codes, error_sent, preferred_element_type=F32)
    return gradient.reshape(local_blocks * BLOCK, shard_width).astype(BF16), row_loss


def on_device(activations, bias_dec, encoder, decoder, active_blocks):
    act = activations.T
    bias = bias_dec
    packed = in_hbm((GROUPS, PACKED, 128))
    full = pltpu.VMEM((FEATURES, SLOTS), BF16)
    sending = [pltpu.VMEM((GROUPS, PACKED, 128), BF16), pltpu.SemaphoreType.DMA((4,))]
    vmem, hbm = pl.BlockSpec(memory_space=pltpu.VMEM), pl.BlockSpec(memory_space=pltpu.HBM)
    spread_flops = 2 * FEATURES * SLOTS * LOCAL * BLOCK
    sent, slots = call(
        prepare_kernel,
        (packed, shape((8, ROWS), jnp.int32)),
        sending,
        2 * FEATURES * SLOTS * ROWS,
        "prepare",
        20,
        out_specs=(hbm, vmem),
    )(act, bias, active_blocks.T)
    received = route(sent)
    place = call(place_kernel, shape((SLOTS, ROWS)), [], 0, "place", 16)(slots)
    turned = encoder.T
    rest = turned[:, 256:].reshape(4, 8, BLOCK, 32).transpose(0, 2, 1, 3).reshape(4 * BLOCK, 256)
    partial, ids, over = call(
        encode_kernel,
        (shape((SHARDS, CHUNK_ROWS, 128)), shape((24, 128), F32), shape((8, 128), jnp.int32)),
        [full],
        spread_flops,
        "encode",
        20,
    )(received, turned[:, :256], rest)
    codes = sum_codes(partial)
    sent = call(
        decode_kernel,
        packed,
        [
            pltpu.VMEM((BLOCK, SLOTS), BF16),
            pltpu.VMEM((384, EXTRA_SLOTS), BF16),
        ]
        + sending,
        spread_flops,
        "decode",
        20,
        out_specs=hbm,
    )(codes, ids, decoder.T)
    received = route(sent)
    heavy = over[0, 0] > 0
    place, heavy = lax.optimization_barrier((place, heavy))
    sent, loss = call(
        combine_kernel,
        (packed, shape((ROWS // 128, 128), F32)),
        [full] + sending,
        4 * FEATURES * SLOTS * ROWS,
        "combine",
        20,
        out_specs=(hbm, vmem),
    )(received, place, act, bias)
    received = route(sent)
    loss = sum_loss(loss)

    def packed_plan():
        gradient, row_loss = call(
            gradient_kernel,
            (in_hbm((FEATURES, LOCAL * BLOCK)), in_hbm((ROWS // 128, 128), F32)),
            [
                full,
                pltpu.VMEM((BLOCK, SLOTS), BF16),
                pltpu.VMEM((FEATURES, LOCAL * BLOCK), BF16),
                pltpu.SemaphoreType.DMA((2,)),
            ],
            spread_flops,
            "gradient",
            24,
            out_specs=(hbm, vmem),
        )(received, codes, ids, loss)
        return gradient.T, row_loss.reshape(ROWS)

    return lax.cond(
        heavy,
        lambda: padded_plan(activations, bias_dec, encoder, decoder, active_blocks),
        packed_plan,
    )


def solution(mesh):
    split = jax.sharding.Mesh(mesh.devices.reshape(4, 4, 8, 4), (OUTER, INNER) + PLANE)
    placed = (
        P(PLANE, DP),
        P(DP),
        P(DP, PLANE),
        P(PLANE, DP),
        P(PLANE, None),
    )
    return jax.shard_map(
        on_device,
        mesh=split,
        in_specs=placed,
        out_specs=(P(PLANE, DP), P(PLANE)),
        check_vma=False,
    )
```

```python
import jax
import jax.numpy as jnp
from jax import lax
from jax.experimental import pallas as pl
from jax.experimental.pallas import tpu as pltpu
from jax.sharding import PartitionSpec as P

BLOCK = 64
PLANE = ("latent", "section")
OUTER, INNER = "dp_outer", "dp_inner"
DP = (OUTER, INNER)
GROUPS = 32
SHARDS = 16
LOCAL = 32
ROWS = 512
FEATURES = 288
HALF = FEATURES // 2
NAMED = 4
QUARTERS = 4
SHARE = 16
MAIN = QUARTERS * SHARE
EXTRA = 16
MAIN_SLOTS = GROUPS * MAIN
EXTRA_SLOTS = GROUPS * EXTRA
SLOTS = MAIN_SLOTS + EXTRA_SLOTS
PACKED = HALF + 3 * EXTRA
PAIRS = GROUPS // 2
EARLY = 12
LANE_TILES = SLOTS // 128
CHUNK_TILES = 5
CHUNK_ROWS = 16 * CHUNK_TILES

NT = (((1,), (1,)), ((), ()))
F32 = jnp.float32
BF16 = jnp.bfloat16


def mm(a, b):
    return jnp.dot(a, b, preferred_element_type=F32)


def mm_nt(a, b):
    return lax.dot_general(a, b, NT, preferred_element_type=F32)


def identity(n):
    rows = lax.broadcasted_iota(jnp.int32, (n, n), 0)
    return jnp.where(rows == lax.broadcasted_iota(jnp.int32, (n, n), 1), 1.0, 0.0).astype(BF16)


def lane_offset(tile, width=128):
    return pl.ds(pl.multiple_of(tile * width, width), width)


def exchange(a, b, width):
    kind = jnp.int16 if a.dtype == BF16 else jnp.int32
    lane = lax.broadcasted_iota(kind, a.shape, 1)
    even = jnp.bitwise_and(lane, jnp.full((), 2 * width - 1, kind)) < jnp.full((), width, kind)
    return jnp.where(even, a, pltpu.roll(b, width, 1)), jnp.where(even, pltpu.roll(a, 128 - width, 1), b)


def regroup(tiles):
    a0, a1 = exchange(tiles[0], tiles[1], 32)
    b0, b1 = exchange(tiles[2], tiles[3], 32)
    return *exchange(a0, b0, 16), *exchange(a1, b1, 16)


def ungroup(tiles):
    a0, b0 = exchange(tiles[0], tiles[1], 16)
    a1, b1 = exchange(tiles[2], tiles[3], 16)
    return *exchange(a0, a1, 32), *exchange(b0, b1, 32)


def store_pair(out_ref, pair, values):
    values = values.astype(BF16)
    first, second = exchange(values[:HALF], values[HALF:], MAIN)
    out_ref[pair, 0:HALF, :] = first
    out_ref[pair + PAIRS, 0:HALF, :] = second


def stage_copies(buffer_ref, out_ref, sems, stage, early):
    first, count = (0, early) if stage == 0 else (early, PAIRS - early)
    copies = []
    for side in range(2):
        devices = pl.ds(side * PAIRS + first, count)
        copies.append(
            pltpu.make_async_copy(buffer_ref.at[devices], out_ref.at[devices], sems.at[2 * stage + side])
        )
    return copies


def start_stage(buffer_ref, out_ref, sems, done, early=EARLY):
    if done in (early, PAIRS):
        for copy in stage_copies(buffer_ref, out_ref, sems, 0 if done == early else 1, early):
            copy.start()


def wait_stages(buffer_ref, out_ref, sems, early=EARLY):
    for stage in range(2):
        for copy in stage_copies(buffer_ref, out_ref, sems, stage, early):
            copy.wait()


def bias_column(bias_ref):
    rows = lax.broadcasted_iota(jnp.int32, (FEATURES, FEATURES), 0)
    lanes = lax.broadcasted_iota(jnp.int32, (FEATURES, FEATURES), 1)
    wide = jnp.broadcast_to(bias_ref[...].astype(F32).reshape(1, FEATURES), (FEATURES, FEATURES))
    return jnp.sum(jnp.where(rows == lanes, wide, 0.0), axis=1, keepdims=True)


def store_extra(out_ref, values):
    for part in range(3):
        piece = values[:, part * 128 : (part + 1) * 128].astype(BF16)
        out_ref[:, HALF + part * EXTRA : HALF + (part + 1) * EXTRA, :] = piece.reshape(GROUPS, EXTRA, 128)


def load_pair(in_ref, pair):
    return exchange(in_ref[pair, 0:HALF, :], in_ref[pair + PAIRS, 0:HALF, :], MAIN)


def unpack(in_ref, full_ref):
    for pair in range(PAIRS):
        top, bottom = load_pair(in_ref, pair)
        full_ref[0:HALF, pair * 128 : (pair + 1) * 128] = top
        full_ref[HALF:, pair * 128 : (pair + 1) * 128] = bottom
    unpack_extra(in_ref, full_ref)


def unpack_grouped(in_ref, full_ref):
    for quad in range(4):
        pairs = [load_pair(in_ref, 4 * quad + j) for j in range(4)]
        for half in range(2):
            tiles = regroup([pair[half] for pair in pairs])
            for quarter in range(QUARTERS):
                tile = 4 * quarter + quad
                full_ref[half * HALF : (half + 1) * HALF, tile * 128 : (tile + 1) * 128] = tiles[quarter]
    return unpack_extra(in_ref, full_ref)


def unpack_extra(in_ref, full_ref):
    eye = identity(128)
    turned, last = None, None
    for part in range(3):
        last = in_ref[:, HALF + part * EXTRA : HALF + (part + 1) * EXTRA, :].reshape(EXTRA_SLOTS, 128)
        turned = mm_nt(eye, last)
        height = min(128, FEATURES - part * 128)
        full_ref[part * 128 : part * 128 + height, MAIN_SLOTS:] = turned[:height].astype(BF16)
    return last, turned


def placed(slots, names, start, count):
    index = lax.broadcasted_iota(jnp.int16, (count, ROWS), 0) + jnp.int16(start)
    named = jnp.zeros((count, ROWS), BF16)
    for k in range(NAMED):
        named = jnp.where(index == jnp.broadcast_to(slots[k], index.shape), names[k], named)
    return named, jnp.minimum(named, BF16(1))


def prepare_kernel(act_ref, bias_ref, blocks_ref, out_ref, slots_ref, send_ref, sems):
    blocks = blocks_ref[...]
    group = lax.shift_right_logical(blocks, 3)
    local = jnp.bitwise_and(blocks, LOCAL - 1)
    count = GROUPS * QUARTERS
    groups = lax.broadcasted_iota(jnp.int32, (count, ROWS), 0)
    hits = [groups == group[k : k + 1, :] for k in range(NAMED)]
    counts = sum(jnp.where(hit, 1.0, 0.0) for hit in hits).astype(BF16)
    before = lax.broadcasted_iota(jnp.int32, (ROWS, ROWS), 0) < lax.broadcasted_iota(jnp.int32, (ROWS, ROWS), 1)
    earlier = mm(counts, jnp.where(before, 1.0, 0.0).astype(BF16))
    beyond = jnp.maximum(mm(counts, jnp.ones((ROWS, 128), BF16)) - SHARE, 0.0).astype(BF16)
    one = lax.broadcasted_iota(jnp.int32, (count, count), 0)
    other = lax.broadcasted_iota(jnp.int32, (count, count), 1)
    same = lax.shift_right_logical(one, 2) == lax.shift_right_logical(other, 2)
    offset = mm(jnp.where(same & (other < one), 1.0, 0.0).astype(BF16), beyond)
    table = earlier + 1024.0 * jnp.concatenate([offset] * (ROWS // 128), axis=1)
    slots, names, most = [], [], jnp.zeros((1, ROWS), jnp.int32)
    for k in range(NAMED):
        mine = group[k : k + 1, :]
        found = jnp.sum(jnp.where(hits[k], table, 0.0), axis=0, keepdims=True).astype(jnp.int32)
        rank = jnp.bitwise_and(found, 1023)
        for previous in range(k):
            rank = rank + jnp.where(group[previous : previous + 1, :] == mine, 1, 0)
        target = lax.shift_right_logical(mine, 2)
        place = (jnp.bitwise_and(target, PAIRS - 1) * 2 + lax.shift_right_logical(target, 4)) * MAIN
        main = place + jnp.bitwise_and(mine, QUARTERS - 1) * SHARE + rank
        extra = lax.shift_right_logical(found, 10) + rank - SHARE
        late = jnp.where(extra < EXTRA, MAIN_SLOTS + target * EXTRA + extra, -1)
        slots.append(jnp.where(rank < SHARE, main, late))
        names.append((local[k : k + 1, :] + 1).astype(F32).astype(BF16))
        most = jnp.maximum(most, jnp.where(rank < SHARE, 0, extra))
    over = jnp.where(jnp.max(most, axis=1, keepdims=True) >= EXTRA, 1.0, 0.0)
    shifted = (act_ref[...].astype(F32) - bias_column(bias_ref)).astype(BF16)

    for k in range(NAMED):
        slots_ref[k : k + 1, :] = slots[k]
    slots_ref[NAMED:, :] = jnp.zeros((8 - NAMED, ROWS), jnp.int32)
    slots = [slot.astype(jnp.int16) for slot in slots]
    named, place = placed(slots, names, MAIN_SLOTS, EXTRA_SLOTS)
    padded = jnp.concatenate([shifted, jnp.zeros((96, ROWS), BF16)], axis=0)
    values = mm_nt(place, padded)
    store_extra(send_ref, values)
    lane = lax.broadcasted_iota(jnp.int32, (EXTRA_SLOTS, 128), 1)
    ids = mm(named, jnp.ones((ROWS, 128), BF16))
    last = jnp.where(lane == 32, ids, values[:, 256:])
    row = lax.broadcasted_iota(jnp.int32, (EXTRA, 128), 0)
    high = lax.broadcasted_iota(jnp.int32, (EXTRA, 128), 1) >= MAIN
    flag = jnp.broadcast_to(over, (EXTRA, 128))
    for double in range(PAIRS // 2):
        named, place = placed(slots, names, double * 256, 256)
        values = mm_nt(shifted, place)
        ids = mm_nt(jnp.ones((EXTRA, ROWS), BF16), named)
        for side in range(2):
            pair = 2 * double + side
            store_pair(send_ref, pair, values[:, side * 128 : (side + 1) * 128])
            for half in range(2):
                device = pair + half * PAIRS
                mine = ids[:, side * 128 : (side + 1) * 128]
                mine = mine if half else pltpu.roll(mine, MAIN, 1)
                tile = last[device * EXTRA : (device + 1) * EXTRA]
                tile = jnp.where(high & (row == 0), mine, tile)
                tile = jnp.where(high & (row == 1), flag, tile)
                send_ref[device, HALF + 2 * EXTRA :, :] = tile.astype(BF16)
        start_stage(send_ref, out_ref, sems, 2 * double + 2)
    wait_stages(send_ref, out_ref, sems)


def encode_kernel(recv_ref, enc_ref, rest_ref, out_ref, ids_ref, over_ref, full_ref):
    last, turned = unpack_grouped(recv_ref, full_ref)
    pick = lax.broadcasted_iota(jnp.int32, (2 * GROUPS, EXTRA_SLOTS), 0)
    column = lax.broadcasted_iota(jnp.int32, (2 * GROUPS, EXTRA_SLOTS), 1)
    wanted = jnp.where(pick < GROUPS, pick * EXTRA, (pick - GROUPS) * EXTRA + 1)
    rows = mm(jnp.where(column == wanted, 1.0, 0.0).astype(BF16), last)
    first, second = rows[:PAIRS], rows[PAIRS:GROUPS]
    low = lax.broadcasted_iota(jnp.int32, (PAIRS, 128), 1) < MAIN
    named = jnp.where(low, pltpu.roll(first, MAIN, 1), second)
    picked = [[named[4 * quad + j : 4 * quad + j + 1] for quad in range(4)] for j in range(4)]
    tiles = regroup([jnp.concatenate(some, axis=0) for some in picked])
    for quarter in range(QUARTERS):
        ids_ref[4 * quarter : 4 * quarter + 4, :] = tiles[quarter]
    for part in range(EXTRA_SLOTS // 128):
        ids_ref[PAIRS + part : PAIRS + part + 1, :] = turned[32:33, part * 128 : (part + 1) * 128]
    ids_ref[LANE_TILES:, :] = jnp.zeros((24 - LANE_TILES, 128), F32)
    flags = jnp.where(lax.broadcasted_iota(jnp.int32, (GROUPS, 128), 1) == MAIN, rows[GROUPS:], 0.0)
    flag = jnp.max(jnp.max(flags, axis=1, keepdims=True), axis=0, keepdims=True)
    over_ref[0, 0] = jnp.max(flag).astype(jnp.int32)

    for tile in range(LANE_TILES // 2):
        lanes = slice(tile * 256, (tile + 1) * 256)
        ids = jnp.concatenate([ids_ref[2 * tile : 2 * tile + 1, :], ids_ref[2 * tile + 1 : 2 * tile + 2, :]], axis=1)
        code = ids.astype(jnp.int32) - 1
        main = tile < PAIRS // 2
        quarter = tile // 2 if main else 0
        first, held = (8 * quarter, 8) if main else (0, LOCAL)
        part = mm(enc_ref[first * BLOCK : (first + held) * BLOCK, :], full_ref[0:256, lanes])
        total = jnp.zeros((BLOCK, 256), F32)
        for b in range(held):
            total = jnp.where(code == first + b, part[b * BLOCK : (b + 1) * BLOCK], total)
        rest = full_ref[256:, lanes]
        member = jnp.broadcast_to(jnp.bitwise_and(code, 7), (32, 256))
        spread = jnp.concatenate([jnp.where(member == m, rest, BF16(0)) for m in range(8)], axis=0)
        if main:
            more = mm(rest_ref[quarter * BLOCK : (quarter + 1) * BLOCK, :], spread)
        else:
            part = mm(rest_ref[...], spread)
            more = jnp.zeros((BLOCK, 256), F32)
            for g in range(QUARTERS):
                wanted = lax.shift_right_arithmetic(code, 3) == g
                more = jnp.where(wanted, part[g * BLOCK : (g + 1) * BLOCK], more)
        total = total + more
        for half in range(2):
            lane_tile = 2 * tile + half
            slot_row = (lane_tile % CHUNK_TILES) * 16
            for quarter in range(4):
                piece = total[quarter * 16 : (quarter + 1) * 16, half * 128 : (half + 1) * 128]
                out_ref[quarter + 4 * (lane_tile // CHUNK_TILES), slot_row : slot_row + 16, :] = piece.astype(BF16)


def load_codes(codes_ref, full_ref):
    for tile in range(LANE_TILES):
        for quarter in range(4):
            full_ref[quarter * 16 : (quarter + 1) * 16, tile * 128 : (tile + 1) * 128] = codes_ref[
                quarter + 4 * (tile // CHUNK_TILES),
                (tile % CHUNK_TILES) * 16 : (tile % CHUNK_TILES + 1) * 16,
                :,
            ]


def decode_kernel(codes_ref, ids_ref, dec_ref, send_ref, full_ref, extra_ref):
    load_codes(codes_ref, full_ref)

    def contribution(tile):
        codes = full_ref[:, tile * 256 : (tile + 1) * 256]
        ids = jnp.concatenate([ids_ref[2 * tile : 2 * tile + 1, :], ids_ref[2 * tile + 1 : 2 * tile + 2, :]], axis=1)
        ids = jnp.broadcast_to(ids, (BLOCK, 256)).astype(BF16)
        main = tile < PAIRS // 2
        first, held = (8 * (tile // 2), 8) if main else (0, LOCAL)
        spread = [jnp.where(ids == BF16(b + 1), codes, BF16(0)) for b in range(first, first + held)]
        weights = dec_ref[:, first * BLOCK : (first + held) * BLOCK]
        return mm(weights, jnp.concatenate(spread, axis=0)).astype(BF16)

    extra_ref[FEATURES:, :] = jnp.zeros((384 - FEATURES, EXTRA_SLOTS), BF16)
    for tile in range(PAIRS // 2, LANE_TILES // 2):
        start = tile * 256 - MAIN_SLOTS
        extra_ref[0:FEATURES, start : start + 256] = contribution(tile)
    store_extra(send_ref, mm_nt(identity(EXTRA_SLOTS), extra_ref[...]))
    for double in range(2):
        values = [contribution(2 * quarter + double) for quarter in range(QUARTERS)]
        for side in range(2):
            lanes = slice(side * 128, (side + 1) * 128)
            tops = ungroup([value[:HALF, lanes] for value in values])
            bottoms = ungroup([value[HALF:, lanes] for value in values])
            for j in range(4):
                pair = 8 * double + 4 * side + j
                first, second = exchange(tops[j], bottoms[j], MAIN)
                send_ref[pair, 0:HALF, :] = first
                send_ref[pair + PAIRS, 0:HALF, :] = second


def combine_kernel(
    recv_ref, slots_ref, act_ref, bias_ref, out_ref, loss_ref, full_ref, place_ref, send_ref, sems
):
    slots = [slots_ref[k : k + 1, :].astype(jnp.int16) for k in range(NAMED)]
    ones = [jnp.ones((1, ROWS), BF16)] * NAMED
    for start in range(0, SLOTS, 256):
        place_ref[start : start + 256, :] = placed(slots, ones, start, 256)[0]
    unpack(recv_ref, full_ref)
    error = mm(full_ref[...], place_ref[...]) + bias_column(bias_ref) - act_ref[...].astype(F32)
    sent = error.astype(BF16)
    padded = jnp.concatenate([sent, jnp.zeros((96, ROWS), BF16)], axis=0)
    store_extra(send_ref, mm_nt(place_ref[MAIN_SLOTS:, :], padded))
    for double in range(PAIRS // 2):
        values = mm_nt(sent, place_ref[double * 256 : (double + 1) * 256, :])
        store_pair(send_ref, 2 * double, values[:, :128])
        store_pair(send_ref, 2 * double + 1, values[:, 128:])
        start_stage(send_ref, out_ref, sems, 2 * double + 2)
    loss = jnp.sum(error * error, axis=0, keepdims=True)
    for part in range(ROWS // 128):
        loss_ref[part : part + 1, :] = loss[:, part * 128 : (part + 1) * 128]
    wait_stages(send_ref, out_ref, sems)


def gradient_kernel(
    recv_ref, codes_ref, ids_ref, loss_ref, out_ref, out_loss_ref, full_ref, code_ref, grad_ref, sems
):
    out_loss_ref[...] = loss_ref[...]
    unpack_grouped(recv_ref, full_ref)
    load_codes(codes_ref, code_ref)
    ids = jnp.concatenate([ids_ref[tile : tile + 1, :] for tile in range(LANE_TILES)], axis=1)
    ids = jnp.broadcast_to(ids, (BLOCK, SLOTS)).astype(BF16)
    copies, begin = [], 0
    for start in range(0, LOCAL * BLOCK, 256):
        stop = start + 256
        width = MAIN_SLOTS // QUARTERS
        lanes = slice(start // 512 * width, (start // 512 + 1) * width)

        def both(values):
            return jnp.concatenate([values[:, lanes], values[:, MAIN_SLOTS:]], axis=1)

        near, codes = both(ids), both(code_ref)
        spread = [jnp.where(near == BF16(b + 1), codes, BF16(0)) for b in range(start // BLOCK, stop // BLOCK)]
        grad_ref[:, start:stop] = mm_nt(both(full_ref), jnp.concatenate(spread, axis=0)).astype(BF16)
        if stop in (LOCAL * BLOCK * 3 // 4, LOCAL * BLOCK):
            lanes = pl.ds(begin, stop - begin)
            copy = pltpu.make_async_copy(grad_ref.at[:, lanes], out_ref.at[:, lanes], sems.at[len(copies)])
            copy.start()
            copies.append(copy)
            begin = stop
    for copy in copies:
        copy.wait()


def call(kernel, out_shape, scratch, flops, name, megabytes, **specs):
    return pl.pallas_call(
        kernel,
        out_shape=out_shape,
        scratch_shapes=scratch,
        name=name,
        **specs,
        compiler_params=pltpu.CompilerParams(vmem_limit_bytes=megabytes * 1024 * 1024),
        cost_estimate=pl.CostEstimate(flops=flops, bytes_accessed=6_000_000, transcendentals=0),
    )


def shape(dims, dtype=BF16):
    return jax.ShapeDtypeStruct(dims, dtype)


def in_hbm(dims, dtype=BF16):
    return pltpu.HBM(dims, dtype)


def route(buffer):
    return lax.all_to_all(buffer, PLANE, split_axis=0, concat_axis=0, tiled=True)


def sum_codes(partial):
    shares = partial.reshape(4, SHARDS // 4 * CHUNK_ROWS, 128)
    received = lax.all_to_all(shares, INNER, split_axis=0, concat_axis=0, tiled=True)
    total = lax.psum(jnp.sum(received.astype(F32), axis=0), OUTER)
    codes = jnp.maximum(total, 0.0).astype(BF16)
    copies = jnp.broadcast_to(codes[None], shares.shape)
    return lax.all_to_all(copies, INNER, split_axis=0, concat_axis=0, tiled=True).reshape(partial.shape)


def sum_loss(part):
    return lax.psum(lax.psum(part, INNER), OUTER)


def padded_plan(activations, bias_dec, encoder, decoder, active_blocks):
    row_count, shard_width = activations.shape
    per_row = active_blocks.shape[1]
    groups = lax.axis_size(PLANE)
    local_blocks = encoder.shape[1] // BLOCK
    total_blocks = local_blocks * groups
    capacity = max(2, 2 * row_count * per_row // total_blocks)
    slot_count = total_blocks * capacity
    pair_blocks = active_blocks.reshape(-1)
    pair_iota = jnp.arange(pair_blocks.shape[0], dtype=jnp.int32)
    same_block = pair_blocks[:, None] == pair_blocks[None, :]
    earlier = pair_iota[None, :] < pair_iota[:, None]
    block_rank = jnp.sum((same_block & earlier).astype(jnp.int32), axis=1)
    slot_index = (pair_blocks * capacity + block_rank).reshape(row_count, per_row)
    slot_iota = jnp.arange(slot_count, dtype=jnp.int32)
    placement = jnp.zeros((slot_count, row_count), BF16)
    for which in range(per_row):
        placement = placement + (slot_index[:, which][None, :] == slot_iota[:, None]).astype(BF16)
    slot_shape = (groups, local_blocks, capacity, shard_width)

    def scatter_rows(values):
        filled = jnp.dot(placement, values, preferred_element_type=F32).astype(values.dtype)
        return filled.reshape(slot_shape)

    bias_wide = bias_dec.astype(F32)[None, :]
    shifted = (activations.astype(F32) - bias_wide).astype(BF16)
    received = route(scatter_rows(shifted))
    enc_local = encoder.reshape(shard_width, local_blocks, BLOCK)
    partial_pre = jnp.einsum("sbkd,dbl->sbkl", received, enc_local, preferred_element_type=F32)
    pre_total = lax.psum(partial_pre, DP)
    latent_codes = jnp.maximum(pre_total, 0.0).astype(BF16)
    dec_local = decoder.reshape(local_blocks, BLOCK, shard_width)
    contrib = jnp.einsum("sbkl,bld->sbkd", latent_codes, dec_local, preferred_element_type=F32).astype(BF16)
    returned = route(contrib).reshape(slot_count, shard_width)
    summed_rows = jnp.einsum("sr,sd->rd", placement, returned, preferred_element_type=F32)
    error = summed_rows + bias_wide - activations.astype(F32)
    row_loss = lax.psum(jnp.sum(error * error, axis=1), DP)
    error_sent = route(scatter_rows(error.astype(BF16)))
    gradient = jnp.einsum("sbkl,sbkd->bld", latent_codes, error_sent, preferred_element_type=F32)
    return gradient.reshape(local_blocks * BLOCK, shard_width).astype(BF16), row_loss


def on_device(activations, bias_dec, encoder, decoder, active_blocks):
    act = activations.T
    bias = bias_dec
    packed = in_hbm((GROUPS, PACKED, 128))
    full = pltpu.VMEM((FEATURES, SLOTS), BF16)
    sending = [pltpu.VMEM((GROUPS, PACKED, 128), BF16), pltpu.SemaphoreType.DMA((4,))]
    vmem, hbm = pl.BlockSpec(memory_space=pltpu.VMEM), pl.BlockSpec(memory_space=pltpu.HBM)
    spread_flops = 2 * FEATURES * SLOTS * LOCAL * BLOCK
    sent, slots = call(
        prepare_kernel,
        (packed, shape((8, ROWS), jnp.int32)),
        sending,
        2 * FEATURES * SLOTS * ROWS,
        "prepare",
        20,
        out_specs=(hbm, vmem),
    )(act, bias, active_blocks.T)
    received = route(sent)
    turned = encoder.T
    rest = turned[:, 256:].reshape(4, 8, BLOCK, 32).transpose(0, 2, 1, 3).reshape(4 * BLOCK, 256)
    partial, ids, over = call(
        encode_kernel,
        (shape((SHARDS, CHUNK_ROWS, 128)), shape((24, 128), F32), shape((1, 1), jnp.int32)),
        [full],
        spread_flops,
        "encode",
        20,
        out_specs=(vmem, vmem, pl.BlockSpec(memory_space=pltpu.SMEM)),
    )(received, turned[:, :256], rest)
    codes = sum_codes(partial)
    sent = call(
        decode_kernel,
        shape((GROUPS, PACKED, 128)),
        [
            pltpu.VMEM((BLOCK, SLOTS), BF16),
            pltpu.VMEM((384, EXTRA_SLOTS), BF16),
        ],
        spread_flops,
        "decode",
        20,
    )(codes, ids, decoder.T)
    received = route(sent)
    sent, loss = call(
        combine_kernel,
        (packed, shape((ROWS // 128, 128), F32)),
        [full, pltpu.VMEM((SLOTS, ROWS), BF16)] + sending,
        4 * FEATURES * SLOTS * ROWS,
        "combine",
        20,
        out_specs=(hbm, vmem),
    )(received, slots, act, bias)
    received = route(sent)
    loss = sum_loss(loss)

    def packed_plan():
        gradient, row_loss = call(
            gradient_kernel,
            (in_hbm((FEATURES, LOCAL * BLOCK)), in_hbm((ROWS // 128, 128), F32)),
            [
                full,
                pltpu.VMEM((BLOCK, SLOTS), BF16),
                pltpu.VMEM((FEATURES, LOCAL * BLOCK), BF16),
                pltpu.SemaphoreType.DMA((2,)),
            ],
            spread_flops,
            "gradient",
            24,
            out_specs=(hbm, vmem),
        )(received, codes, ids, loss)
        return gradient.T, row_loss.reshape(ROWS)

    return lax.cond(
        over[0, 0] > 0,
        lambda: padded_plan(activations, bias_dec, encoder, decoder, active_blocks),
        packed_plan,
    )


def solution(mesh):
    split = jax.sharding.Mesh(mesh.devices.reshape(4, 4, 8, 4), (OUTER, INNER) + PLANE)
    placed = (
        P(PLANE, DP),
        P(DP),
        P(DP, PLANE),
        P(PLANE, DP),
        P(PLANE, None),
    )
    return jax.shard_map(
        on_device,
        mesh=split,
        in_specs=placed,
        out_specs=(P(PLANE, DP), P(PLANE)),
        check_vma=False,
    )
```

```python
import jax
import jax.numpy as jnp
from jax import lax
from jax.experimental import pallas as pl
from jax.experimental.pallas import tpu as pltpu
from jax.sharding import PartitionSpec as P

BLOCK = 64
PLANE = ("latent", "section")
OUTER, INNER = "dp_outer", "dp_inner"
DP = (OUTER, INNER)
GROUPS = 32
SHARDS = 16
LOCAL = 32
ROWS = 512
FEATURES = 288
HALF = FEATURES // 2
NAMED = 4
QUARTERS = 4
SHARE = 16
MAIN = QUARTERS * SHARE
EXTRA = 16
MAIN_SLOTS = GROUPS * MAIN
EXTRA_SLOTS = GROUPS * EXTRA
SLOTS = MAIN_SLOTS + EXTRA_SLOTS
PACKED = HALF + 3 * EXTRA
PAIRS = GROUPS // 2
EARLY = 12
LANE_TILES = SLOTS // 128
CHUNK_TILES = 5
CHUNK_ROWS = 16 * CHUNK_TILES

NT = (((1,), (1,)), ((), ()))
F32 = jnp.float32
BF16 = jnp.bfloat16


def mm(a, b):
    return jnp.dot(a, b, preferred_element_type=F32)


def mm_nt(a, b):
    return lax.dot_general(a, b, NT, preferred_element_type=F32)


def identity(n):
    rows = lax.broadcasted_iota(jnp.int32, (n, n), 0)
    return jnp.where(rows == lax.broadcasted_iota(jnp.int32, (n, n), 1), 1.0, 0.0).astype(BF16)


def lane_offset(tile, width=128):
    return pl.ds(pl.multiple_of(tile * width, width), width)


def exchange(a, b, width):
    kind = jnp.int16 if a.dtype == BF16 else jnp.int32
    lane = lax.broadcasted_iota(kind, a.shape, 1)
    even = jnp.bitwise_and(lane, jnp.full((), 2 * width - 1, kind)) < jnp.full((), width, kind)
    return jnp.where(even, a, pltpu.roll(b, width, 1)), jnp.where(even, pltpu.roll(a, 128 - width, 1), b)


def regroup(tiles):
    a0, a1 = exchange(tiles[0], tiles[1], 32)
    b0, b1 = exchange(tiles[2], tiles[3], 32)
    return *exchange(a0, b0, 16), *exchange(a1, b1, 16)


def ungroup(tiles):
    a0, b0 = exchange(tiles[0], tiles[1], 16)
    a1, b1 = exchange(tiles[2], tiles[3], 16)
    return *exchange(a0, a1, 32), *exchange(b0, b1, 32)


def store_pair(out_ref, pair, values):
    values = values.astype(BF16)
    first, second = exchange(values[:HALF], values[HALF:], MAIN)
    out_ref[pair, 0:HALF, :] = first
    out_ref[pair + PAIRS, 0:HALF, :] = second


def stage_copies(buffer_ref, out_ref, sems, stage, early):
    first, count = (0, early) if stage == 0 else (early, PAIRS - early)
    copies = []
    for side in range(2):
        devices = pl.ds(side * PAIRS + first, count)
        copies.append(
            pltpu.make_async_copy(buffer_ref.at[devices], out_ref.at[devices], sems.at[2 * stage + side])
        )
    return copies


def start_stage(buffer_ref, out_ref, sems, done, early=EARLY):
    if done in (early, PAIRS):
        for copy in stage_copies(buffer_ref, out_ref, sems, 0 if done == early else 1, early):
            copy.start()


def wait_stages(buffer_ref, out_ref, sems, early=EARLY):
    for stage in range(2):
        for copy in stage_copies(buffer_ref, out_ref, sems, stage, early):
            copy.wait()


def bias_column(bias_ref):
    rows = lax.broadcasted_iota(jnp.int32, (FEATURES, FEATURES), 0)
    lanes = lax.broadcasted_iota(jnp.int32, (FEATURES, FEATURES), 1)
    wide = jnp.broadcast_to(bias_ref[...].astype(F32).reshape(1, FEATURES), (FEATURES, FEATURES))
    return jnp.sum(jnp.where(rows == lanes, wide, 0.0), axis=1, keepdims=True)


def store_extra(out_ref, values):
    for part in range(3):
        piece = values[:, part * 128 : (part + 1) * 128].astype(BF16)
        out_ref[:, HALF + part * EXTRA : HALF + (part + 1) * EXTRA, :] = piece.reshape(GROUPS, EXTRA, 128)


def load_pair(in_ref, pair):
    return exchange(in_ref[pair, 0:HALF, :], in_ref[pair + PAIRS, 0:HALF, :], MAIN)


def unpack(in_ref, full_ref):
    for pair in range(PAIRS):
        top, bottom = load_pair(in_ref, pair)
        full_ref[0:HALF, pair * 128 : (pair + 1) * 128] = top
        full_ref[HALF:, pair * 128 : (pair + 1) * 128] = bottom
    unpack_extra(in_ref, full_ref)


def unpack_grouped(in_ref, full_ref):
    for quad in range(4):
        pairs = [load_pair(in_ref, 4 * quad + j) for j in range(4)]
        for half in range(2):
            tiles = regroup([pair[half] for pair in pairs])
            for quarter in range(QUARTERS):
                tile = 4 * quarter + quad
                full_ref[half * HALF : (half + 1) * HALF, tile * 128 : (tile + 1) * 128] = tiles[quarter]
    return unpack_extra(in_ref, full_ref)


def unpack_extra(in_ref, full_ref):
    eye = identity(128)
    turned, last = None, None
    for part in range(3):
        last = in_ref[:, HALF + part * EXTRA : HALF + (part + 1) * EXTRA, :].reshape(EXTRA_SLOTS, 128)
        turned = mm_nt(eye, last)
        height = min(128, FEATURES - part * 128)
        full_ref[part * 128 : part * 128 + height, MAIN_SLOTS:] = turned[:height].astype(BF16)
    return last, turned


def placed(slots, names, start, count):
    index = lax.broadcasted_iota(jnp.int16, (count, ROWS), 0) + jnp.int16(start)
    named = jnp.zeros((count, ROWS), BF16)
    for k in range(NAMED):
        named = jnp.where(index == jnp.broadcast_to(slots[k], index.shape), names[k], named)
    return named, jnp.minimum(named, BF16(1))


def prepare_kernel(act_ref, bias_ref, blocks_ref, out_ref, slots_ref, send_ref, sems):
    blocks = blocks_ref[...]
    group = lax.shift_right_logical(blocks, 3)
    local = jnp.bitwise_and(blocks, LOCAL - 1)
    count = GROUPS * QUARTERS
    groups = lax.broadcasted_iota(jnp.int32, (count, ROWS), 0)
    hits = [groups == group[k : k + 1, :] for k in range(NAMED)]
    counts = sum(jnp.where(hit, 1.0, 0.0) for hit in hits).astype(BF16)
    before = lax.broadcasted_iota(jnp.int32, (ROWS, ROWS), 0) < lax.broadcasted_iota(jnp.int32, (ROWS, ROWS), 1)
    earlier = mm(counts, jnp.where(before, 1.0, 0.0).astype(BF16))
    beyond = jnp.maximum(mm(counts, jnp.ones((ROWS, 128), BF16)) - SHARE, 0.0).astype(BF16)
    one = lax.broadcasted_iota(jnp.int32, (count, count), 0)
    other = lax.broadcasted_iota(jnp.int32, (count, count), 1)
    same = lax.shift_right_logical(one, 2) == lax.shift_right_logical(other, 2)
    offset = mm(jnp.where(same & (other < one), 1.0, 0.0).astype(BF16), beyond)
    table = earlier + 1024.0 * jnp.concatenate([offset] * (ROWS // 128), axis=1)
    slots, names, most = [], [], jnp.zeros((1, ROWS), jnp.int32)
    for k in range(NAMED):
        mine = group[k : k + 1, :]
        found = jnp.sum(jnp.where(hits[k], table, 0.0), axis=0, keepdims=True).astype(jnp.int32)
        rank = jnp.bitwise_and(found, 1023)
        for previous in range(k):
            rank = rank + jnp.where(group[previous : previous + 1, :] == mine, 1, 0)
        target = lax.shift_right_logical(mine, 2)
        place = (jnp.bitwise_and(target, PAIRS - 1) * 2 + lax.shift_right_logical(target, 4)) * MAIN
        main = place + jnp.bitwise_and(mine, QUARTERS - 1) * SHARE + rank
        extra = lax.shift_right_logical(found, 10) + rank - SHARE
        late = jnp.where(extra < EXTRA, MAIN_SLOTS + target * EXTRA + extra, -1)
        slots.append(jnp.where(rank < SHARE, main, late))
        names.append((local[k : k + 1, :] + 1).astype(F32).astype(BF16))
        most = jnp.maximum(most, jnp.where(rank < SHARE, 0, extra))
    over = jnp.where(jnp.max(most, axis=1, keepdims=True) >= EXTRA, 1.0, 0.0)
    shifted = (act_ref[...].astype(F32) - bias_column(bias_ref)).astype(BF16)

    for k in range(NAMED):
        slots_ref[k : k + 1, :] = slots[k]
    slots_ref[NAMED:, :] = jnp.zeros((8 - NAMED, ROWS), jnp.int32)
    slots = [slot.astype(jnp.int16) for slot in slots]
    named, place = placed(slots, names, MAIN_SLOTS, EXTRA_SLOTS)
    padded = jnp.concatenate([shifted, jnp.zeros((96, ROWS), BF16)], axis=0)
    values = mm_nt(place, padded)
    store_extra(send_ref, values)
    lane = lax.broadcasted_iota(jnp.int32, (EXTRA_SLOTS, 128), 1)
    ids = mm(named, jnp.ones((ROWS, 128), BF16))
    last = jnp.where(lane == 32, ids, values[:, 256:])
    row = lax.broadcasted_iota(jnp.int32, (EXTRA, 128), 0)
    high = lax.broadcasted_iota(jnp.int32, (EXTRA, 128), 1) >= MAIN
    flag = jnp.broadcast_to(over, (EXTRA, 128))
    for double in range(PAIRS // 2):
        named, place = placed(slots, names, double * 256, 256)
        values = mm_nt(shifted, place)
        ids = mm_nt(jnp.ones((EXTRA, ROWS), BF16), named)
        for side in range(2):
            pair = 2 * double + side
            store_pair(send_ref, pair, values[:, side * 128 : (side + 1) * 128])
            for half in range(2):
                device = pair + half * PAIRS
                mine = ids[:, side * 128 : (side + 1) * 128]
                mine = mine if half else pltpu.roll(mine, MAIN, 1)
                tile = last[device * EXTRA : (device + 1) * EXTRA]
                tile = jnp.where(high & (row == 0), mine, tile)
                tile = jnp.where(high & (row == 1), flag, tile)
                send_ref[device, HALF + 2 * EXTRA :, :] = tile.astype(BF16)
        start_stage(send_ref, out_ref, sems, 2 * double + 2)
    wait_stages(send_ref, out_ref, sems)


def encode_kernel(recv_ref, enc_ref, rest_ref, out_ref, ids_ref, over_ref, full_ref):
    last, turned = unpack_grouped(recv_ref, full_ref)
    pick = lax.broadcasted_iota(jnp.int32, (2 * GROUPS, EXTRA_SLOTS), 0)
    column = lax.broadcasted_iota(jnp.int32, (2 * GROUPS, EXTRA_SLOTS), 1)
    wanted = jnp.where(pick < GROUPS, pick * EXTRA, (pick - GROUPS) * EXTRA + 1)
    rows = mm(jnp.where(column == wanted, 1.0, 0.0).astype(BF16), last)
    first, second = rows[:PAIRS], rows[PAIRS:GROUPS]
    low = lax.broadcasted_iota(jnp.int32, (PAIRS, 128), 1) < MAIN
    named = jnp.where(low, pltpu.roll(first, MAIN, 1), second)
    picked = [[named[4 * quad + j : 4 * quad + j + 1] for quad in range(4)] for j in range(4)]
    tiles = regroup([jnp.concatenate(some, axis=0) for some in picked])
    for quarter in range(QUARTERS):
        ids_ref[4 * quarter : 4 * quarter + 4, :] = tiles[quarter]
    for part in range(EXTRA_SLOTS // 128):
        ids_ref[PAIRS + part : PAIRS + part + 1, :] = turned[32:33, part * 128 : (part + 1) * 128]
    ids_ref[LANE_TILES:, :] = jnp.zeros((24 - LANE_TILES, 128), F32)
    flags = jnp.where(lax.broadcasted_iota(jnp.int32, (GROUPS, 128), 1) == MAIN, rows[GROUPS:], 0.0)
    flag = jnp.max(jnp.max(flags, axis=1, keepdims=True), axis=0, keepdims=True)
    over_ref[0, 0] = jnp.max(flag).astype(jnp.int32)

    for tile in range(LANE_TILES // 2):
        lanes = slice(tile * 256, (tile + 1) * 256)
        ids = jnp.concatenate([ids_ref[2 * tile : 2 * tile + 1, :], ids_ref[2 * tile + 1 : 2 * tile + 2, :]], axis=1)
        code = ids.astype(jnp.int32) - 1
        main = tile < PAIRS // 2
        quarter = tile // 2 if main else 0
        first, held = (8 * quarter, 8) if main else (0, LOCAL)
        part = mm(enc_ref[first * BLOCK : (first + held) * BLOCK, 0:256], full_ref[0:256, lanes])
        total = jnp.zeros((BLOCK, 256), F32)
        for b in range(held):
            total = jnp.where(code == first + b, part[b * BLOCK : (b + 1) * BLOCK], total)
        rest = full_ref[256:, lanes]
        member = jnp.broadcast_to(jnp.bitwise_and(code, 7), (32, 256))
        spread = jnp.concatenate([jnp.where(member == m, rest, BF16(0)) for m in range(8)], axis=0)
        if main:
            more = mm(rest_ref[quarter * BLOCK : (quarter + 1) * BLOCK, :], spread)
        else:
            part = mm(rest_ref[...], spread)
            more = jnp.zeros((BLOCK, 256), F32)
            for g in range(QUARTERS):
                wanted = lax.shift_right_arithmetic(code, 3) == g
                more = jnp.where(wanted, part[g * BLOCK : (g + 1) * BLOCK], more)
        total = total + more
        for half in range(2):
            lane_tile = 2 * tile + half
            slot_row = (lane_tile % CHUNK_TILES) * 16
            for quarter in range(4):
                piece = total[quarter * 16 : (quarter + 1) * 16, half * 128 : (half + 1) * 128]
                out_ref[quarter + 4 * (lane_tile // CHUNK_TILES), slot_row : slot_row + 16, :] = piece.astype(BF16)


def load_codes(codes_ref, full_ref):
    for tile in range(LANE_TILES):
        for quarter in range(4):
            full_ref[quarter * 16 : (quarter + 1) * 16, tile * 128 : (tile + 1) * 128] = codes_ref[
                quarter + 4 * (tile // CHUNK_TILES),
                (tile % CHUNK_TILES) * 16 : (tile % CHUNK_TILES + 1) * 16,
                :,
            ]


def decode_kernel(codes_ref, ids_ref, dec_ref, send_ref, full_ref, extra_ref):
    load_codes(codes_ref, full_ref)

    def contribution(tile):
        codes = full_ref[:, tile * 256 : (tile + 1) * 256]
        ids = jnp.concatenate([ids_ref[2 * tile : 2 * tile + 1, :], ids_ref[2 * tile + 1 : 2 * tile + 2, :]], axis=1)
        ids = jnp.broadcast_to(ids, (BLOCK, 256)).astype(BF16)
        main = tile < PAIRS // 2
        first, held = (8 * (tile // 2), 8) if main else (0, LOCAL)
        spread = [jnp.where(ids == BF16(b + 1), codes, BF16(0)) for b in range(first, first + held)]
        weights = dec_ref[:, first * BLOCK : (first + held) * BLOCK]
        return mm(weights, jnp.concatenate(spread, axis=0)).astype(BF16)

    extra_ref[FEATURES:, :] = jnp.zeros((384 - FEATURES, EXTRA_SLOTS), BF16)
    for tile in range(PAIRS // 2, LANE_TILES // 2):
        start = tile * 256 - MAIN_SLOTS
        extra_ref[0:FEATURES, start : start + 256] = contribution(tile)
    store_extra(send_ref, mm_nt(identity(EXTRA_SLOTS), extra_ref[...]))
    for double in range(2):
        values = [contribution(2 * quarter + double) for quarter in range(QUARTERS)]
        for side in range(2):
            lanes = slice(side * 128, (side + 1) * 128)
            tops = ungroup([value[:HALF, lanes] for value in values])
            bottoms = ungroup([value[HALF:, lanes] for value in values])
            for j in range(4):
                pair = 8 * double + 4 * side + j
                first, second = exchange(tops[j], bottoms[j], MAIN)
                send_ref[pair, 0:HALF, :] = first
                send_ref[pair + PAIRS, 0:HALF, :] = second


def combine_kernel(
    recv_ref, slots_ref, act_ref, bias_ref, out_ref, loss_ref, full_ref, place_ref, send_ref, sems
):
    slots = [slots_ref[k : k + 1, :].astype(jnp.int16) for k in range(NAMED)]
    ones = [jnp.ones((1, ROWS), BF16)] * NAMED
    for start in range(0, SLOTS, 256):
        place_ref[start : start + 256, :] = placed(slots, ones, start, 256)[0]
    unpack(recv_ref, full_ref)
    error = mm(full_ref[...], place_ref[...]) + bias_column(bias_ref) - act_ref[...].astype(F32)
    sent = error.astype(BF16)
    padded = jnp.concatenate([sent, jnp.zeros((96, ROWS), BF16)], axis=0)
    store_extra(send_ref, mm_nt(place_ref[MAIN_SLOTS:, :], padded))
    for double in range(PAIRS // 2):
        values = mm_nt(sent, place_ref[double * 256 : (double + 1) * 256, :])
        store_pair(send_ref, 2 * double, values[:, :128])
        store_pair(send_ref, 2 * double + 1, values[:, 128:])
        start_stage(send_ref, out_ref, sems, 2 * double + 2)
    loss = jnp.sum(error * error, axis=0, keepdims=True)
    for part in range(ROWS // 128):
        loss_ref[part : part + 1, :] = loss[:, part * 128 : (part + 1) * 128]
    wait_stages(send_ref, out_ref, sems)


def gradient_kernel(
    recv_ref, codes_ref, ids_ref, loss_ref, out_ref, out_loss_ref, full_ref, code_ref, grad_ref, sems
):
    out_loss_ref[...] = loss_ref[...]
    unpack_grouped(recv_ref, full_ref)
    load_codes(codes_ref, code_ref)
    ids = jnp.concatenate([ids_ref[tile : tile + 1, :] for tile in range(LANE_TILES)], axis=1)
    ids = jnp.broadcast_to(ids, (BLOCK, SLOTS)).astype(BF16)
    copies, begin = [], 0
    for start in range(0, LOCAL * BLOCK, 256):
        stop = start + 256
        width = MAIN_SLOTS // QUARTERS
        lanes = slice(start // 512 * width, (start // 512 + 1) * width)

        def both(values):
            return jnp.concatenate([values[:, lanes], values[:, MAIN_SLOTS:]], axis=1)

        near, codes = both(ids), both(code_ref)
        spread = [jnp.where(near == BF16(b + 1), codes, BF16(0)) for b in range(start // BLOCK, stop // BLOCK)]
        grad_ref[:, start:stop] = mm_nt(both(full_ref), jnp.concatenate(spread, axis=0)).astype(BF16)
        if stop in (LOCAL * BLOCK * 3 // 4, LOCAL * BLOCK):
            lanes = pl.ds(begin, stop - begin)
            copy = pltpu.make_async_copy(grad_ref.at[:, lanes], out_ref.at[:, lanes], sems.at[len(copies)])
            copy.start()
            copies.append(copy)
            begin = stop
    for copy in copies:
        copy.wait()


def call(kernel, out_shape, scratch, flops, name, megabytes, **specs):
    return pl.pallas_call(
        kernel,
        out_shape=out_shape,
        scratch_shapes=scratch,
        name=name,
        **specs,
        compiler_params=pltpu.CompilerParams(vmem_limit_bytes=megabytes * 1024 * 1024),
        cost_estimate=pl.CostEstimate(flops=flops, bytes_accessed=6_000_000, transcendentals=0),
    )


def shape(dims, dtype=BF16):
    return jax.ShapeDtypeStruct(dims, dtype)


def in_hbm(dims, dtype=BF16):
    return pltpu.HBM(dims, dtype)


def route(buffer):
    return lax.all_to_all(buffer, PLANE, split_axis=0, concat_axis=0, tiled=True)


def sum_codes(partial):
    shares = partial.reshape(4, SHARDS // 4 * CHUNK_ROWS, 128)
    received = lax.all_to_all(shares, INNER, split_axis=0, concat_axis=0, tiled=True)
    total = lax.psum(jnp.sum(received.astype(F32), axis=0), OUTER)
    codes = jnp.maximum(total, 0.0).astype(BF16)
    copies = jnp.broadcast_to(codes[None], shares.shape)
    return lax.all_to_all(copies, INNER, split_axis=0, concat_axis=0, tiled=True).reshape(partial.shape)


def sum_loss(part):
    return lax.psum(lax.psum(part, INNER), OUTER)


def padded_plan(activations, bias_dec, encoder, decoder, active_blocks):
    row_count, shard_width = activations.shape
    per_row = active_blocks.shape[1]
    groups = lax.axis_size(PLANE)
    local_blocks = encoder.shape[1] // BLOCK
    total_blocks = local_blocks * groups
    capacity = max(2, 2 * row_count * per_row // total_blocks)
    slot_count = total_blocks * capacity
    pair_blocks = active_blocks.reshape(-1)
    pair_iota = jnp.arange(pair_blocks.shape[0], dtype=jnp.int32)
    same_block = pair_blocks[:, None] == pair_blocks[None, :]
    earlier = pair_iota[None, :] < pair_iota[:, None]
    block_rank = jnp.sum((same_block & earlier).astype(jnp.int32), axis=1)
    slot_index = (pair_blocks * capacity + block_rank).reshape(row_count, per_row)
    slot_iota = jnp.arange(slot_count, dtype=jnp.int32)
    placement = jnp.zeros((slot_count, row_count), BF16)
    for which in range(per_row):
        placement = placement + (slot_index[:, which][None, :] == slot_iota[:, None]).astype(BF16)
    slot_shape = (groups, local_blocks, capacity, shard_width)

    def scatter_rows(values):
        filled = jnp.dot(placement, values, preferred_element_type=F32).astype(values.dtype)
        return filled.reshape(slot_shape)

    bias_wide = bias_dec.astype(F32)[None, :]
    shifted = (activations.astype(F32) - bias_wide).astype(BF16)
    received = route(scatter_rows(shifted))
    enc_local = encoder.reshape(shard_width, local_blocks, BLOCK)
    partial_pre = jnp.einsum("sbkd,dbl->sbkl", received, enc_local, preferred_element_type=F32)
    pre_total = lax.psum(partial_pre, DP)
    latent_codes = jnp.maximum(pre_total, 0.0).astype(BF16)
    dec_local = decoder.reshape(local_blocks, BLOCK, shard_width)
    contrib = jnp.einsum("sbkl,bld->sbkd", latent_codes, dec_local, preferred_element_type=F32).astype(BF16)
    returned = route(contrib).reshape(slot_count, shard_width)
    summed_rows = jnp.einsum("sr,sd->rd", placement, returned, preferred_element_type=F32)
    error = summed_rows + bias_wide - activations.astype(F32)
    row_loss = lax.psum(jnp.sum(error * error, axis=1), DP)
    error_sent = route(scatter_rows(error.astype(BF16)))
    gradient = jnp.einsum("sbkl,sbkd->bld", latent_codes, error_sent, preferred_element_type=F32)
    return gradient.reshape(local_blocks * BLOCK, shard_width).astype(BF16), row_loss


def on_device(activations, bias_dec, encoder, decoder, active_blocks):
    act = activations.T
    bias = bias_dec
    packed = in_hbm((GROUPS, PACKED, 128))
    full = pltpu.VMEM((FEATURES, SLOTS), BF16)
    sending = [pltpu.VMEM((GROUPS, PACKED, 128), BF16), pltpu.SemaphoreType.DMA((4,))]
    vmem, hbm = pl.BlockSpec(memory_space=pltpu.VMEM), pl.BlockSpec(memory_space=pltpu.HBM)
    spread_flops = 2 * FEATURES * SLOTS * LOCAL * BLOCK
    sent, slots = call(
        prepare_kernel,
        (packed, shape((8, ROWS), jnp.int32)),
        sending,
        2 * FEATURES * SLOTS * ROWS,
        "prepare",
        20,
        out_specs=(hbm, vmem),
    )(act, bias, active_blocks.T)
    received = route(sent)
    turned = encoder.T
    rest = turned[:, 256:].reshape(4, 8, BLOCK, 32).transpose(0, 2, 1, 3).reshape(4 * BLOCK, 256)
    partial, ids, over = call(
        encode_kernel,
        (shape((SHARDS, CHUNK_ROWS, 128)), shape((24, 128), F32), shape((1, 1), jnp.int32)),
        [full],
        spread_flops,
        "encode",
        20,
        out_specs=(vmem, vmem, pl.BlockSpec(memory_space=pltpu.SMEM)),
    )(received, turned, rest)
    codes = sum_codes(partial)
    sent = call(
        decode_kernel,
        shape((GROUPS, PACKED, 128)),
        [
            pltpu.VMEM((BLOCK, SLOTS), BF16),
            pltpu.VMEM((384, EXTRA_SLOTS), BF16),
        ],
        spread_flops,
        "decode",
        20,
    )(codes, ids, pltpu.with_memory_space_constraint(decoder.T, pltpu.VMEM))
    received = route(sent)
    sent, loss = call(
        combine_kernel,
        (packed, shape((ROWS // 128, 128), F32)),
        [full, pltpu.VMEM((SLOTS, ROWS), BF16)] + sending,
        4 * FEATURES * SLOTS * ROWS,
        "combine",
        20,
        out_specs=(hbm, vmem),
    )(received, slots, act, bias)
    received = route(sent)
    loss = sum_loss(loss)

    def packed_plan():
        gradient, row_loss = call(
            gradient_kernel,
            (in_hbm((FEATURES, LOCAL * BLOCK)), in_hbm((ROWS // 128, 128), F32)),
            [
                full,
                pltpu.VMEM((BLOCK, SLOTS), BF16),
                pltpu.VMEM((FEATURES, LOCAL * BLOCK), BF16),
                pltpu.SemaphoreType.DMA((2,)),
            ],
            spread_flops,
            "gradient",
            24,
            out_specs=(hbm, vmem),
        )(pltpu.with_memory_space_constraint(received, pltpu.VMEM), codes, ids, loss)
        return gradient.T, row_loss.reshape(ROWS)

    return lax.cond(
        over[0, 0] > 0,
        lambda: padded_plan(activations, bias_dec, encoder, decoder, active_blocks),
        packed_plan,
    )


def solution(mesh):
    split = jax.sharding.Mesh(mesh.devices.reshape(4, 4, 8, 4), (OUTER, INNER) + PLANE)
    placed = (
        P(PLANE, DP),
        P(DP),
        P(DP, PLANE),
        P(PLANE, DP),
        P(PLANE, None),
    )
    return jax.shard_map(
        on_device,
        mesh=split,
        in_specs=placed,
        out_specs=(P(PLANE, DP), P(PLANE)),
        check_vma=False,
    )
```

```python
import jax
import jax.numpy as jnp
from jax import lax
from jax.experimental import pallas as pl
from jax.experimental.pallas import tpu as pltpu
from jax.sharding import PartitionSpec as P

BLOCK = 64
PLANE = ("latent", "section")
OUTER, INNER = "dp_outer", "dp_inner"
DP = (OUTER, INNER)
GROUPS = 32
SHARDS = 16
LOCAL = 32
ROWS = 512
FEATURES = 288
HALF = FEATURES // 2
NAMED = 4
QUARTERS = 4
SHARE = 16
MAIN = QUARTERS * SHARE
EXTRA = 16
MAIN_SLOTS = GROUPS * MAIN
EXTRA_SLOTS = GROUPS * EXTRA
SLOTS = MAIN_SLOTS + EXTRA_SLOTS
PACKED = HALF + 3 * EXTRA
PAIRS = GROUPS // 2
EARLY = 12
LANE_TILES = SLOTS // 128
CHUNK_TILES = 5
CHUNK_ROWS = 16 * CHUNK_TILES

NT = (((1,), (1,)), ((), ()))
F32 = jnp.float32
BF16 = jnp.bfloat16


def mm(a, b):
    return jnp.dot(a, b, preferred_element_type=F32)


def mm_nt(a, b):
    return lax.dot_general(a, b, NT, preferred_element_type=F32)


def identity(n):
    rows = lax.broadcasted_iota(jnp.int32, (n, n), 0)
    return jnp.where(rows == lax.broadcasted_iota(jnp.int32, (n, n), 1), 1.0, 0.0).astype(BF16)


def lane_offset(tile, width=128):
    return pl.ds(pl.multiple_of(tile * width, width), width)


def exchange(a, b, width):
    kind = jnp.int16 if a.dtype == BF16 else jnp.int32
    lane = lax.broadcasted_iota(kind, a.shape, 1)
    even = jnp.bitwise_and(lane, jnp.full((), 2 * width - 1, kind)) < jnp.full((), width, kind)
    return jnp.where(even, a, pltpu.roll(b, width, 1)), jnp.where(even, pltpu.roll(a, 128 - width, 1), b)


def regroup(tiles):
    a0, a1 = exchange(tiles[0], tiles[1], 32)
    b0, b1 = exchange(tiles[2], tiles[3], 32)
    return *exchange(a0, b0, 16), *exchange(a1, b1, 16)


def ungroup(tiles):
    a0, b0 = exchange(tiles[0], tiles[1], 16)
    a1, b1 = exchange(tiles[2], tiles[3], 16)
    return *exchange(a0, a1, 32), *exchange(b0, b1, 32)


def store_pair(out_ref, pair, values):
    values = values.astype(BF16)
    first, second = exchange(values[:HALF], values[HALF:], MAIN)
    out_ref[pair, 0:HALF, :] = first
    out_ref[pair + PAIRS, 0:HALF, :] = second


def stage_copies(buffer_ref, out_ref, sems, stage, early):
    first, count = (0, early) if stage == 0 else (early, PAIRS - early)
    copies = []
    for side in range(2):
        devices = pl.ds(side * PAIRS + first, count)
        copies.append(
            pltpu.make_async_copy(buffer_ref.at[devices], out_ref.at[devices], sems.at[2 * stage + side])
        )
    return copies


def start_stage(buffer_ref, out_ref, sems, done, early=EARLY):
    if done in (early, PAIRS):
        for copy in stage_copies(buffer_ref, out_ref, sems, 0 if done == early else 1, early):
            copy.start()


def wait_stages(buffer_ref, out_ref, sems, early=EARLY):
    for stage in range(2):
        for copy in stage_copies(buffer_ref, out_ref, sems, stage, early):
            copy.wait()


def bias_column(bias_ref):
    rows = lax.broadcasted_iota(jnp.int32, (FEATURES, FEATURES), 0)
    lanes = lax.broadcasted_iota(jnp.int32, (FEATURES, FEATURES), 1)
    wide = jnp.broadcast_to(bias_ref[...].astype(F32).reshape(1, FEATURES), (FEATURES, FEATURES))
    return jnp.sum(jnp.where(rows == lanes, wide, 0.0), axis=1, keepdims=True)


def store_extra(out_ref, values):
    for part in range(3):
        piece = values[:, part * 128 : (part + 1) * 128].astype(BF16)
        out_ref[:, HALF + part * EXTRA : HALF + (part + 1) * EXTRA, :] = piece.reshape(GROUPS, EXTRA, 128)


def load_pair(in_ref, pair):
    return exchange(in_ref[pair, 0:HALF, :], in_ref[pair + PAIRS, 0:HALF, :], MAIN)


def unpack(in_ref, full_ref):
    for pair in range(PAIRS):
        top, bottom = load_pair(in_ref, pair)
        full_ref[0:HALF, pair * 128 : (pair + 1) * 128] = top
        full_ref[HALF:, pair * 128 : (pair + 1) * 128] = bottom
    unpack_extra(in_ref, full_ref)


def unpack_grouped(in_ref, full_ref):
    for quad in range(4):
        pairs = [load_pair(in_ref, 4 * quad + j) for j in range(4)]
        for half in range(2):
            tiles = regroup([pair[half] for pair in pairs])
            for quarter in range(QUARTERS):
                tile = 4 * quarter + quad
                full_ref[half * HALF : (half + 1) * HALF, tile * 128 : (tile + 1) * 128] = tiles[quarter]
    return unpack_extra(in_ref, full_ref)


def unpack_extra(in_ref, full_ref):
    eye = identity(128)
    turned, last = None, None
    for part in range(3):
        last = in_ref[:, HALF + part * EXTRA : HALF + (part + 1) * EXTRA, :].reshape(EXTRA_SLOTS, 128)
        turned = mm_nt(eye, last)
        height = min(128, FEATURES - part * 128)
        full_ref[part * 128 : part * 128 + height, MAIN_SLOTS:] = turned[:height].astype(BF16)
    return last, turned


def placed(slots, names, start, count):
    index = lax.broadcasted_iota(jnp.int16, (count, ROWS), 0) + jnp.int16(start)
    named = jnp.zeros((count, ROWS), BF16)
    for k in range(NAMED):
        named = jnp.where(index == jnp.broadcast_to(slots[k], index.shape), names[k], named)
    return named, jnp.minimum(named, BF16(1))


def prepare_kernel(act_ref, bias_ref, blocks_ref, out_ref, slots_ref, send_ref, sems):
    blocks = blocks_ref[...]
    group = lax.shift_right_logical(blocks, 3)
    local = jnp.bitwise_and(blocks, LOCAL - 1)
    count = GROUPS * QUARTERS
    groups = lax.broadcasted_iota(jnp.int32, (count, ROWS), 0)
    hits = [groups == group[k : k + 1, :] for k in range(NAMED)]
    counts = sum(jnp.where(hit, 1.0, 0.0) for hit in hits).astype(BF16)
    before = lax.broadcasted_iota(jnp.int32, (ROWS, ROWS), 0) < lax.broadcasted_iota(jnp.int32, (ROWS, ROWS), 1)
    earlier = mm(counts, jnp.where(before, 1.0, 0.0).astype(BF16))
    beyond = jnp.maximum(mm(counts, jnp.ones((ROWS, 128), BF16)) - SHARE, 0.0).astype(BF16)
    one = lax.broadcasted_iota(jnp.int32, (count, count), 0)
    other = lax.broadcasted_iota(jnp.int32, (count, count), 1)
    same = lax.shift_right_logical(one, 2) == lax.shift_right_logical(other, 2)
    offset = mm(jnp.where(same & (other < one), 1.0, 0.0).astype(BF16), beyond)
    table = earlier + 1024.0 * jnp.concatenate([offset] * (ROWS // 128), axis=1)
    slots, names, most = [], [], jnp.zeros((1, ROWS), jnp.int32)
    for k in range(NAMED):
        mine = group[k : k + 1, :]
        found = jnp.sum(jnp.where(hits[k], table, 0.0), axis=0, keepdims=True).astype(jnp.int32)
        rank = jnp.bitwise_and(found, 1023)
        for previous in range(k):
            rank = rank + jnp.where(group[previous : previous + 1, :] == mine, 1, 0)
        target = lax.shift_right_logical(mine, 2)
        place = (jnp.bitwise_and(target, PAIRS - 1) * 2 + lax.shift_right_logical(target, 4)) * MAIN
        main = place + jnp.bitwise_and(mine, QUARTERS - 1) * SHARE + rank
        extra = lax.shift_right_logical(found, 10) + rank - SHARE
        late = jnp.where(extra < EXTRA, MAIN_SLOTS + target * EXTRA + extra, -1)
        slots.append(jnp.where(rank < SHARE, main, late))
        names.append((local[k : k + 1, :] + 1).astype(F32).astype(BF16))
        most = jnp.maximum(most, jnp.where(rank < SHARE, 0, extra))
    over = jnp.where(jnp.max(most, axis=1, keepdims=True) >= EXTRA, 1.0, 0.0)
    shifted = (act_ref[...].astype(F32) - bias_column(bias_ref)).astype(BF16)

    for k in range(NAMED):
        slots_ref[k : k + 1, :] = slots[k]
    slots_ref[NAMED:, :] = jnp.zeros((8 - NAMED, ROWS), jnp.int32)
    slots = [slot.astype(jnp.int16) for slot in slots]
    named, place = placed(slots, names, MAIN_SLOTS, EXTRA_SLOTS)
    padded = jnp.concatenate([shifted, jnp.zeros((96, ROWS), BF16)], axis=0)
    values = mm_nt(place, padded)
    store_extra(send_ref, values)
    lane = lax.broadcasted_iota(jnp.int32, (EXTRA_SLOTS, 128), 1)
    ids = mm(named, jnp.ones((ROWS, 128), BF16))
    last = jnp.where(lane == 32, ids, values[:, 256:])
    row = lax.broadcasted_iota(jnp.int32, (EXTRA, 128), 0)
    high = lax.broadcasted_iota(jnp.int32, (EXTRA, 128), 1) >= MAIN
    flag = jnp.broadcast_to(over, (EXTRA, 128))
    for double in range(PAIRS // 2):
        named, place = placed(slots, names, double * 256, 256)
        values = mm_nt(shifted, place)
        ids = mm_nt(jnp.ones((EXTRA, ROWS), BF16), named)
        for side in range(2):
            pair = 2 * double + side
            store_pair(send_ref, pair, values[:, side * 128 : (side + 1) * 128])
            for half in range(2):
                device = pair + half * PAIRS
                mine = ids[:, side * 128 : (side + 1) * 128]
                mine = mine if half else pltpu.roll(mine, MAIN, 1)
                tile = last[device * EXTRA : (device + 1) * EXTRA]
                tile = jnp.where(high & (row == 0), mine, tile)
                tile = jnp.where(high & (row == 1), flag, tile)
                send_ref[device, HALF + 2 * EXTRA :, :] = tile.astype(BF16)
        start_stage(send_ref, out_ref, sems, 2 * double + 2)
    wait_stages(send_ref, out_ref, sems)


def encode_kernel(recv_ref, enc_ref, rest_ref, out_ref, ids_ref, over_ref, full_ref):
    last, turned = unpack_grouped(recv_ref, full_ref)
    pick = lax.broadcasted_iota(jnp.int32, (2 * GROUPS, EXTRA_SLOTS), 0)
    column = lax.broadcasted_iota(jnp.int32, (2 * GROUPS, EXTRA_SLOTS), 1)
    wanted = jnp.where(pick < GROUPS, pick * EXTRA, (pick - GROUPS) * EXTRA + 1)
    rows = mm(jnp.where(column == wanted, 1.0, 0.0).astype(BF16), last)
    first, second = rows[:PAIRS], rows[PAIRS:GROUPS]
    low = lax.broadcasted_iota(jnp.int32, (PAIRS, 128), 1) < MAIN
    named = jnp.where(low, pltpu.roll(first, MAIN, 1), second)
    picked = [[named[4 * quad + j : 4 * quad + j + 1] for quad in range(4)] for j in range(4)]
    tiles = regroup([jnp.concatenate(some, axis=0) for some in picked])
    for quarter in range(QUARTERS):
        ids_ref[4 * quarter : 4 * quarter + 4, :] = tiles[quarter]
    for part in range(EXTRA_SLOTS // 128):
        ids_ref[PAIRS + part : PAIRS + part + 1, :] = turned[32:33, part * 128 : (part + 1) * 128]
    ids_ref[LANE_TILES:, :] = jnp.zeros((24 - LANE_TILES, 128), F32)
    flags = jnp.where(lax.broadcasted_iota(jnp.int32, (GROUPS, 128), 1) == MAIN, rows[GROUPS:], 0.0)
    flag = jnp.max(jnp.max(flags, axis=1, keepdims=True), axis=0, keepdims=True)
    over_ref[0, 0] = jnp.max(flag).astype(jnp.int32)

    for tile in range(LANE_TILES // 2):
        lanes = slice(tile * 256, (tile + 1) * 256)
        ids = jnp.concatenate([ids_ref[2 * tile : 2 * tile + 1, :], ids_ref[2 * tile + 1 : 2 * tile + 2, :]], axis=1)
        code = ids.astype(jnp.int32) - 1
        main = tile < PAIRS // 2
        quarter = tile // 2 if main else 0
        first, held = (8 * quarter, 8) if main else (0, LOCAL)
        part = mm(enc_ref[first * BLOCK : (first + held) * BLOCK, 0:256], full_ref[0:256, lanes])
        total = jnp.zeros((BLOCK, 256), F32)
        for b in range(held):
            total = jnp.where(code == first + b, part[b * BLOCK : (b + 1) * BLOCK], total)
        rest = full_ref[256:, lanes]
        member = jnp.broadcast_to(jnp.bitwise_and(code, 7), (32, 256))
        spread = jnp.concatenate([jnp.where(member == m, rest, BF16(0)) for m in range(8)], axis=0)
        if main:
            more = mm(rest_ref[quarter * BLOCK : (quarter + 1) * BLOCK, :], spread)
        else:
            part = mm(rest_ref[...], spread)
            more = jnp.zeros((BLOCK, 256), F32)
            for g in range(QUARTERS):
                wanted = lax.shift_right_arithmetic(code, 3) == g
                more = jnp.where(wanted, part[g * BLOCK : (g + 1) * BLOCK], more)
        total = total + more
        for half in range(2):
            lane_tile = 2 * tile + half
            slot_row = (lane_tile % CHUNK_TILES) * 16
            for quarter in range(4):
                piece = total[quarter * 16 : (quarter + 1) * 16, half * 128 : (half + 1) * 128]
                out_ref[quarter + 4 * (lane_tile // CHUNK_TILES), slot_row : slot_row + 16, :] = piece.astype(BF16)


def load_codes(codes_ref, full_ref):
    for tile in range(LANE_TILES):
        for quarter in range(4):
            full_ref[quarter * 16 : (quarter + 1) * 16, tile * 128 : (tile + 1) * 128] = codes_ref[
                quarter + 4 * (tile // CHUNK_TILES),
                (tile % CHUNK_TILES) * 16 : (tile % CHUNK_TILES + 1) * 16,
                :,
            ]


def decode_kernel(codes_ref, ids_ref, weights_ref, send_ref, full_ref, extra_ref, dec_ref, sems):
    fetches = []
    for quarter in range(QUARTERS):
        lanes = pl.ds(quarter * 8 * BLOCK, 8 * BLOCK)
        fetches.append(
            pltpu.make_async_copy(weights_ref.at[:, lanes], dec_ref.at[:, lanes], sems.at[quarter])
        )
        fetches[-1].start()
    load_codes(codes_ref, full_ref)

    def contribution(tile):
        codes = full_ref[:, tile * 256 : (tile + 1) * 256]
        ids = jnp.concatenate([ids_ref[2 * tile : 2 * tile + 1, :], ids_ref[2 * tile + 1 : 2 * tile + 2, :]], axis=1)
        ids = jnp.broadcast_to(ids, (BLOCK, 256)).astype(BF16)
        main = tile < PAIRS // 2
        first, held = (8 * (tile // 2), 8) if main else (0, LOCAL)
        spread = [jnp.where(ids == BF16(b + 1), codes, BF16(0)) for b in range(first, first + held)]
        weights = dec_ref[:, first * BLOCK : (first + held) * BLOCK]
        return mm(weights, jnp.concatenate(spread, axis=0)).astype(BF16)

    for double in range(2):
        values = []
        for quarter in range(QUARTERS):
            if double == 0:
                fetches[quarter].wait()
            values.append(contribution(2 * quarter + double))
        for side in range(2):
            lanes = slice(side * 128, (side + 1) * 128)
            tops = ungroup([value[:HALF, lanes] for value in values])
            bottoms = ungroup([value[HALF:, lanes] for value in values])
            for j in range(4):
                pair = 8 * double + 4 * side + j
                first, second = exchange(tops[j], bottoms[j], MAIN)
                send_ref[pair, 0:HALF, :] = first
                send_ref[pair + PAIRS, 0:HALF, :] = second
    extra_ref[FEATURES:, :] = jnp.zeros((384 - FEATURES, EXTRA_SLOTS), BF16)
    for tile in range(PAIRS // 2, LANE_TILES // 2):
        start = tile * 256 - MAIN_SLOTS
        extra_ref[0:FEATURES, start : start + 256] = contribution(tile)
    store_extra(send_ref, mm_nt(identity(EXTRA_SLOTS), extra_ref[...]))


def combine_kernel(
    recv_ref, slots_ref, act_ref, bias_ref, out_ref, loss_ref, full_ref, place_ref, send_ref, sems
):
    slots = [slots_ref[k : k + 1, :].astype(jnp.int16) for k in range(NAMED)]
    ones = [jnp.ones((1, ROWS), BF16)] * NAMED
    for start in range(0, SLOTS, 256):
        place_ref[start : start + 256, :] = placed(slots, ones, start, 256)[0]
    unpack(recv_ref, full_ref)
    error = mm(full_ref[...], place_ref[...]) + bias_column(bias_ref) - act_ref[...].astype(F32)
    sent = error.astype(BF16)
    padded = jnp.concatenate([sent, jnp.zeros((96, ROWS), BF16)], axis=0)
    store_extra(send_ref, mm_nt(place_ref[MAIN_SLOTS:, :], padded))
    for double in range(PAIRS // 2):
        values = mm_nt(sent, place_ref[double * 256 : (double + 1) * 256, :])
        store_pair(send_ref, 2 * double, values[:, :128])
        store_pair(send_ref, 2 * double + 1, values[:, 128:])
        start_stage(send_ref, out_ref, sems, 2 * double + 2)
    loss = jnp.sum(error * error, axis=0, keepdims=True)
    for part in range(ROWS // 128):
        loss_ref[part : part + 1, :] = loss[:, part * 128 : (part + 1) * 128]
    wait_stages(send_ref, out_ref, sems)


def gradient_kernel(
    recv_ref, codes_ref, ids_ref, loss_ref, out_ref, out_loss_ref, full_ref, code_ref, grad_ref, sems
):
    out_loss_ref[...] = loss_ref[...]
    unpack_grouped(recv_ref, full_ref)
    load_codes(codes_ref, code_ref)
    ids = jnp.concatenate([ids_ref[tile : tile + 1, :] for tile in range(LANE_TILES)], axis=1)
    ids = jnp.broadcast_to(ids, (BLOCK, SLOTS)).astype(BF16)
    copies, begin = [], 0
    for start in range(0, LOCAL * BLOCK, 256):
        stop = start + 256
        width = MAIN_SLOTS // QUARTERS
        lanes = slice(start // 512 * width, (start // 512 + 1) * width)

        def both(values):
            return jnp.concatenate([values[:, lanes], values[:, MAIN_SLOTS:]], axis=1)

        near, codes = both(ids), both(code_ref)
        spread = [jnp.where(near == BF16(b + 1), codes, BF16(0)) for b in range(start // BLOCK, stop // BLOCK)]
        grad_ref[:, start:stop] = mm_nt(both(full_ref), jnp.concatenate(spread, axis=0)).astype(BF16)
        if stop in (LOCAL * BLOCK * 3 // 4, LOCAL * BLOCK):
            lanes = pl.ds(begin, stop - begin)
            copy = pltpu.make_async_copy(grad_ref.at[:, lanes], out_ref.at[:, lanes], sems.at[len(copies)])
            copy.start()
            copies.append(copy)
            begin = stop
    for copy in copies:
        copy.wait()


def call(kernel, out_shape, scratch, flops, name, megabytes, **specs):
    return pl.pallas_call(
        kernel,
        out_shape=out_shape,
        scratch_shapes=scratch,
        name=name,
        **specs,
        compiler_params=pltpu.CompilerParams(vmem_limit_bytes=megabytes * 1024 * 1024),
        cost_estimate=pl.CostEstimate(flops=flops, bytes_accessed=6_000_000, transcendentals=0),
    )


def shape(dims, dtype=BF16):
    return jax.ShapeDtypeStruct(dims, dtype)


def in_hbm(dims, dtype=BF16):
    return pltpu.HBM(dims, dtype)


def route(buffer):
    return lax.all_to_all(buffer, PLANE, split_axis=0, concat_axis=0, tiled=True)


def sum_codes(partial):
    shares = partial.reshape(4, SHARDS // 4 * CHUNK_ROWS, 128)
    received = lax.all_to_all(shares, INNER, split_axis=0, concat_axis=0, tiled=True)
    total = lax.psum(jnp.sum(received.astype(F32), axis=0), OUTER)
    codes = jnp.maximum(total, 0.0).astype(BF16)
    copies = jnp.broadcast_to(codes[None], shares.shape)
    return lax.all_to_all(copies, INNER, split_axis=0, concat_axis=0, tiled=True).reshape(partial.shape)


def sum_loss(part):
    return lax.psum(lax.psum(part, OUTER), INNER)


def padded_plan(activations, bias_dec, encoder, decoder, active_blocks):
    row_count, shard_width = activations.shape
    per_row = active_blocks.shape[1]
    groups = lax.axis_size(PLANE)
    local_blocks = encoder.shape[1] // BLOCK
    total_blocks = local_blocks * groups
    capacity = max(2, 2 * row_count * per_row // total_blocks)
    slot_count = total_blocks * capacity
    pair_blocks = active_blocks.reshape(-1)
    pair_iota = jnp.arange(pair_blocks.shape[0], dtype=jnp.int32)
    same_block = pair_blocks[:, None] == pair_blocks[None, :]
    earlier = pair_iota[None, :] < pair_iota[:, None]
    block_rank = jnp.sum((same_block & earlier).astype(jnp.int32), axis=1)
    slot_index = (pair_blocks * capacity + block_rank).reshape(row_count, per_row)
    slot_iota = jnp.arange(slot_count, dtype=jnp.int32)
    placement = jnp.zeros((slot_count, row_count), BF16)
    for which in range(per_row):
        placement = placement + (slot_index[:, which][None, :] == slot_iota[:, None]).astype(BF16)
    slot_shape = (groups, local_blocks, capacity, shard_width)

    def scatter_rows(values):
        filled = jnp.dot(placement, values, preferred_element_type=F32).astype(values.dtype)
        return filled.reshape(slot_shape)

    bias_wide = bias_dec.astype(F32)[None, :]
    shifted = (activations.astype(F32) - bias_wide).astype(BF16)
    received = route(scatter_rows(shifted))
    enc_local = encoder.reshape(shard_width, local_blocks, BLOCK)
    partial_pre = jnp.einsum("sbkd,dbl->sbkl", received, enc_local, preferred_element_type=F32)
    pre_total = lax.psum(partial_pre, DP)
    latent_codes = jnp.maximum(pre_total, 0.0).astype(BF16)
    dec_local = decoder.reshape(local_blocks, BLOCK, shard_width)
    contrib = jnp.einsum("sbkl,bld->sbkd", latent_codes, dec_local, preferred_element_type=F32).astype(BF16)
    returned = route(contrib).reshape(slot_count, shard_width)
    summed_rows = jnp.einsum("sr,sd->rd", placement, returned, preferred_element_type=F32)
    error = summed_rows + bias_wide - activations.astype(F32)
    row_loss = lax.psum(jnp.sum(error * error, axis=1), DP)
    error_sent = route(scatter_rows(error.astype(BF16)))
    gradient = jnp.einsum("sbkl,sbkd->bld", latent_codes, error_sent, preferred_element_type=F32)
    return gradient.reshape(local_blocks * BLOCK, shard_width).astype(BF16), row_loss


def on_device(activations, bias_dec, encoder, decoder, active_blocks):
    act = activations.T
    bias = bias_dec
    packed = in_hbm((GROUPS, PACKED, 128))
    full = pltpu.VMEM((FEATURES, SLOTS), BF16)
    sending = [pltpu.VMEM((GROUPS, PACKED, 128), BF16), pltpu.SemaphoreType.DMA((4,))]
    vmem, hbm = pl.BlockSpec(memory_space=pltpu.VMEM), pl.BlockSpec(memory_space=pltpu.HBM)
    spread_flops = 2 * FEATURES * SLOTS * LOCAL * BLOCK
    sent, slots = call(
        prepare_kernel,
        (packed, shape((8, ROWS), jnp.int32)),
        sending,
        2 * FEATURES * SLOTS * ROWS,
        "prepare",
        20,
        out_specs=(hbm, vmem),
    )(act, bias, active_blocks.T)
    received = route(sent)
    turned = encoder.T
    rest = turned[:, 256:].reshape(4, 8, BLOCK, 32).transpose(0, 2, 1, 3).reshape(4 * BLOCK, 256)
    partial, ids, over = call(
        encode_kernel,
        (shape((SHARDS, CHUNK_ROWS, 128)), shape((24, 128), F32), shape((1, 1), jnp.int32)),
        [full],
        spread_flops,
        "encode",
        20,
        out_specs=(vmem, vmem, pl.BlockSpec(memory_space=pltpu.SMEM)),
    )(received, turned, rest)
    codes = sum_codes(partial)
    sent = call(
        decode_kernel,
        shape((GROUPS, PACKED, 128)),
        [
            pltpu.VMEM((BLOCK, SLOTS), BF16),
            pltpu.VMEM((384, EXTRA_SLOTS), BF16),
            pltpu.VMEM((FEATURES, LOCAL * BLOCK), BF16),
            pltpu.SemaphoreType.DMA((QUARTERS,)),
        ],
        spread_flops,
        "decode",
        20,
        in_specs=(vmem, vmem, hbm),
    )(codes, ids, decoder.T)
    received = route(sent)
    sent, loss = call(
        combine_kernel,
        (packed, shape((ROWS // 128, 128), F32)),
        [full, pltpu.VMEM((SLOTS, ROWS), BF16)] + sending,
        4 * FEATURES * SLOTS * ROWS,
        "combine",
        20,
        out_specs=(hbm, vmem),
    )(received, slots, act, bias)
    received = route(sent)
    loss = sum_loss(loss)

    def packed_plan():
        gradient, row_loss = call(
            gradient_kernel,
            (in_hbm((FEATURES, LOCAL * BLOCK)), in_hbm((ROWS // 128, 128), F32)),
            [
                full,
                pltpu.VMEM((BLOCK, SLOTS), BF16),
                pltpu.VMEM((FEATURES, LOCAL * BLOCK), BF16),
                pltpu.SemaphoreType.DMA((2,)),
            ],
            spread_flops,
            "gradient",
            24,
            out_specs=(hbm, vmem),
        )(pltpu.with_memory_space_constraint(received, pltpu.VMEM), codes, ids, loss)
        return gradient.T, row_loss.reshape(ROWS)

    return lax.cond(
        over[0, 0] > 0,
        lambda: padded_plan(activations, bias_dec, encoder, decoder, active_blocks),
        packed_plan,
    )


def solution(mesh):
    split = jax.sharding.Mesh(mesh.devices.reshape(4, 4, 8, 4), (OUTER, INNER) + PLANE)
    placed = (
        P(PLANE, DP),
        P(DP),
        P(DP, PLANE),
        P(PLANE, DP),
        P(PLANE, None),
    )
    return jax.shard_map(
        on_device,
        mesh=split,
        in_specs=placed,
        out_specs=(P(PLANE, DP), P(PLANE)),
        check_vma=False,
    )
```

```python
import jax
import jax.numpy as jnp
from jax import lax
from jax.experimental import pallas as pl
from jax.experimental.pallas import tpu as pltpu
from jax.sharding import PartitionSpec as P

BLOCK = 64
PLANE = ("latent", "section")
OUTER, INNER = "dp_outer", "dp_inner"
DP = (OUTER, INNER)
GROUPS = 32
SHARDS = 16
LOCAL = 32
ROWS = 512
FEATURES = 288
HALF = FEATURES // 2
NAMED = 4
QUARTERS = 4
SHARE = 16
MAIN = QUARTERS * SHARE
EXTRA = 16
MAIN_SLOTS = GROUPS * MAIN
EXTRA_SLOTS = GROUPS * EXTRA
SLOTS = MAIN_SLOTS + EXTRA_SLOTS
PACKED = HALF + 3 * EXTRA
PAIRS = GROUPS // 2
STAGE = 4
LANE_TILES = SLOTS // 128
CHUNK_TILES = 5
CHUNK_ROWS = 16 * CHUNK_TILES

NT = (((1,), (1,)), ((), ()))
F32 = jnp.float32
BF16 = jnp.bfloat16


def mm(a, b):
    return jnp.dot(a, b, preferred_element_type=F32)


def mm_nt(a, b):
    return lax.dot_general(a, b, NT, preferred_element_type=F32)


def identity(n):
    rows = lax.broadcasted_iota(jnp.int32, (n, n), 0)
    return jnp.where(rows == lax.broadcasted_iota(jnp.int32, (n, n), 1), 1.0, 0.0).astype(BF16)


def lane_offset(tile, width=128):
    return pl.ds(pl.multiple_of(tile * width, width), width)


def exchange(a, b, width):
    kind = jnp.int16 if a.dtype == BF16 else jnp.int32
    lane = lax.broadcasted_iota(kind, a.shape, 1)
    even = jnp.bitwise_and(lane, jnp.full((), 2 * width - 1, kind)) < jnp.full((), width, kind)
    return jnp.where(even, a, pltpu.roll(b, width, 1)), jnp.where(even, pltpu.roll(a, 128 - width, 1), b)


def regroup(tiles):
    a0, a1 = exchange(tiles[0], tiles[1], 32)
    b0, b1 = exchange(tiles[2], tiles[3], 32)
    return *exchange(a0, b0, 16), *exchange(a1, b1, 16)


def ungroup(tiles):
    a0, b0 = exchange(tiles[0], tiles[1], 16)
    a1, b1 = exchange(tiles[2], tiles[3], 16)
    return *exchange(a0, a1, 32), *exchange(b0, b1, 32)


def store_pair(out_ref, pair, values):
    values = values.astype(BF16)
    first, second = exchange(values[:HALF], values[HALF:], MAIN)
    out_ref[pair, 0:HALF, :] = first
    out_ref[pair + PAIRS, 0:HALF, :] = second


def stage_copies(buffer_ref, out_ref, sems, stage):
    copies = []
    for side in range(2):
        devices = pl.ds(side * PAIRS + stage * STAGE, STAGE)
        copies.append(
            pltpu.make_async_copy(buffer_ref.at[devices], out_ref.at[devices], sems.at[2 * stage + side])
        )
    return copies


def start_stage(buffer_ref, out_ref, sems, done):
    if done % STAGE == 0:
        for copy in stage_copies(buffer_ref, out_ref, sems, done // STAGE - 1):
            copy.start()


def wait_stages(buffer_ref, out_ref, sems):
    for stage in range(PAIRS // STAGE):
        for copy in stage_copies(buffer_ref, out_ref, sems, stage):
            copy.wait()


def bias_column(bias_ref):
    rows = lax.broadcasted_iota(jnp.int32, (FEATURES, FEATURES), 0)
    lanes = lax.broadcasted_iota(jnp.int32, (FEATURES, FEATURES), 1)
    wide = jnp.broadcast_to(bias_ref[...].astype(F32).reshape(1, FEATURES), (FEATURES, FEATURES))
    return jnp.sum(jnp.where(rows == lanes, wide, 0.0), axis=1, keepdims=True)


def store_extra(out_ref, values):
    for part in range(3):
        piece = values[:, part * 128 : (part + 1) * 128].astype(BF16)
        out_ref[:, HALF + part * EXTRA : HALF + (part + 1) * EXTRA, :] = piece.reshape(GROUPS, EXTRA, 128)


def load_pair(in_ref, pair):
    return exchange(in_ref[pair, 0:HALF, :], in_ref[pair + PAIRS, 0:HALF, :], MAIN)


def unpack(in_ref, full_ref):
    for pair in range(PAIRS):
        top, bottom = load_pair(in_ref, pair)
        full_ref[0:HALF, pair * 128 : (pair + 1) * 128] = top
        full_ref[HALF:, pair * 128 : (pair + 1) * 128] = bottom
    unpack_extra(in_ref, full_ref)


def unpack_grouped(in_ref, full_ref):
    for quad in range(4):
        pairs = [load_pair(in_ref, 4 * quad + j) for j in range(4)]
        for half in range(2):
            tiles = regroup([pair[half] for pair in pairs])
            for quarter in range(QUARTERS):
                tile = 4 * quarter + quad
                full_ref[half * HALF : (half + 1) * HALF, tile * 128 : (tile + 1) * 128] = tiles[quarter]
    return unpack_extra(in_ref, full_ref)


def unpack_extra(in_ref, full_ref):
    eye = identity(128)
    turned, last = None, None
    for part in range(3):
        last = in_ref[:, HALF + part * EXTRA : HALF + (part + 1) * EXTRA, :].reshape(EXTRA_SLOTS, 128)
        turned = mm_nt(eye, last)
        height = min(128, FEATURES - part * 128)
        full_ref[part * 128 : part * 128 + height, MAIN_SLOTS:] = turned[:height].astype(BF16)
    return last, turned


def placed(slots, names, start, count):
    index = lax.broadcasted_iota(jnp.int16, (count, ROWS), 0) + jnp.int16(start)
    named = jnp.zeros((count, ROWS), BF16)
    for k in range(NAMED):
        named = jnp.where(index == jnp.broadcast_to(slots[k], index.shape), names[k], named)
    return named, jnp.minimum(named, BF16(1))


def prepare_kernel(act_ref, bias_ref, blocks_ref, out_ref, slots_ref, send_ref, sems):
    blocks = blocks_ref[...]
    group = lax.shift_right_logical(blocks, 3)
    local = jnp.bitwise_and(blocks, LOCAL - 1)
    count = GROUPS * QUARTERS
    groups = lax.broadcasted_iota(jnp.int32, (count, ROWS), 0)
    hits = [groups == group[k : k + 1, :] for k in range(NAMED)]
    small = lax.broadcasted_iota(jnp.int16, (count, ROWS), 0)
    counts = jnp.zeros((count, ROWS), BF16)
    for k in range(NAMED):
        hit = small == jnp.broadcast_to(group[k : k + 1, :].astype(jnp.int16), small.shape)
        counts = counts + jnp.where(hit, BF16(1), BF16(0))
    before = lax.broadcasted_iota(jnp.int16, (ROWS, ROWS), 0) < lax.broadcasted_iota(jnp.int16, (ROWS, ROWS), 1)
    earlier = mm(counts, jnp.where(before, BF16(1), BF16(0)))
    beyond = jnp.maximum(mm(counts, jnp.ones((ROWS, 128), BF16)) - SHARE, 0.0).astype(BF16)
    one = lax.broadcasted_iota(jnp.int32, (count, count), 0)
    other = lax.broadcasted_iota(jnp.int32, (count, count), 1)
    same = lax.shift_right_logical(one, 2) == lax.shift_right_logical(other, 2)
    offset = mm(jnp.where(same & (other < one), 1.0, 0.0).astype(BF16), beyond)
    table = earlier + 1024.0 * jnp.concatenate([offset] * (ROWS // 128), axis=1)
    slots, names, most = [], [], jnp.zeros((1, ROWS), jnp.int32)
    for k in range(NAMED):
        mine = group[k : k + 1, :]
        found = jnp.sum(jnp.where(hits[k], table, 0.0), axis=0, keepdims=True).astype(jnp.int32)
        rank = jnp.bitwise_and(found, 1023)
        for previous in range(k):
            rank = rank + jnp.where(group[previous : previous + 1, :] == mine, 1, 0)
        target = lax.shift_right_logical(mine, 2)
        place = (jnp.bitwise_and(target, PAIRS - 1) * 2 + lax.shift_right_logical(target, 4)) * MAIN
        main = place + jnp.bitwise_and(mine, QUARTERS - 1) * SHARE + rank
        extra = lax.shift_right_logical(found, 10) + rank - SHARE
        late = jnp.where(extra < EXTRA, MAIN_SLOTS + target * EXTRA + extra, -1)
        slots.append(jnp.where(rank < SHARE, main, late))
        names.append((local[k : k + 1, :] + 1).astype(F32).astype(BF16))
        most = jnp.maximum(most, jnp.where(rank < SHARE, 0, extra))
    over = jnp.where(jnp.max(most, axis=1, keepdims=True) >= EXTRA, 1.0, 0.0)
    shifted = (act_ref[...].astype(F32) - bias_column(bias_ref)).astype(BF16)

    for k in range(NAMED):
        slots_ref[k : k + 1, :] = slots[k]
    slots_ref[NAMED:, :] = jnp.zeros((8 - NAMED, ROWS), jnp.int32)
    slots = [slot.astype(jnp.int16) for slot in slots]
    named, place = placed(slots, names, MAIN_SLOTS, EXTRA_SLOTS)
    padded = jnp.concatenate([shifted, jnp.zeros((96, ROWS), BF16)], axis=0)
    values = mm_nt(place, padded)
    store_extra(send_ref, values)
    lane = lax.broadcasted_iota(jnp.int32, (EXTRA_SLOTS, 128), 1)
    ids = mm(named, jnp.ones((ROWS, 128), BF16))
    last = jnp.where(lane == 32, ids, values[:, 256:])
    row = lax.broadcasted_iota(jnp.int32, (EXTRA, 128), 0)
    high = lax.broadcasted_iota(jnp.int32, (EXTRA, 128), 1) >= MAIN
    flag = jnp.broadcast_to(over, (EXTRA, 128))
    for double in range(PAIRS // 2):
        named, place = placed(slots, names, double * 256, 256)
        values = mm_nt(shifted, place)
        ids = mm_nt(jnp.ones((EXTRA, ROWS), BF16), named)
        for side in range(2):
            pair = 2 * double + side
            store_pair(send_ref, pair, values[:, side * 128 : (side + 1) * 128])
            for half in range(2):
                device = pair + half * PAIRS
                mine = ids[:, side * 128 : (side + 1) * 128]
                mine = mine if half else pltpu.roll(mine, MAIN, 1)
                tile = last[device * EXTRA : (device + 1) * EXTRA]
                tile = jnp.where(high & (row == 0), mine, tile)
                tile = jnp.where(high & (row == 1), flag, tile)
                send_ref[device, HALF + 2 * EXTRA :, :] = tile.astype(BF16)
        start_stage(send_ref, out_ref, sems, 2 * double + 2)
    wait_stages(send_ref, out_ref, sems)


def encode_kernel(recv_ref, enc_ref, rest_ref, out_ref, ids_ref, over_ref, full_ref):
    last, turned = unpack_grouped(recv_ref, full_ref)
    pick = lax.broadcasted_iota(jnp.int32, (2 * GROUPS, EXTRA_SLOTS), 0)
    column = lax.broadcasted_iota(jnp.int32, (2 * GROUPS, EXTRA_SLOTS), 1)
    wanted = jnp.where(pick < GROUPS, pick * EXTRA, (pick - GROUPS) * EXTRA + 1)
    rows = mm(jnp.where(column == wanted, 1.0, 0.0).astype(BF16), last)
    first, second = rows[:PAIRS], rows[PAIRS:GROUPS]
    low = lax.broadcasted_iota(jnp.int32, (PAIRS, 128), 1) < MAIN
    named = jnp.where(low, pltpu.roll(first, MAIN, 1), second)
    picked = [[named[4 * quad + j : 4 * quad + j + 1] for quad in range(4)] for j in range(4)]
    tiles = regroup([jnp.concatenate(some, axis=0) for some in picked])
    for quarter in range(QUARTERS):
        ids_ref[4 * quarter : 4 * quarter + 4, :] = tiles[quarter]
    for part in range(EXTRA_SLOTS // 128):
        ids_ref[PAIRS + part : PAIRS + part + 1, :] = turned[32:33, part * 128 : (part + 1) * 128]
    ids_ref[LANE_TILES:, :] = jnp.zeros((24 - LANE_TILES, 128), F32)
    flags = jnp.where(lax.broadcasted_iota(jnp.int32, (GROUPS, 128), 1) == MAIN, rows[GROUPS:], 0.0)
    flag = jnp.max(jnp.max(flags, axis=1, keepdims=True), axis=0, keepdims=True)
    over_ref[0, 0] = jnp.max(flag).astype(jnp.int32)

    for tile in range(LANE_TILES // 2):
        lanes = slice(tile * 256, (tile + 1) * 256)
        ids = jnp.concatenate([ids_ref[2 * tile : 2 * tile + 1, :], ids_ref[2 * tile + 1 : 2 * tile + 2, :]], axis=1)
        code = ids.astype(jnp.int32) - 1
        main = tile < PAIRS // 2
        quarter = tile // 2 if main else 0
        first, held = (8 * quarter, 8) if main else (0, LOCAL)
        part = mm(enc_ref[first * BLOCK : (first + held) * BLOCK, 0:256], full_ref[0:256, lanes])
        total = jnp.zeros((BLOCK, 256), F32)
        for b in range(held):
            total = jnp.where(code == first + b, part[b * BLOCK : (b + 1) * BLOCK], total)
        rest = full_ref[256:, lanes]
        member = jnp.broadcast_to(jnp.bitwise_and(code, 7), (32, 256))
        spread = jnp.concatenate([jnp.where(member == m, rest, BF16(0)) for m in range(8)], axis=0)
        if main:
            more = mm(rest_ref[quarter * BLOCK : (quarter + 1) * BLOCK, :], spread)
        else:
            part = mm(rest_ref[...], spread)
            more = jnp.zeros((BLOCK, 256), F32)
            for g in range(QUARTERS):
                wanted = lax.shift_right_arithmetic(code, 3) == g
                more = jnp.where(wanted, part[g * BLOCK : (g + 1) * BLOCK], more)
        total = total + more
        for half in range(2):
            lane_tile = 2 * tile + half
            slot_row = (lane_tile % CHUNK_TILES) * 16
            for quarter in range(4):
                piece = total[quarter * 16 : (quarter + 1) * 16, half * 128 : (half + 1) * 128]
                out_ref[quarter + 4 * (lane_tile // CHUNK_TILES), slot_row : slot_row + 16, :] = piece.astype(BF16)


def load_codes(codes_ref, full_ref):
    for tile in range(LANE_TILES):
        for quarter in range(4):
            full_ref[quarter * 16 : (quarter + 1) * 16, tile * 128 : (tile + 1) * 128] = codes_ref[
                quarter + 4 * (tile // CHUNK_TILES),
                (tile % CHUNK_TILES) * 16 : (tile % CHUNK_TILES + 1) * 16,
                :,
            ]


def decode_kernel(codes_ref, ids_ref, dec_ref, send_ref, full_ref, extra_ref):
    load_codes(codes_ref, full_ref)

    def contribution(tile):
        codes = full_ref[:, tile * 256 : (tile + 1) * 256]
        ids = jnp.concatenate([ids_ref[2 * tile : 2 * tile + 1, :], ids_ref[2 * tile + 1 : 2 * tile + 2, :]], axis=1)
        ids = jnp.broadcast_to(ids, (BLOCK, 256)).astype(BF16)
        main = tile < PAIRS // 2
        first, held = (8 * (tile // 2), 8) if main else (0, LOCAL)
        spread = [jnp.where(ids == BF16(b + 1), codes, BF16(0)) for b in range(first, first + held)]
        weights = dec_ref[:, first * BLOCK : (first + held) * BLOCK]
        return mm(weights, jnp.concatenate(spread, axis=0)).astype(BF16)

    extra_ref[FEATURES:, :] = jnp.zeros((384 - FEATURES, EXTRA_SLOTS), BF16)
    for tile in range(PAIRS // 2, LANE_TILES // 2):
        start = tile * 256 - MAIN_SLOTS
        extra_ref[0:FEATURES, start : start + 256] = contribution(tile)
    store_extra(send_ref, mm_nt(identity(EXTRA_SLOTS), extra_ref[...]))
    for double in range(2):
        values = [contribution(2 * quarter + double) for quarter in range(QUARTERS)]
        for side in range(2):
            lanes = slice(side * 128, (side + 1) * 128)
            tops = ungroup([value[:HALF, lanes] for value in values])
            bottoms = ungroup([value[HALF:, lanes] for value in values])
            for j in range(4):
                pair = 8 * double + 4 * side + j
                first, second = exchange(tops[j], bottoms[j], MAIN)
                send_ref[pair, 0:HALF, :] = first
                send_ref[pair + PAIRS, 0:HALF, :] = second


def combine_kernel(
    recv_ref, slots_ref, act_ref, bias_ref, out_ref, loss_ref, full_ref, place_ref, send_ref, sems
):
    slots = [slots_ref[k : k + 1, :].astype(jnp.int16) for k in range(NAMED)]
    ones = [jnp.ones((1, ROWS), BF16)] * NAMED
    for start in range(0, SLOTS, 256):
        place_ref[start : start + 256, :] = placed(slots, ones, start, 256)[0]
    unpack(recv_ref, full_ref)
    error = mm(full_ref[...], place_ref[...]) + bias_column(bias_ref) - act_ref[...].astype(F32)
    sent = error.astype(BF16)
    padded = jnp.concatenate([sent, jnp.zeros((96, ROWS), BF16)], axis=0)
    store_extra(send_ref, mm_nt(place_ref[MAIN_SLOTS:, :], padded))
    for double in range(PAIRS // 2):
        values = mm_nt(sent, place_ref[double * 256 : (double + 1) * 256, :])
        store_pair(send_ref, 2 * double, values[:, :128])
        store_pair(send_ref, 2 * double + 1, values[:, 128:])
        start_stage(send_ref, out_ref, sems, 2 * double + 2)
    loss = jnp.sum(error * error, axis=0, keepdims=True)
    for part in range(ROWS // 128):
        loss_ref[part : part + 1, :] = loss[:, part * 128 : (part + 1) * 128]
    wait_stages(send_ref, out_ref, sems)


def gradient_kernel(
    recv_ref, codes_ref, ids_ref, loss_ref, out_ref, out_loss_ref, full_ref, code_ref, grad_ref, sems
):
    out_loss_ref[...] = loss_ref[...]
    unpack_grouped(recv_ref, full_ref)
    load_codes(codes_ref, code_ref)
    ids = jnp.concatenate([ids_ref[tile : tile + 1, :] for tile in range(LANE_TILES)], axis=1)
    ids = jnp.broadcast_to(ids, (BLOCK, SLOTS)).astype(BF16)
    copies, begin = [], 0
    for start in range(0, LOCAL * BLOCK, 256):
        stop = start + 256
        width = MAIN_SLOTS // QUARTERS
        lanes = slice(start // 512 * width, (start // 512 + 1) * width)

        def both(values):
            return jnp.concatenate([values[:, lanes], values[:, MAIN_SLOTS:]], axis=1)

        near, codes = both(ids), both(code_ref)
        spread = [jnp.where(near == BF16(b + 1), codes, BF16(0)) for b in range(start // BLOCK, stop // BLOCK)]
        grad_ref[:, start:stop] = mm_nt(both(full_ref), jnp.concatenate(spread, axis=0)).astype(BF16)
        if stop in (LOCAL * BLOCK * 3 // 4, LOCAL * BLOCK):
            lanes = pl.ds(begin, stop - begin)
            copy = pltpu.make_async_copy(grad_ref.at[:, lanes], out_ref.at[:, lanes], sems.at[len(copies)])
            copy.start()
            copies.append(copy)
            begin = stop
    for copy in copies:
        copy.wait()


def call(kernel, out_shape, scratch, flops, name, megabytes, **specs):
    return pl.pallas_call(
        kernel,
        out_shape=out_shape,
        scratch_shapes=scratch,
        name=name,
        **specs,
        compiler_params=pltpu.CompilerParams(vmem_limit_bytes=megabytes * 1024 * 1024),
        cost_estimate=pl.CostEstimate(flops=flops, bytes_accessed=6_000_000, transcendentals=0),
    )


def shape(dims, dtype=BF16):
    return jax.ShapeDtypeStruct(dims, dtype)


def in_hbm(dims, dtype=BF16):
    return pltpu.HBM(dims, dtype)


def route(buffer):
    return lax.all_to_all(buffer, PLANE, split_axis=0, concat_axis=0, tiled=True)


def fetch_kernel(weights_ref, held_ref, sem):
    copy = pltpu.make_async_copy(weights_ref, held_ref, sem)
    copy.start()
    copy.wait()


def sum_codes(partial, weights):
    shares = partial.reshape(4, SHARDS // 4 * CHUNK_ROWS, 128)
    received = lax.all_to_all(shares, INNER, split_axis=0, concat_axis=0, tiled=True)
    total = lax.psum(jnp.sum(received.astype(F32), axis=0), OUTER)
    codes = jnp.maximum(total, 0.0).astype(BF16)
    codes, weights = lax.optimization_barrier((codes, weights))
    copies = jnp.broadcast_to(codes[None], shares.shape)
    codes = lax.all_to_all(copies, INNER, split_axis=0, concat_axis=0, tiled=True)
    held = call(
        fetch_kernel,
        pltpu.VMEM(weights.shape, BF16),
        [pltpu.SemaphoreType.DMA],
        0,
        "fetch",
        4,
        in_specs=[pl.BlockSpec(memory_space=pltpu.HBM)],
        out_specs=pl.BlockSpec(memory_space=pltpu.VMEM),
    )(weights)
    return codes.reshape(partial.shape), held


def sum_loss(part):
    return lax.psum(lax.psum(part, OUTER), INNER)


def padded_plan(activations, bias_dec, encoder, decoder, active_blocks):
    row_count, shard_width = activations.shape
    per_row = active_blocks.shape[1]
    groups = lax.axis_size(PLANE)
    local_blocks = encoder.shape[1] // BLOCK
    total_blocks = local_blocks * groups
    capacity = max(2, 2 * row_count * per_row // total_blocks)
    slot_count = total_blocks * capacity
    pair_blocks = active_blocks.reshape(-1)
    pair_iota = jnp.arange(pair_blocks.shape[0], dtype=jnp.int32)
    same_block = pair_blocks[:, None] == pair_blocks[None, :]
    earlier = pair_iota[None, :] < pair_iota[:, None]
    block_rank = jnp.sum((same_block & earlier).astype(jnp.int32), axis=1)
    slot_index = (pair_blocks * capacity + block_rank).reshape(row_count, per_row)
    slot_iota = jnp.arange(slot_count, dtype=jnp.int32)
    placement = jnp.zeros((slot_count, row_count), BF16)
    for which in range(per_row):
        placement = placement + (slot_index[:, which][None, :] == slot_iota[:, None]).astype(BF16)
    slot_shape = (groups, local_blocks, capacity, shard_width)

    def scatter_rows(values):
        filled = jnp.dot(placement, values, preferred_element_type=F32).astype(values.dtype)
        return filled.reshape(slot_shape)

    bias_wide = bias_dec.astype(F32)[None, :]
    shifted = (activations.astype(F32) - bias_wide).astype(BF16)
    received = route(scatter_rows(shifted))
    enc_local = encoder.reshape(shard_width, local_blocks, BLOCK)
    partial_pre = jnp.einsum("sbkd,dbl->sbkl", received, enc_local, preferred_element_type=F32)
    pre_total = lax.psum(partial_pre, DP)
    latent_codes = jnp.maximum(pre_total, 0.0).astype(BF16)
    dec_local = decoder.reshape(local_blocks, BLOCK, shard_width)
    contrib = jnp.einsum("sbkl,bld->sbkd", latent_codes, dec_local, preferred_element_type=F32).astype(BF16)
    returned = route(contrib).reshape(slot_count, shard_width)
    summed_rows = jnp.einsum("sr,sd->rd", placement, returned, preferred_element_type=F32)
    error = summed_rows + bias_wide - activations.astype(F32)
    row_loss = lax.psum(jnp.sum(error * error, axis=1), DP)
    error_sent = route(scatter_rows(error.astype(BF16)))
    gradient = jnp.einsum("sbkl,sbkd->bld", latent_codes, error_sent, preferred_element_type=F32)
    return gradient.reshape(local_blocks * BLOCK, shard_width).astype(BF16), row_loss


def on_device(activations, bias_dec, encoder, decoder, active_blocks):
    act = activations.T
    bias = bias_dec
    packed = in_hbm((GROUPS, PACKED, 128))
    full = pltpu.VMEM((FEATURES, SLOTS), BF16)
    sending = [pltpu.VMEM((GROUPS, PACKED, 128), BF16), pltpu.SemaphoreType.DMA((2 * PAIRS // STAGE,))]
    vmem, hbm = pl.BlockSpec(memory_space=pltpu.VMEM), pl.BlockSpec(memory_space=pltpu.HBM)
    spread_flops = 2 * FEATURES * SLOTS * LOCAL * BLOCK
    sent, slots = call(
        prepare_kernel,
        (packed, shape((8, ROWS), jnp.int32)),
        sending,
        2 * FEATURES * SLOTS * ROWS,
        "prepare",
        20,
        out_specs=(hbm, vmem),
    )(act, bias, active_blocks.T)
    received = route(sent)
    turned = encoder.T
    rest = turned[:, 256:].reshape(4, 8, BLOCK, 32).transpose(0, 2, 1, 3).reshape(4 * BLOCK, 256)
    partial, ids, over = call(
        encode_kernel,
        (shape((SHARDS, CHUNK_ROWS, 128)), shape((24, 128), F32), shape((1, 1), jnp.int32)),
        [full],
        spread_flops,
        "encode",
        20,
        out_specs=(vmem, vmem, pl.BlockSpec(memory_space=pltpu.SMEM)),
    )(received, turned, rest)
    codes, weights = sum_codes(partial, decoder.T)
    sent = call(
        decode_kernel,
        shape((GROUPS, PACKED, 128)),
        [
            pltpu.VMEM((BLOCK, SLOTS), BF16),
            pltpu.VMEM((384, EXTRA_SLOTS), BF16),
        ],
        spread_flops,
        "decode",
        20,
    )(codes, ids, weights)
    received = route(sent)
    sent, loss = call(
        combine_kernel,
        (packed, shape((ROWS // 128, 128), F32)),
        [full, pltpu.VMEM((SLOTS, ROWS), BF16)] + sending,
        4 * FEATURES * SLOTS * ROWS,
        "combine",
        20,
        out_specs=(hbm, vmem),
    )(received, slots, act, bias)
    received = route(sent)
    loss = sum_loss(loss)

    def packed_plan():
        gradient, row_loss = call(
            gradient_kernel,
            (in_hbm((FEATURES, LOCAL * BLOCK)), in_hbm((ROWS // 128, 128), F32)),
            [
                full,
                pltpu.VMEM((BLOCK, SLOTS), BF16),
                pltpu.VMEM((FEATURES, LOCAL * BLOCK), BF16),
                pltpu.SemaphoreType.DMA((2,)),
            ],
            spread_flops,
            "gradient",
            24,
            out_specs=(hbm, vmem),
        )(pltpu.with_memory_space_constraint(received, pltpu.VMEM), codes, ids, loss)
        return gradient.T, row_loss.reshape(ROWS)

    return lax.cond(
        over[0, 0] > 0,
        lambda: padded_plan(activations, bias_dec, encoder, decoder, active_blocks),
        packed_plan,
    )


def solution(mesh):
    split = jax.sharding.Mesh(mesh.devices.reshape(4, 4, 8, 4), (OUTER, INNER) + PLANE)
    placed = (
        P(PLANE, DP),
        P(DP),
        P(DP, PLANE),
        P(PLANE, DP),
        P(PLANE, None),
    )
    return jax.shard_map(
        on_device,
        mesh=split,
        in_specs=placed,
        out_specs=(P(PLANE, DP), P(PLANE)),
        check_vma=False,
    )
```

```python
import jax
import jax.numpy as jnp
from jax import lax
from jax.experimental import pallas as pl
from jax.experimental.pallas import tpu as pltpu
from jax.sharding import PartitionSpec as P

BLOCK = 64
PLANE = ("latent", "section")
OUTER, INNER = "dp_outer", "dp_inner"
DP = (OUTER, INNER)
GROUPS = 32
SHARDS = 16
LOCAL = 32
ROWS = 512
FEATURES = 288
HALF = FEATURES // 2
NAMED = 4
QUARTERS = 4
SHARE = 16
MAIN = QUARTERS * SHARE
EXTRA = 16
MAIN_SLOTS = GROUPS * MAIN
EXTRA_SLOTS = GROUPS * EXTRA
SLOTS = MAIN_SLOTS + EXTRA_SLOTS
PACKED = HALF + 3 * EXTRA
PAIRS = GROUPS // 2
STAGE = 4
LANE_TILES = SLOTS // 128
CHUNK_TILES = 5
CHUNK_ROWS = 16 * CHUNK_TILES

NT = (((1,), (1,)), ((), ()))
F32 = jnp.float32
BF16 = jnp.bfloat16


def mm(a, b):
    return jnp.dot(a, b, preferred_element_type=F32)


def mm_nt(a, b):
    return lax.dot_general(a, b, NT, preferred_element_type=F32)


def identity(n):
    rows = lax.broadcasted_iota(jnp.int32, (n, n), 0)
    return jnp.where(rows == lax.broadcasted_iota(jnp.int32, (n, n), 1), 1.0, 0.0).astype(BF16)


def lane_offset(tile, width=128):
    return pl.ds(pl.multiple_of(tile * width, width), width)


def exchange(a, b, width):
    kind = jnp.int16 if a.dtype == BF16 else jnp.int32
    lane = lax.broadcasted_iota(kind, a.shape, 1)
    even = jnp.bitwise_and(lane, jnp.full((), 2 * width - 1, kind)) < jnp.full((), width, kind)
    return jnp.where(even, a, pltpu.roll(b, width, 1)), jnp.where(even, pltpu.roll(a, 128 - width, 1), b)


def regroup(tiles):
    a0, a1 = exchange(tiles[0], tiles[1], 32)
    b0, b1 = exchange(tiles[2], tiles[3], 32)
    return *exchange(a0, b0, 16), *exchange(a1, b1, 16)


def ungroup(tiles):
    a0, b0 = exchange(tiles[0], tiles[1], 16)
    a1, b1 = exchange(tiles[2], tiles[3], 16)
    return *exchange(a0, a1, 32), *exchange(b0, b1, 32)


def store_pair(out_ref, pair, values):
    values = values.astype(BF16)
    first, second = exchange(values[:HALF], values[HALF:], MAIN)
    out_ref[pair, 0:HALF, :] = first
    out_ref[pair + PAIRS, 0:HALF, :] = second


def stage_copies(buffer_ref, out_ref, sems, stage):
    copies = []
    for side in range(2):
        devices = pl.ds(side * PAIRS + stage * STAGE, STAGE)
        copies.append(
            pltpu.make_async_copy(buffer_ref.at[devices], out_ref.at[devices], sems.at[2 * stage + side])
        )
    return copies


def start_stage(buffer_ref, out_ref, sems, done):
    if done % STAGE == 0:
        for copy in stage_copies(buffer_ref, out_ref, sems, done // STAGE - 1):
            copy.start()


def wait_stages(buffer_ref, out_ref, sems):
    for stage in range(PAIRS // STAGE):
        for copy in stage_copies(buffer_ref, out_ref, sems, stage):
            copy.wait()


def bias_column(bias_ref):
    rows = lax.broadcasted_iota(jnp.int32, (FEATURES, FEATURES), 0)
    lanes = lax.broadcasted_iota(jnp.int32, (FEATURES, FEATURES), 1)
    wide = jnp.broadcast_to(bias_ref[...].astype(F32).reshape(1, FEATURES), (FEATURES, FEATURES))
    return jnp.sum(jnp.where(rows == lanes, wide, 0.0), axis=1, keepdims=True)


def store_extra(out_ref, values):
    for part in range(3):
        piece = values[:, part * 128 : (part + 1) * 128].astype(BF16)
        out_ref[:, HALF + part * EXTRA : HALF + (part + 1) * EXTRA, :] = piece.reshape(GROUPS, EXTRA, 128)


def load_pair(in_ref, pair):
    return exchange(in_ref[pair, 0:HALF, :], in_ref[pair + PAIRS, 0:HALF, :], MAIN)


def unpack(in_ref, full_ref):
    for pair in range(PAIRS):
        top, bottom = load_pair(in_ref, pair)
        full_ref[0:HALF, pair * 128 : (pair + 1) * 128] = top
        full_ref[HALF:, pair * 128 : (pair + 1) * 128] = bottom
    unpack_extra(in_ref, full_ref)


def unpack_grouped(in_ref, full_ref):
    for quad in range(4):
        pairs = [load_pair(in_ref, 4 * quad + j) for j in range(4)]
        for half in range(2):
            tiles = regroup([pair[half] for pair in pairs])
            for quarter in range(QUARTERS):
                tile = 4 * quarter + quad
                full_ref[half * HALF : (half + 1) * HALF, tile * 128 : (tile + 1) * 128] = tiles[quarter]
    return unpack_extra(in_ref, full_ref)


def unpack_extra(in_ref, full_ref):
    eye = identity(128)
    turned, last = None, None
    for part in range(3):
        last = in_ref[:, HALF + part * EXTRA : HALF + (part + 1) * EXTRA, :].reshape(EXTRA_SLOTS, 128)
        turned = mm_nt(eye, last)
        height = min(128, FEATURES - part * 128)
        full_ref[part * 128 : part * 128 + height, MAIN_SLOTS:] = turned[:height].astype(BF16)
    return last, turned


def placed(slots, names, start, count):
    index = lax.broadcasted_iota(jnp.int16, (count, ROWS), 0) + jnp.int16(start)
    named = jnp.zeros((count, ROWS), BF16)
    for k in range(NAMED):
        named = jnp.where(index == jnp.broadcast_to(slots[k], index.shape), names[k], named)
    return named, jnp.minimum(named, BF16(1))


def prepare_kernel(act_ref, bias_ref, blocks_ref, out_ref, slots_ref, send_ref, sems):
    blocks = blocks_ref[...]
    group = lax.shift_right_logical(blocks, 3)
    local = jnp.bitwise_and(blocks, LOCAL - 1)
    count = GROUPS * QUARTERS
    groups = lax.broadcasted_iota(jnp.int32, (count, ROWS), 0)
    hits = [groups == group[k : k + 1, :] for k in range(NAMED)]
    small = lax.broadcasted_iota(jnp.int16, (count, ROWS), 0)
    counts = jnp.zeros((count, ROWS), BF16)
    for k in range(NAMED):
        hit = small == jnp.broadcast_to(group[k : k + 1, :].astype(jnp.int16), small.shape)
        counts = counts + jnp.where(hit, BF16(1), BF16(0))
    before = lax.broadcasted_iota(jnp.int16, (ROWS, ROWS), 0) < lax.broadcasted_iota(jnp.int16, (ROWS, ROWS), 1)
    earlier = mm(counts, jnp.where(before, BF16(1), BF16(0)))
    beyond = jnp.maximum(mm(counts, jnp.ones((ROWS, 128), BF16)) - SHARE, 0.0).astype(BF16)
    one = lax.broadcasted_iota(jnp.int32, (count, count), 0)
    other = lax.broadcasted_iota(jnp.int32, (count, count), 1)
    same = lax.shift_right_logical(one, 2) == lax.shift_right_logical(other, 2)
    offset = mm(jnp.where(same & (other < one), 1.0, 0.0).astype(BF16), beyond)
    table = earlier + 1024.0 * jnp.concatenate([offset] * (ROWS // 128), axis=1)
    slots, names, most = [], [], jnp.zeros((1, ROWS), jnp.int32)
    for k in range(NAMED):
        mine = group[k : k + 1, :]
        found = jnp.sum(jnp.where(hits[k], table, 0.0), axis=0, keepdims=True).astype(jnp.int32)
        rank = jnp.bitwise_and(found, 1023)
        for previous in range(k):
            rank = rank + jnp.where(group[previous : previous + 1, :] == mine, 1, 0)
        target = lax.shift_right_logical(mine, 2)
        place = (jnp.bitwise_and(target, PAIRS - 1) * 2 + lax.shift_right_logical(target, 4)) * MAIN
        main = place + jnp.bitwise_and(mine, QUARTERS - 1) * SHARE + rank
        extra = lax.shift_right_logical(found, 10) + rank - SHARE
        late = jnp.where(extra < EXTRA, MAIN_SLOTS + target * EXTRA + extra, -1)
        slots.append(jnp.where(rank < SHARE, main, late))
        names.append((local[k : k + 1, :] + 1).astype(F32).astype(BF16))
        most = jnp.maximum(most, jnp.where(rank < SHARE, 0, extra))
    over = jnp.where(jnp.max(most, axis=1, keepdims=True) >= EXTRA, 1.0, 0.0)
    shifted = (act_ref[...].astype(F32) - bias_column(bias_ref)).astype(BF16)

    for k in range(NAMED):
        slots_ref[k : k + 1, :] = slots[k]
    slots_ref[NAMED:, :] = jnp.zeros((8 - NAMED, ROWS), jnp.int32)
    slots = [slot.astype(jnp.int16) for slot in slots]
    named, place = placed(slots, names, MAIN_SLOTS, EXTRA_SLOTS)
    padded = jnp.concatenate([shifted, jnp.zeros((96, ROWS), BF16)], axis=0)
    values = mm_nt(place, padded)
    store_extra(send_ref, values)
    lane = lax.broadcasted_iota(jnp.int32, (EXTRA_SLOTS, 128), 1)
    ids = mm(named, jnp.ones((ROWS, 128), BF16))
    last = jnp.where(lane == 32, ids, values[:, 256:])
    row = lax.broadcasted_iota(jnp.int32, (EXTRA, 128), 0)
    high = lax.broadcasted_iota(jnp.int32, (EXTRA, 128), 1) >= MAIN
    flag = jnp.broadcast_to(over, (EXTRA, 128))
    for double in range(PAIRS // 2):
        named, place = placed(slots, names, double * 256, 256)
        values = mm_nt(shifted, place)
        ids = mm_nt(jnp.ones((EXTRA, ROWS), BF16), named)
        for side in range(2):
            pair = 2 * double + side
            store_pair(send_ref, pair, values[:, side * 128 : (side + 1) * 128])
            for half in range(2):
                device = pair + half * PAIRS
                mine = ids[:, side * 128 : (side + 1) * 128]
                mine = mine if half else pltpu.roll(mine, MAIN, 1)
                tile = last[device * EXTRA : (device + 1) * EXTRA]
                tile = jnp.where(high & (row == 0), mine, tile)
                tile = jnp.where(high & (row == 1), flag, tile)
                send_ref[device, HALF + 2 * EXTRA :, :] = tile.astype(BF16)
        start_stage(send_ref, out_ref, sems, 2 * double + 2)
    wait_stages(send_ref, out_ref, sems)


def encode_kernel(recv_ref, enc_ref, rest_ref, out_ref, ids_ref, over_ref, full_ref):
    last, turned = unpack_grouped(recv_ref, full_ref)
    pick = lax.broadcasted_iota(jnp.int32, (2 * GROUPS, EXTRA_SLOTS), 0)
    column = lax.broadcasted_iota(jnp.int32, (2 * GROUPS, EXTRA_SLOTS), 1)
    wanted = jnp.where(pick < GROUPS, pick * EXTRA, (pick - GROUPS) * EXTRA + 1)
    rows = mm(jnp.where(column == wanted, 1.0, 0.0).astype(BF16), last)
    first, second = rows[:PAIRS], rows[PAIRS:GROUPS]
    low = lax.broadcasted_iota(jnp.int32, (PAIRS, 128), 1) < MAIN
    named = jnp.where(low, pltpu.roll(first, MAIN, 1), second)
    picked = [[named[4 * quad + j : 4 * quad + j + 1] for quad in range(4)] for j in range(4)]
    tiles = regroup([jnp.concatenate(some, axis=0) for some in picked])
    for quarter in range(QUARTERS):
        ids_ref[4 * quarter : 4 * quarter + 4, :] = tiles[quarter]
    for part in range(EXTRA_SLOTS // 128):
        ids_ref[PAIRS + part : PAIRS + part + 1, :] = turned[32:33, part * 128 : (part + 1) * 128]
    ids_ref[LANE_TILES:, :] = jnp.zeros((24 - LANE_TILES, 128), F32)
    flags = jnp.where(lax.broadcasted_iota(jnp.int32, (GROUPS, 128), 1) == MAIN, rows[GROUPS:], 0.0)
    flag = jnp.max(jnp.max(flags, axis=1, keepdims=True), axis=0, keepdims=True)
    over_ref[0, 0] = jnp.max(flag).astype(jnp.int32)

    for tile in range(LANE_TILES // 2):
        lanes = slice(tile * 256, (tile + 1) * 256)
        ids = jnp.concatenate([ids_ref[2 * tile : 2 * tile + 1, :], ids_ref[2 * tile + 1 : 2 * tile + 2, :]], axis=1)
        code = ids.astype(jnp.int32) - 1
        main = tile < PAIRS // 2
        quarter = tile // 2 if main else 0
        first, held = (8 * quarter, 8) if main else (0, LOCAL)
        part = mm(enc_ref[first * BLOCK : (first + held) * BLOCK, 0:256], full_ref[0:256, lanes])
        total = jnp.zeros((BLOCK, 256), F32)
        for b in range(held):
            total = jnp.where(code == first + b, part[b * BLOCK : (b + 1) * BLOCK], total)
        rest = full_ref[256:, lanes]
        member = jnp.broadcast_to(jnp.bitwise_and(code, 7), (32, 256))
        spread = jnp.concatenate([jnp.where(member == m, rest, BF16(0)) for m in range(8)], axis=0)
        if main:
            more = mm(rest_ref[quarter * BLOCK : (quarter + 1) * BLOCK, :], spread)
        else:
            part = mm(rest_ref[...], spread)
            more = jnp.zeros((BLOCK, 256), F32)
            for g in range(QUARTERS):
                wanted = lax.shift_right_arithmetic(code, 3) == g
                more = jnp.where(wanted, part[g * BLOCK : (g + 1) * BLOCK], more)
        total = total + more
        for half in range(2):
            lane_tile = 2 * tile + half
            slot_row = (lane_tile % CHUNK_TILES) * 16
            for quarter in range(4):
                piece = total[quarter * 16 : (quarter + 1) * 16, half * 128 : (half + 1) * 128]
                out_ref[quarter + 4 * (lane_tile // CHUNK_TILES), slot_row : slot_row + 16, :] = piece.astype(BF16)


def load_codes(codes_ref, full_ref):
    for tile in range(LANE_TILES):
        for quarter in range(4):
            full_ref[quarter * 16 : (quarter + 1) * 16, tile * 128 : (tile + 1) * 128] = codes_ref[
                quarter + 4 * (tile // CHUNK_TILES),
                (tile % CHUNK_TILES) * 16 : (tile % CHUNK_TILES + 1) * 16,
                :,
            ]


def decode_kernel(codes_ref, ids_ref, weights_ref, send_ref, full_ref, extra_ref, dec_ref, sems):
    fetches = []
    for quarter in range(QUARTERS):
        lanes = pl.ds(quarter * 8 * BLOCK, 8 * BLOCK)
        fetches.append(
            pltpu.make_async_copy(weights_ref.at[:, lanes], dec_ref.at[:, lanes], sems.at[quarter])
        )
        fetches[-1].start()
    load_codes(codes_ref, full_ref)

    def contribution(tile):
        codes = full_ref[:, tile * 256 : (tile + 1) * 256]
        ids = jnp.concatenate([ids_ref[2 * tile : 2 * tile + 1, :], ids_ref[2 * tile + 1 : 2 * tile + 2, :]], axis=1)
        ids = jnp.broadcast_to(ids, (BLOCK, 256)).astype(BF16)
        main = tile < PAIRS // 2
        first, held = (8 * (tile // 2), 8) if main else (0, LOCAL)
        spread = [jnp.where(ids == BF16(b + 1), codes, BF16(0)) for b in range(first, first + held)]
        weights = dec_ref[:, first * BLOCK : (first + held) * BLOCK]
        return mm(weights, jnp.concatenate(spread, axis=0)).astype(BF16)

    for double in range(2):
        values = []
        for quarter in range(QUARTERS):
            if double == 0:
                fetches[quarter].wait()
            values.append(contribution(2 * quarter + double))
        for side in range(2):
            lanes = slice(side * 128, (side + 1) * 128)
            tops = ungroup([value[:HALF, lanes] for value in values])
            bottoms = ungroup([value[HALF:, lanes] for value in values])
            for j in range(4):
                pair = 8 * double + 4 * side + j
                first, second = exchange(tops[j], bottoms[j], MAIN)
                send_ref[pair, 0:HALF, :] = first
                send_ref[pair + PAIRS, 0:HALF, :] = second
    extra_ref[FEATURES:, :] = jnp.zeros((384 - FEATURES, EXTRA_SLOTS), BF16)
    for tile in range(PAIRS // 2, LANE_TILES // 2):
        start = tile * 256 - MAIN_SLOTS
        extra_ref[0:FEATURES, start : start + 256] = contribution(tile)
    store_extra(send_ref, mm_nt(identity(EXTRA_SLOTS), extra_ref[...]))


def combine_kernel(
    recv_ref, slots_ref, act_ref, bias_ref, out_ref, loss_ref, full_ref, place_ref, send_ref, sems
):
    slots = [slots_ref[k : k + 1, :].astype(jnp.int16) for k in range(NAMED)]
    ones = [jnp.ones((1, ROWS), BF16)] * NAMED
    for start in range(0, SLOTS, 256):
        place_ref[start : start + 256, :] = placed(slots, ones, start, 256)[0]
    unpack(recv_ref, full_ref)
    error = mm(full_ref[...], place_ref[...]) + bias_column(bias_ref) - act_ref[...].astype(F32)
    sent = error.astype(BF16)
    padded = jnp.concatenate([sent, jnp.zeros((96, ROWS), BF16)], axis=0)
    store_extra(send_ref, mm_nt(place_ref[MAIN_SLOTS:, :], padded))
    for double in range(PAIRS // 2):
        values = mm_nt(sent, place_ref[double * 256 : (double + 1) * 256, :])
        store_pair(send_ref, 2 * double, values[:, :128])
        store_pair(send_ref, 2 * double + 1, values[:, 128:])
        start_stage(send_ref, out_ref, sems, 2 * double + 2)
    loss = jnp.sum(error * error, axis=0, keepdims=True)
    for part in range(ROWS // 128):
        loss_ref[part : part + 1, :] = loss[:, part * 128 : (part + 1) * 128]
    wait_stages(send_ref, out_ref, sems)


def gradient_kernel(
    recv_ref, codes_ref, ids_ref, loss_ref, out_ref, out_loss_ref, full_ref, code_ref, grad_ref, sems
):
    out_loss_ref[...] = loss_ref[...]
    unpack_grouped(recv_ref, full_ref)
    load_codes(codes_ref, code_ref)
    ids = jnp.concatenate([ids_ref[tile : tile + 1, :] for tile in range(LANE_TILES)], axis=1)
    ids = jnp.broadcast_to(ids, (BLOCK, SLOTS)).astype(BF16)
    copies, begin = [], 0
    for start in range(0, LOCAL * BLOCK, 256):
        stop = start + 256
        width = MAIN_SLOTS // QUARTERS
        lanes = slice(start // 512 * width, (start // 512 + 1) * width)

        def both(values):
            return jnp.concatenate([values[:, lanes], values[:, MAIN_SLOTS:]], axis=1)

        near, codes = both(ids), both(code_ref)
        spread = [jnp.where(near == BF16(b + 1), codes, BF16(0)) for b in range(start // BLOCK, stop // BLOCK)]
        grad_ref[:, start:stop] = mm_nt(both(full_ref), jnp.concatenate(spread, axis=0)).astype(BF16)
        if stop in (LOCAL * BLOCK * 3 // 4, LOCAL * BLOCK):
            lanes = pl.ds(begin, stop - begin)
            copy = pltpu.make_async_copy(grad_ref.at[:, lanes], out_ref.at[:, lanes], sems.at[len(copies)])
            copy.start()
            copies.append(copy)
            begin = stop
    for copy in copies:
        copy.wait()


def call(kernel, out_shape, scratch, flops, name, megabytes, **specs):
    return pl.pallas_call(
        kernel,
        out_shape=out_shape,
        scratch_shapes=scratch,
        name=name,
        **specs,
        compiler_params=pltpu.CompilerParams(vmem_limit_bytes=megabytes * 1024 * 1024),
        cost_estimate=pl.CostEstimate(flops=flops, bytes_accessed=6_000_000, transcendentals=0),
    )


def shape(dims, dtype=BF16):
    return jax.ShapeDtypeStruct(dims, dtype)


def in_hbm(dims, dtype=BF16):
    return pltpu.HBM(dims, dtype)


def route(buffer):
    return lax.all_to_all(buffer, PLANE, split_axis=0, concat_axis=0, tiled=True)


def sum_codes(partial):
    shares = partial.reshape(4, SHARDS // 4 * CHUNK_ROWS, 128)
    received = lax.all_to_all(shares, INNER, split_axis=0, concat_axis=0, tiled=True)
    total = lax.psum(jnp.sum(received.astype(F32), axis=0), OUTER)
    codes = jnp.maximum(total, 0.0).astype(BF16)
    copies = jnp.broadcast_to(codes[None], shares.shape)
    return lax.all_to_all(copies, INNER, split_axis=0, concat_axis=0, tiled=True).reshape(partial.shape)


def sum_loss(part):
    return lax.psum(lax.psum(part, OUTER), INNER)


def padded_plan(activations, bias_dec, encoder, decoder, active_blocks):
    row_count, shard_width = activations.shape
    per_row = active_blocks.shape[1]
    groups = lax.axis_size(PLANE)
    local_blocks = encoder.shape[1] // BLOCK
    total_blocks = local_blocks * groups
    capacity = max(2, 2 * row_count * per_row // total_blocks)
    slot_count = total_blocks * capacity
    pair_blocks = active_blocks.reshape(-1)
    pair_iota = jnp.arange(pair_blocks.shape[0], dtype=jnp.int32)
    same_block = pair_blocks[:, None] == pair_blocks[None, :]
    earlier = pair_iota[None, :] < pair_iota[:, None]
    block_rank = jnp.sum((same_block & earlier).astype(jnp.int32), axis=1)
    slot_index = (pair_blocks * capacity + block_rank).reshape(row_count, per_row)
    slot_iota = jnp.arange(slot_count, dtype=jnp.int32)
    placement = jnp.zeros((slot_count, row_count), BF16)
    for which in range(per_row):
        placement = placement + (slot_index[:, which][None, :] == slot_iota[:, None]).astype(BF16)
    slot_shape = (groups, local_blocks, capacity, shard_width)

    def scatter_rows(values):
        filled = jnp.dot(placement, values, preferred_element_type=F32).astype(values.dtype)
        return filled.reshape(slot_shape)

    bias_wide = bias_dec.astype(F32)[None, :]
    shifted = (activations.astype(F32) - bias_wide).astype(BF16)
    received = route(scatter_rows(shifted))
    enc_local = encoder.reshape(shard_width, local_blocks, BLOCK)
    partial_pre = jnp.einsum("sbkd,dbl->sbkl", received, enc_local, preferred_element_type=F32)
    pre_total = lax.psum(partial_pre, DP)
    latent_codes = jnp.maximum(pre_total, 0.0).astype(BF16)
    dec_local = decoder.reshape(local_blocks, BLOCK, shard_width)
    contrib = jnp.einsum("sbkl,bld->sbkd", latent_codes, dec_local, preferred_element_type=F32).astype(BF16)
    returned = route(contrib).reshape(slot_count, shard_width)
    summed_rows = jnp.einsum("sr,sd->rd", placement, returned, preferred_element_type=F32)
    error = summed_rows + bias_wide - activations.astype(F32)
    row_loss = lax.psum(jnp.sum(error * error, axis=1), DP)
    error_sent = route(scatter_rows(error.astype(BF16)))
    gradient = jnp.einsum("sbkl,sbkd->bld", latent_codes, error_sent, preferred_element_type=F32)
    return gradient.reshape(local_blocks * BLOCK, shard_width).astype(BF16), row_loss


def on_device(activations, bias_dec, encoder, decoder, active_blocks):
    act = activations.T
    bias = bias_dec
    packed = in_hbm((GROUPS, PACKED, 128))
    full = pltpu.VMEM((FEATURES, SLOTS), BF16)
    sending = [pltpu.VMEM((GROUPS, PACKED, 128), BF16), pltpu.SemaphoreType.DMA((2 * PAIRS // STAGE,))]
    vmem, hbm = pl.BlockSpec(memory_space=pltpu.VMEM), pl.BlockSpec(memory_space=pltpu.HBM)
    spread_flops = 2 * FEATURES * SLOTS * LOCAL * BLOCK
    sent, slots = call(
        prepare_kernel,
        (packed, shape((8, ROWS), jnp.int32)),
        sending,
        2 * FEATURES * SLOTS * ROWS,
        "prepare",
        20,
        out_specs=(hbm, vmem),
    )(act, bias, active_blocks.T)
    received = route(sent)
    turned = encoder.T
    rest = turned[:, 256:].reshape(4, 8, BLOCK, 32).transpose(0, 2, 1, 3).reshape(4 * BLOCK, 256)
    partial, ids, over = call(
        encode_kernel,
        (shape((SHARDS, CHUNK_ROWS, 128)), shape((24, 128), F32), shape((1, 1), jnp.int32)),
        [full],
        spread_flops,
        "encode",
        20,
        out_specs=(vmem, vmem, pl.BlockSpec(memory_space=pltpu.SMEM)),
    )(received, turned, rest)
    codes = sum_codes(partial)
    sent = call(
        decode_kernel,
        shape((GROUPS, PACKED, 128)),
        [
            pltpu.VMEM((BLOCK, SLOTS), BF16),
            pltpu.VMEM((384, EXTRA_SLOTS), BF16),
            pltpu.VMEM((FEATURES, LOCAL * BLOCK), BF16),
            pltpu.SemaphoreType.DMA((QUARTERS,)),
        ],
        spread_flops,
        "decode",
        20,
        in_specs=(vmem, vmem, hbm),
    )(codes, ids, decoder.T)
    received = route(sent)
    sent, loss = call(
        combine_kernel,
        (packed, shape((ROWS // 128, 128), F32)),
        [full, pltpu.VMEM((SLOTS, ROWS), BF16)] + sending,
        4 * FEATURES * SLOTS * ROWS,
        "combine",
        20,
        out_specs=(hbm, vmem),
    )(received, slots, act, bias)
    received = route(sent)
    loss = sum_loss(loss)

    def packed_plan():
        gradient, row_loss = call(
            gradient_kernel,
            (in_hbm((FEATURES, LOCAL * BLOCK)), in_hbm((ROWS // 128, 128), F32)),
            [
                full,
                pltpu.VMEM((BLOCK, SLOTS), BF16),
                pltpu.VMEM((FEATURES, LOCAL * BLOCK), BF16),
                pltpu.SemaphoreType.DMA((2,)),
            ],
            spread_flops,
            "gradient",
            24,
            out_specs=(hbm, vmem),
        )(pltpu.with_memory_space_constraint(received, pltpu.VMEM), codes, ids, loss)
        return gradient.T, row_loss.reshape(ROWS)

    return lax.cond(
        over[0, 0] > 0,
        lambda: padded_plan(activations, bias_dec, encoder, decoder, active_blocks),
        packed_plan,
    )


def solution(mesh):
    split = jax.sharding.Mesh(mesh.devices.reshape(4, 4, 8, 4), (OUTER, INNER) + PLANE)
    placed = (
        P(PLANE, DP),
        P(DP),
        P(DP, PLANE),
        P(PLANE, DP),
        P(PLANE, None),
    )
    return jax.shard_map(
        on_device,
        mesh=split,
        in_specs=placed,
        out_specs=(P(PLANE, DP), P(PLANE)),
        check_vma=False,
    )
```

```python
import jax
import jax.numpy as jnp
from jax import lax
from jax.experimental import pallas as pl
from jax.experimental.pallas import tpu as pltpu
from jax.sharding import PartitionSpec as P

BLOCK = 64
PLANE = ("latent", "section")
OUTER, INNER = "dp_outer", "dp_inner"
DP = (OUTER, INNER)
GROUPS = 32
SHARDS = 16
LOCAL = 32
ROWS = 512
FEATURES = 288
HALF = FEATURES // 2
NAMED = 4
QUARTERS = 4
SHARE = 16
MAIN = QUARTERS * SHARE
EXTRA = 16
MAIN_SLOTS = GROUPS * MAIN
EXTRA_SLOTS = GROUPS * EXTRA
SLOTS = MAIN_SLOTS + EXTRA_SLOTS
PACKED = HALF + 3 * EXTRA
PAIRS = GROUPS // 2
STAGE = 4
LANE_TILES = SLOTS // 128
CHUNK_TILES = 5
CHUNK_ROWS = 16 * CHUNK_TILES

NT = (((1,), (1,)), ((), ()))
F32 = jnp.float32
BF16 = jnp.bfloat16


def mm(a, b):
    return jnp.dot(a, b, preferred_element_type=F32)


def mm_nt(a, b):
    return lax.dot_general(a, b, NT, preferred_element_type=F32)


def identity(n):
    rows = lax.broadcasted_iota(jnp.int32, (n, n), 0)
    return jnp.where(rows == lax.broadcasted_iota(jnp.int32, (n, n), 1), 1.0, 0.0).astype(BF16)


def lane_offset(tile, width=128):
    return pl.ds(pl.multiple_of(tile * width, width), width)


def exchange(a, b, width):
    kind = jnp.int16 if a.dtype == BF16 else jnp.int32
    lane = lax.broadcasted_iota(kind, a.shape, 1)
    even = jnp.bitwise_and(lane, jnp.full((), 2 * width - 1, kind)) < jnp.full((), width, kind)
    return jnp.where(even, a, pltpu.roll(b, width, 1)), jnp.where(even, pltpu.roll(a, 128 - width, 1), b)


def regroup(tiles):
    a0, a1 = exchange(tiles[0], tiles[1], 32)
    b0, b1 = exchange(tiles[2], tiles[3], 32)
    return *exchange(a0, b0, 16), *exchange(a1, b1, 16)


def ungroup(tiles):
    a0, b0 = exchange(tiles[0], tiles[1], 16)
    a1, b1 = exchange(tiles[2], tiles[3], 16)
    return *exchange(a0, a1, 32), *exchange(b0, b1, 32)


def store_pair(out_ref, pair, values):
    values = values.astype(BF16)
    first, second = exchange(values[:HALF], values[HALF:], MAIN)
    out_ref[pair, 0:HALF, :] = first
    out_ref[pair + PAIRS, 0:HALF, :] = second


def stage_copies(buffer_ref, out_ref, sems, stage):
    copies = []
    for side in range(2):
        devices = pl.ds(side * PAIRS + stage * STAGE, STAGE)
        copies.append(
            pltpu.make_async_copy(buffer_ref.at[devices], out_ref.at[devices], sems.at[2 * stage + side])
        )
    return copies


def start_stage(buffer_ref, out_ref, sems, done):
    if done % STAGE == 0:
        for copy in stage_copies(buffer_ref, out_ref, sems, done // STAGE - 1):
            copy.start()


def wait_stages(buffer_ref, out_ref, sems):
    for stage in range(PAIRS // STAGE):
        for copy in stage_copies(buffer_ref, out_ref, sems, stage):
            copy.wait()


def bias_column(bias_ref):
    rows = lax.broadcasted_iota(jnp.int32, (FEATURES, FEATURES), 0)
    lanes = lax.broadcasted_iota(jnp.int32, (FEATURES, FEATURES), 1)
    wide = jnp.broadcast_to(bias_ref[...].astype(F32).reshape(1, FEATURES), (FEATURES, FEATURES))
    return jnp.sum(jnp.where(rows == lanes, wide, 0.0), axis=1, keepdims=True)


def store_extra(out_ref, values):
    for part in range(3):
        piece = values[:, part * 128 : (part + 1) * 128].astype(BF16)
        out_ref[:, HALF + part * EXTRA : HALF + (part + 1) * EXTRA, :] = piece.reshape(GROUPS, EXTRA, 128)


def load_pair(in_ref, pair):
    return exchange(in_ref[pair, 0:HALF, :], in_ref[pair + PAIRS, 0:HALF, :], MAIN)


def unpack(in_ref, full_ref):
    for pair in range(PAIRS):
        top, bottom = load_pair(in_ref, pair)
        full_ref[0:HALF, pair * 128 : (pair + 1) * 128] = top
        full_ref[HALF:, pair * 128 : (pair + 1) * 128] = bottom
    unpack_extra(in_ref, full_ref)


def unpack_grouped(in_ref, full_ref):
    for quad in range(4):
        pairs = [load_pair(in_ref, 4 * quad + j) for j in range(4)]
        for half in range(2):
            tiles = regroup([pair[half] for pair in pairs])
            for quarter in range(QUARTERS):
                tile = 4 * quarter + quad
                full_ref[half * HALF : (half + 1) * HALF, tile * 128 : (tile + 1) * 128] = tiles[quarter]
    return unpack_extra(in_ref, full_ref)


def unpack_extra(in_ref, full_ref):
    eye = identity(128)
    turned, last = None, None
    for part in range(3):
        last = in_ref[:, HALF + part * EXTRA : HALF + (part + 1) * EXTRA, :].reshape(EXTRA_SLOTS, 128)
        turned = mm_nt(eye, last)
        height = min(128, FEATURES - part * 128)
        full_ref[part * 128 : part * 128 + height, MAIN_SLOTS:] = turned[:height].astype(BF16)
    return last, turned


def placed(slots, names, start, count):
    index = lax.broadcasted_iota(jnp.int16, (count, ROWS), 0) + jnp.int16(start)
    named = jnp.zeros((count, ROWS), BF16)
    for k in range(NAMED):
        named = jnp.where(index == jnp.broadcast_to(slots[k], index.shape), names[k], named)
    return named, jnp.minimum(named, BF16(1))


def prepare_kernel(act_ref, bias_ref, blocks_ref, out_ref, slots_ref, send_ref, sems):
    blocks = blocks_ref[...]
    group = lax.shift_right_logical(blocks, 3)
    local = jnp.bitwise_and(blocks, LOCAL - 1)
    count = GROUPS * QUARTERS
    groups = lax.broadcasted_iota(jnp.int32, (count, ROWS), 0)
    hits = [groups == group[k : k + 1, :] for k in range(NAMED)]
    small = lax.broadcasted_iota(jnp.int16, (count, ROWS), 0)
    counts = jnp.zeros((count, ROWS), BF16)
    for k in range(NAMED):
        hit = small == jnp.broadcast_to(group[k : k + 1, :].astype(jnp.int16), small.shape)
        counts = counts + jnp.where(hit, BF16(1), BF16(0))
    before = lax.broadcasted_iota(jnp.int16, (ROWS, ROWS), 0) < lax.broadcasted_iota(jnp.int16, (ROWS, ROWS), 1)
    earlier = mm(counts, jnp.where(before, BF16(1), BF16(0)))
    beyond = jnp.maximum(mm(counts, jnp.ones((ROWS, 128), BF16)) - SHARE, 0.0).astype(BF16)
    one = lax.broadcasted_iota(jnp.int32, (count, count), 0)
    other = lax.broadcasted_iota(jnp.int32, (count, count), 1)
    same = lax.shift_right_logical(one, 2) == lax.shift_right_logical(other, 2)
    offset = mm(jnp.where(same & (other < one), 1.0, 0.0).astype(BF16), beyond)
    table = earlier + 1024.0 * jnp.concatenate([offset] * (ROWS // 128), axis=1)
    slots, names, most = [], [], jnp.zeros((1, ROWS), jnp.int32)
    for k in range(NAMED):
        mine = group[k : k + 1, :]
        found = jnp.sum(jnp.where(hits[k], table, 0.0), axis=0, keepdims=True).astype(jnp.int32)
        rank = jnp.bitwise_and(found, 1023)
        for previous in range(k):
            rank = rank + jnp.where(group[previous : previous + 1, :] == mine, 1, 0)
        target = lax.shift_right_logical(mine, 2)
        place = (jnp.bitwise_and(target, PAIRS - 1) * 2 + lax.shift_right_logical(target, 4)) * MAIN
        main = place + jnp.bitwise_and(mine, QUARTERS - 1) * SHARE + rank
        extra = lax.shift_right_logical(found, 10) + rank - SHARE
        late = jnp.where(extra < EXTRA, MAIN_SLOTS + target * EXTRA + extra, -1)
        slots.append(jnp.where(rank < SHARE, main, late))
        names.append((local[k : k + 1, :] + 1).astype(F32).astype(BF16))
        most = jnp.maximum(most, jnp.where(rank < SHARE, 0, extra))
    over = jnp.where(jnp.max(most, axis=1, keepdims=True) >= EXTRA, 1.0, 0.0)
    shifted = (act_ref[...].astype(F32) - bias_column(bias_ref)).astype(BF16)

    for k in range(NAMED):
        slots_ref[k : k + 1, :] = slots[k]
    slots_ref[NAMED:, :] = jnp.zeros((8 - NAMED, ROWS), jnp.int32)
    slots = [slot.astype(jnp.int16) for slot in slots]
    named, place = placed(slots, names, MAIN_SLOTS, EXTRA_SLOTS)
    padded = jnp.concatenate([shifted, jnp.zeros((96, ROWS), BF16)], axis=0)
    values = mm_nt(place, padded)
    store_extra(send_ref, values)
    lane = lax.broadcasted_iota(jnp.int32, (EXTRA_SLOTS, 128), 1)
    ids = mm(named, jnp.ones((ROWS, 128), BF16))
    last = jnp.where(lane == 32, ids, values[:, 256:])
    row = lax.broadcasted_iota(jnp.int32, (EXTRA, 128), 0)
    high = lax.broadcasted_iota(jnp.int32, (EXTRA, 128), 1) >= MAIN
    flag = jnp.broadcast_to(over, (EXTRA, 128))
    for double in range(PAIRS // 2):
        named, place = placed(slots, names, double * 256, 256)
        values = mm_nt(shifted, place)
        ids = mm_nt(jnp.ones((EXTRA, ROWS), BF16), named)
        for side in range(2):
            pair = 2 * double + side
            store_pair(send_ref, pair, values[:, side * 128 : (side + 1) * 128])
            for half in range(2):
                device = pair + half * PAIRS
                mine = ids[:, side * 128 : (side + 1) * 128]
                mine = mine if half else pltpu.roll(mine, MAIN, 1)
                tile = last[device * EXTRA : (device + 1) * EXTRA]
                tile = jnp.where(high & (row == 0), mine, tile)
                tile = jnp.where(high & (row == 1), flag, tile)
                send_ref[device, HALF + 2 * EXTRA :, :] = tile.astype(BF16)
        start_stage(send_ref, out_ref, sems, 2 * double + 2)
    wait_stages(send_ref, out_ref, sems)


def encode_kernel(recv_ref, enc_ref, rest_ref, out_ref, ids_ref, over_ref, full_ref):
    last, turned = unpack_grouped(recv_ref, full_ref)
    pick = lax.broadcasted_iota(jnp.int32, (2 * GROUPS, EXTRA_SLOTS), 0)
    column = lax.broadcasted_iota(jnp.int32, (2 * GROUPS, EXTRA_SLOTS), 1)
    wanted = jnp.where(pick < GROUPS, pick * EXTRA, (pick - GROUPS) * EXTRA + 1)
    rows = mm(jnp.where(column == wanted, 1.0, 0.0).astype(BF16), last)
    first, second = rows[:PAIRS], rows[PAIRS:GROUPS]
    low = lax.broadcasted_iota(jnp.int32, (PAIRS, 128), 1) < MAIN
    named = jnp.where(low, pltpu.roll(first, MAIN, 1), second)
    picked = [[named[4 * quad + j : 4 * quad + j + 1] for quad in range(4)] for j in range(4)]
    tiles = regroup([jnp.concatenate(some, axis=0) for some in picked])
    for quarter in range(QUARTERS):
        ids_ref[4 * quarter : 4 * quarter + 4, :] = tiles[quarter]
    for part in range(EXTRA_SLOTS // 128):
        ids_ref[PAIRS + part : PAIRS + part + 1, :] = turned[32:33, part * 128 : (part + 1) * 128]
    ids_ref[LANE_TILES:, :] = jnp.zeros((24 - LANE_TILES, 128), F32)
    flags = jnp.where(lax.broadcasted_iota(jnp.int32, (GROUPS, 128), 1) == MAIN, rows[GROUPS:], 0.0)
    flag = jnp.max(jnp.max(flags, axis=1, keepdims=True), axis=0, keepdims=True)
    over_ref[0, 0] = jnp.max(flag).astype(jnp.int32)

    for tile in range(LANE_TILES // 2):
        lanes = slice(tile * 256, (tile + 1) * 256)
        ids = jnp.concatenate([ids_ref[2 * tile : 2 * tile + 1, :], ids_ref[2 * tile + 1 : 2 * tile + 2, :]], axis=1)
        code = ids.astype(jnp.int32) - 1
        main = tile < PAIRS // 2
        quarter = tile // 2 if main else 0
        first, held = (8 * quarter, 8) if main else (0, LOCAL)
        part = mm(enc_ref[first * BLOCK : (first + held) * BLOCK, 0:256], full_ref[0:256, lanes])
        total = jnp.zeros((BLOCK, 256), F32)
        for b in range(held):
            total = jnp.where(code == first + b, part[b * BLOCK : (b + 1) * BLOCK], total)
        rest = full_ref[256:, lanes]
        member = jnp.broadcast_to(jnp.bitwise_and(code, 7), (32, 256))
        spread = jnp.concatenate([jnp.where(member == m, rest, BF16(0)) for m in range(8)], axis=0)
        if main:
            more = mm(rest_ref[quarter * BLOCK : (quarter + 1) * BLOCK, :], spread)
        else:
            part = mm(rest_ref[...], spread)
            more = jnp.zeros((BLOCK, 256), F32)
            for g in range(QUARTERS):
                wanted = lax.shift_right_arithmetic(code, 3) == g
                more = jnp.where(wanted, part[g * BLOCK : (g + 1) * BLOCK], more)
        total = total + more
        for half in range(2):
            lane_tile = 2 * tile + half
            slot_row = (lane_tile % CHUNK_TILES) * 16
            for quarter in range(4):
                piece = total[quarter * 16 : (quarter + 1) * 16, half * 128 : (half + 1) * 128]
                out_ref[quarter + 4 * (lane_tile // CHUNK_TILES), slot_row : slot_row + 16, :] = piece.astype(BF16)


def load_codes(codes_ref, full_ref):
    for tile in range(LANE_TILES):
        for quarter in range(4):
            full_ref[quarter * 16 : (quarter + 1) * 16, tile * 128 : (tile + 1) * 128] = codes_ref[
                quarter + 4 * (tile // CHUNK_TILES),
                (tile % CHUNK_TILES) * 16 : (tile % CHUNK_TILES + 1) * 16,
                :,
            ]


def decode_kernel(codes_ref, ids_ref, weights_ref, send_ref, full_ref, extra_ref, dec_ref, sems):
    fetches = []
    for quarter in range(QUARTERS):
        lanes = pl.ds(quarter * 8 * BLOCK, 8 * BLOCK)
        fetches.append(
            pltpu.make_async_copy(weights_ref.at[:, lanes], dec_ref.at[:, lanes], sems.at[quarter])
        )
        fetches[-1].start()
    load_codes(codes_ref, full_ref)

    def contribution(tile):
        codes = full_ref[:, tile * 256 : (tile + 1) * 256]
        ids = jnp.concatenate([ids_ref[2 * tile : 2 * tile + 1, :], ids_ref[2 * tile + 1 : 2 * tile + 2, :]], axis=1)
        ids = jnp.broadcast_to(ids, (BLOCK, 256)).astype(BF16)
        main = tile < PAIRS // 2
        first, held = (8 * (tile // 2), 8) if main else (0, LOCAL)
        spread = [jnp.where(ids == BF16(b + 1), codes, BF16(0)) for b in range(first, first + held)]
        weights = dec_ref[:, first * BLOCK : (first + held) * BLOCK]
        return mm(weights, jnp.concatenate(spread, axis=0)).astype(BF16)

    for double in range(2):
        values = []
        for quarter in range(QUARTERS):
            if double == 0:
                fetches[quarter].wait()
            values.append(contribution(2 * quarter + double))
        for side in range(2):
            lanes = slice(side * 128, (side + 1) * 128)
            tops = ungroup([value[:HALF, lanes] for value in values])
            bottoms = ungroup([value[HALF:, lanes] for value in values])
            for j in range(4):
                pair = 8 * double + 4 * side + j
                first, second = exchange(tops[j], bottoms[j], MAIN)
                send_ref[pair, 0:HALF, :] = first
                send_ref[pair + PAIRS, 0:HALF, :] = second
    extra_ref[FEATURES:, :] = jnp.zeros((384 - FEATURES, EXTRA_SLOTS), BF16)
    for tile in range(PAIRS // 2, LANE_TILES // 2):
        start = tile * 256 - MAIN_SLOTS
        extra_ref[0:FEATURES, start : start + 256] = contribution(tile)
    store_extra(send_ref, mm_nt(identity(EXTRA_SLOTS), extra_ref[...]))


def combine_kernel(
    recv_ref, slots_ref, act_ref, bias_ref, out_ref, loss_ref, full_ref, place_ref, send_ref, sems
):
    slots = [slots_ref[k : k + 1, :].astype(jnp.int16) for k in range(NAMED)]
    ones = [jnp.ones((1, ROWS), BF16)] * NAMED
    for start in range(0, SLOTS, 256):
        place_ref[start : start + 256, :] = placed(slots, ones, start, 256)[0]
    unpack(recv_ref, full_ref)
    error = mm(full_ref[...], place_ref[...]) + bias_column(bias_ref) - act_ref[...].astype(F32)
    sent = error.astype(BF16)
    padded = jnp.concatenate([sent, jnp.zeros((96, ROWS), BF16)], axis=0)
    store_extra(send_ref, mm_nt(place_ref[MAIN_SLOTS:, :], padded))
    for double in range(PAIRS // 2):
        values = mm_nt(sent, place_ref[double * 256 : (double + 1) * 256, :])
        store_pair(send_ref, 2 * double, values[:, :128])
        store_pair(send_ref, 2 * double + 1, values[:, 128:])
        start_stage(send_ref, out_ref, sems, 2 * double + 2)
    loss = jnp.sum(error * error, axis=0, keepdims=True)
    for part in range(ROWS // 128):
        loss_ref[part : part + 1, :] = loss[:, part * 128 : (part + 1) * 128]
    wait_stages(send_ref, out_ref, sems)


def gradient_kernel(
    recv_ref, codes_ref, ids_ref, loss_ref, out_ref, out_loss_ref, full_ref, code_ref, grad_ref, sems
):
    out_loss_ref[...] = loss_ref[...]
    unpack_grouped(recv_ref, full_ref)
    load_codes(codes_ref, code_ref)
    ids = jnp.concatenate([ids_ref[tile : tile + 1, :] for tile in range(LANE_TILES)], axis=1)
    ids = jnp.broadcast_to(ids, (BLOCK, SLOTS)).astype(BF16)
    copies, begin = [], 0
    for start in range(0, LOCAL * BLOCK, 256):
        stop = start + 256
        width = MAIN_SLOTS // QUARTERS
        lanes = slice(start // 512 * width, (start // 512 + 1) * width)

        def both(values):
            return jnp.concatenate([values[:, lanes], values[:, MAIN_SLOTS:]], axis=1)

        near, codes = both(ids), both(code_ref)
        spread = [jnp.where(near == BF16(b + 1), codes, BF16(0)) for b in range(start // BLOCK, stop // BLOCK)]
        grad_ref[:, start:stop] = mm_nt(both(full_ref), jnp.concatenate(spread, axis=0)).astype(BF16)
        if stop in (LOCAL * BLOCK * 3 // 4, LOCAL * BLOCK):
            lanes = pl.ds(begin, stop - begin)
            copy = pltpu.make_async_copy(grad_ref.at[:, lanes], out_ref.at[:, lanes], sems.at[len(copies)])
            copy.start()
            copies.append(copy)
            begin = stop
    for copy in copies:
        copy.wait()


def call(kernel, out_shape, scratch, flops, name, megabytes, **specs):
    return pl.pallas_call(
        kernel,
        out_shape=out_shape,
        scratch_shapes=scratch,
        name=name,
        **specs,
        compiler_params=pltpu.CompilerParams(vmem_limit_bytes=megabytes * 1024 * 1024),
        cost_estimate=pl.CostEstimate(flops=flops, bytes_accessed=6_000_000, transcendentals=0),
    )


def shape(dims, dtype=BF16):
    return jax.ShapeDtypeStruct(dims, dtype)


def in_hbm(dims, dtype=BF16):
    return pltpu.HBM(dims, dtype)


def route(buffer):
    return lax.all_to_all(buffer, PLANE, split_axis=0, concat_axis=0, tiled=True)


def sum_codes(partial):
    shares = partial.reshape(4, SHARDS // 4 * CHUNK_ROWS, 128)
    received = lax.all_to_all(shares, INNER, split_axis=0, concat_axis=0, tiled=True)
    run = jnp.sum(received.astype(F32), axis=0).astype(BF16)
    runs = jnp.broadcast_to(run[None], shares.shape)
    runs = lax.all_to_all(runs, OUTER, split_axis=0, concat_axis=0, tiled=True)
    codes = jnp.maximum(jnp.sum(runs.astype(F32), axis=0), 0.0).astype(BF16)
    copies = jnp.broadcast_to(codes[None], shares.shape)
    return lax.all_to_all(copies, INNER, split_axis=0, concat_axis=0, tiled=True).reshape(partial.shape)


def sum_loss(part):
    return lax.psum(lax.psum(part, OUTER), INNER)


def padded_plan(activations, bias_dec, encoder, decoder, active_blocks):
    row_count, shard_width = activations.shape
    per_row = active_blocks.shape[1]
    groups = lax.axis_size(PLANE)
    local_blocks = encoder.shape[1] // BLOCK
    total_blocks = local_blocks * groups
    capacity = max(2, 2 * row_count * per_row // total_blocks)
    slot_count = total_blocks * capacity
    pair_blocks = active_blocks.reshape(-1)
    pair_iota = jnp.arange(pair_blocks.shape[0], dtype=jnp.int32)
    same_block = pair_blocks[:, None] == pair_blocks[None, :]
    earlier = pair_iota[None, :] < pair_iota[:, None]
    block_rank = jnp.sum((same_block & earlier).astype(jnp.int32), axis=1)
    slot_index = (pair_blocks * capacity + block_rank).reshape(row_count, per_row)
    slot_iota = jnp.arange(slot_count, dtype=jnp.int32)
    placement = jnp.zeros((slot_count, row_count), BF16)
    for which in range(per_row):
        placement = placement + (slot_index[:, which][None, :] == slot_iota[:, None]).astype(BF16)
    slot_shape = (groups, local_blocks, capacity, shard_width)

    def scatter_rows(values):
        filled = jnp.dot(placement, values, preferred_element_type=F32).astype(values.dtype)
        return filled.reshape(slot_shape)

    bias_wide = bias_dec.astype(F32)[None, :]
    shifted = (activations.astype(F32) - bias_wide).astype(BF16)
    received = route(scatter_rows(shifted))
    enc_local = encoder.reshape(shard_width, local_blocks, BLOCK)
    partial_pre = jnp.einsum("sbkd,dbl->sbkl", received, enc_local, preferred_element_type=F32)
    pre_total = lax.psum(partial_pre, DP)
    latent_codes = jnp.maximum(pre_total, 0.0).astype(BF16)
    dec_local = decoder.reshape(local_blocks, BLOCK, shard_width)
    contrib = jnp.einsum("sbkl,bld->sbkd", latent_codes, dec_local, preferred_element_type=F32).astype(BF16)
    returned = route(contrib).reshape(slot_count, shard_width)
    summed_rows = jnp.einsum("sr,sd->rd", placement, returned, preferred_element_type=F32)
    error = summed_rows + bias_wide - activations.astype(F32)
    row_loss = lax.psum(jnp.sum(error * error, axis=1), DP)
    error_sent = route(scatter_rows(error.astype(BF16)))
    gradient = jnp.einsum("sbkl,sbkd->bld", latent_codes, error_sent, preferred_element_type=F32)
    return gradient.reshape(local_blocks * BLOCK, shard_width).astype(BF16), row_loss


def on_device(activations, bias_dec, encoder, decoder, active_blocks):
    act = activations.T
    bias = bias_dec
    packed = in_hbm((GROUPS, PACKED, 128))
    full = pltpu.VMEM((FEATURES, SLOTS), BF16)
    sending = [pltpu.VMEM((GROUPS, PACKED, 128), BF16), pltpu.SemaphoreType.DMA((2 * PAIRS // STAGE,))]
    vmem, hbm = pl.BlockSpec(memory_space=pltpu.VMEM), pl.BlockSpec(memory_space=pltpu.HBM)
    spread_flops = 2 * FEATURES * SLOTS * LOCAL * BLOCK
    sent, slots = call(
        prepare_kernel,
        (packed, shape((8, ROWS), jnp.int32)),
        sending,
        2 * FEATURES * SLOTS * ROWS,
        "prepare",
        20,
        out_specs=(hbm, vmem),
    )(act, bias, active_blocks.T)
    received = route(sent)
    turned = encoder.T
    rest = turned[:, 256:].reshape(4, 8, BLOCK, 32).transpose(0, 2, 1, 3).reshape(4 * BLOCK, 256)
    partial, ids, over = call(
        encode_kernel,
        (shape((SHARDS, CHUNK_ROWS, 128)), shape((24, 128), F32), shape((1, 1), jnp.int32)),
        [full],
        spread_flops,
        "encode",
        20,
        out_specs=(vmem, vmem, pl.BlockSpec(memory_space=pltpu.SMEM)),
    )(received, turned, rest)
    codes = sum_codes(partial)
    sent = call(
        decode_kernel,
        shape((GROUPS, PACKED, 128)),
        [
            pltpu.VMEM((BLOCK, SLOTS), BF16),
            pltpu.VMEM((384, EXTRA_SLOTS), BF16),
            pltpu.VMEM((FEATURES, LOCAL * BLOCK), BF16),
            pltpu.SemaphoreType.DMA((QUARTERS,)),
        ],
        spread_flops,
        "decode",
        20,
        in_specs=(vmem, vmem, hbm),
    )(codes, ids, decoder.T)
    received = route(sent)
    sent, loss = call(
        combine_kernel,
        (packed, shape((ROWS // 128, 128), F32)),
        [full, pltpu.VMEM((SLOTS, ROWS), BF16)] + sending,
        4 * FEATURES * SLOTS * ROWS,
        "combine",
        20,
        out_specs=(hbm, vmem),
    )(received, slots, act, bias)
    received = route(sent)
    loss = sum_loss(loss)

    def packed_plan():
        gradient, row_loss = call(
            gradient_kernel,
            (in_hbm((FEATURES, LOCAL * BLOCK)), in_hbm((ROWS // 128, 128), F32)),
            [
                full,
                pltpu.VMEM((BLOCK, SLOTS), BF16),
                pltpu.VMEM((FEATURES, LOCAL * BLOCK), BF16),
                pltpu.SemaphoreType.DMA((2,)),
            ],
            spread_flops,
            "gradient",
            24,
            out_specs=(hbm, vmem),
        )(pltpu.with_memory_space_constraint(received, pltpu.VMEM), codes, ids, loss)
        return gradient.T, row_loss.reshape(ROWS)

    return lax.cond(
        over[0, 0] > 0,
        lambda: padded_plan(activations, bias_dec, encoder, decoder, active_blocks),
        packed_plan,
    )


def solution(mesh):
    split = jax.sharding.Mesh(mesh.devices.reshape(4, 4, 8, 4), (OUTER, INNER) + PLANE)
    placed = (
        P(PLANE, DP),
        P(DP),
        P(DP, PLANE),
        P(PLANE, DP),
        P(PLANE, None),
    )
    return jax.shard_map(
        on_device,
        mesh=split,
        in_specs=placed,
        out_specs=(P(PLANE, DP), P(PLANE)),
        check_vma=False,
    )
```

```python
import jax
import jax.numpy as jnp
from jax import lax
from jax.experimental import pallas as pl
from jax.experimental.pallas import tpu as pltpu
from jax.sharding import PartitionSpec as P

BLOCK = 64
PLANE = ("latent", "section")
OUTER, INNER = "dp_outer", "dp_inner"
DP = (OUTER, INNER)
GROUPS = 32
SHARDS = 16
LOCAL = 32
ROWS = 512
FEATURES = 288
HALF = FEATURES // 2
NAMED = 4
QUARTERS = 4
SHARE = 16
MAIN = QUARTERS * SHARE
EXTRA = 16
MAIN_SLOTS = GROUPS * MAIN
EXTRA_SLOTS = GROUPS * EXTRA
SLOTS = MAIN_SLOTS + EXTRA_SLOTS
PACKED = HALF + 3 * EXTRA
PAIRS = GROUPS // 2
STAGE = 4
LANE_TILES = SLOTS // 128
CHUNK_TILES = 5
CHUNK_ROWS = 16 * CHUNK_TILES

NT = (((1,), (1,)), ((), ()))
F32 = jnp.float32
BF16 = jnp.bfloat16


def mm(a, b):
    return jnp.dot(a, b, preferred_element_type=F32)


def mm_nt(a, b):
    return lax.dot_general(a, b, NT, preferred_element_type=F32)


def identity(n):
    rows = lax.broadcasted_iota(jnp.int32, (n, n), 0)
    return jnp.where(rows == lax.broadcasted_iota(jnp.int32, (n, n), 1), 1.0, 0.0).astype(BF16)


def lane_offset(tile, width=128):
    return pl.ds(pl.multiple_of(tile * width, width), width)


def exchange(a, b, width):
    kind = jnp.int16 if a.dtype == BF16 else jnp.int32
    lane = lax.broadcasted_iota(kind, a.shape, 1)
    even = jnp.bitwise_and(lane, jnp.full((), 2 * width - 1, kind)) < jnp.full((), width, kind)
    return jnp.where(even, a, pltpu.roll(b, width, 1)), jnp.where(even, pltpu.roll(a, 128 - width, 1), b)


def regroup(tiles):
    a0, a1 = exchange(tiles[0], tiles[1], 32)
    b0, b1 = exchange(tiles[2], tiles[3], 32)
    return *exchange(a0, b0, 16), *exchange(a1, b1, 16)


def ungroup(tiles):
    a0, b0 = exchange(tiles[0], tiles[1], 16)
    a1, b1 = exchange(tiles[2], tiles[3], 16)
    return *exchange(a0, a1, 32), *exchange(b0, b1, 32)


def store_pair(out_ref, pair, values):
    values = values.astype(BF16)
    first, second = exchange(values[:HALF], values[HALF:], MAIN)
    out_ref[pair, 0:HALF, :] = first
    out_ref[pair + PAIRS, 0:HALF, :] = second


def stage_copies(buffer_ref, out_ref, sems, stage):
    copies = []
    for side in range(2):
        devices = pl.ds(side * PAIRS + stage * STAGE, STAGE)
        copies.append(
            pltpu.make_async_copy(buffer_ref.at[devices], out_ref.at[devices], sems.at[2 * stage + side])
        )
    return copies


def start_stage(buffer_ref, out_ref, sems, done):
    if done % STAGE == 0:
        for copy in stage_copies(buffer_ref, out_ref, sems, done // STAGE - 1):
            copy.start()


def wait_stages(buffer_ref, out_ref, sems):
    for stage in range(PAIRS // STAGE):
        for copy in stage_copies(buffer_ref, out_ref, sems, stage):
            copy.wait()


def bias_column(bias_ref):
    rows = lax.broadcasted_iota(jnp.int32, (FEATURES, FEATURES), 0)
    lanes = lax.broadcasted_iota(jnp.int32, (FEATURES, FEATURES), 1)
    wide = jnp.broadcast_to(bias_ref[...].astype(F32).reshape(1, FEATURES), (FEATURES, FEATURES))
    return jnp.sum(jnp.where(rows == lanes, wide, 0.0), axis=1, keepdims=True)


def store_extra(out_ref, values):
    for part in range(3):
        piece = values[:, part * 128 : (part + 1) * 128].astype(BF16)
        out_ref[:, HALF + part * EXTRA : HALF + (part + 1) * EXTRA, :] = piece.reshape(GROUPS, EXTRA, 128)


def load_pair(in_ref, pair):
    return exchange(in_ref[pair, 0:HALF, :], in_ref[pair + PAIRS, 0:HALF, :], MAIN)


def unpack(in_ref, full_ref):
    for pair in range(PAIRS):
        top, bottom = load_pair(in_ref, pair)
        full_ref[0:HALF, pair * 128 : (pair + 1) * 128] = top
        full_ref[HALF:, pair * 128 : (pair + 1) * 128] = bottom
    unpack_extra(in_ref, full_ref)


def unpack_grouped(in_ref, full_ref):
    for quad in range(4):
        pairs = [load_pair(in_ref, 4 * quad + j) for j in range(4)]
        for half in range(2):
            tiles = regroup([pair[half] for pair in pairs])
            for quarter in range(QUARTERS):
                tile = 4 * quarter + quad
                full_ref[half * HALF : (half + 1) * HALF, tile * 128 : (tile + 1) * 128] = tiles[quarter]
    return unpack_extra(in_ref, full_ref)


def unpack_extra(in_ref, full_ref):
    eye = identity(128)
    turned, last = None, None
    for part in range(3):
        last = in_ref[:, HALF + part * EXTRA : HALF + (part + 1) * EXTRA, :].reshape(EXTRA_SLOTS, 128)
        turned = mm_nt(eye, last)
        height = min(128, FEATURES - part * 128)
        full_ref[part * 128 : part * 128 + height, MAIN_SLOTS:] = turned[:height].astype(BF16)
    return last, turned


def placed(slots, names, start, count):
    index = lax.broadcasted_iota(jnp.int16, (count, ROWS), 0) + jnp.int16(start)
    named = jnp.zeros((count, ROWS), BF16)
    for k in range(NAMED):
        named = jnp.where(index == jnp.broadcast_to(slots[k], index.shape), names[k], named)
    return named, jnp.minimum(named, BF16(1))


def prepare_kernel(act_ref, bias_ref, blocks_ref, out_ref, slots_ref, send_ref, sems):
    blocks = blocks_ref[...]
    group = lax.shift_right_logical(blocks, 3)
    local = jnp.bitwise_and(blocks, LOCAL - 1)
    count = GROUPS * QUARTERS
    groups = lax.broadcasted_iota(jnp.int32, (count, ROWS), 0)
    hits = [groups == group[k : k + 1, :] for k in range(NAMED)]
    small = lax.broadcasted_iota(jnp.int16, (count, ROWS), 0)
    counts = jnp.zeros((count, ROWS), BF16)
    for k in range(NAMED):
        hit = small == jnp.broadcast_to(group[k : k + 1, :].astype(jnp.int16), small.shape)
        counts = counts + jnp.where(hit, BF16(1), BF16(0))
    before = lax.broadcasted_iota(jnp.int16, (ROWS, ROWS), 0) < lax.broadcasted_iota(jnp.int16, (ROWS, ROWS), 1)
    earlier = mm(counts, jnp.where(before, BF16(1), BF16(0)))
    beyond = jnp.maximum(mm(counts, jnp.ones((ROWS, 128), BF16)) - SHARE, 0.0).astype(BF16)
    one = lax.broadcasted_iota(jnp.int32, (count, count), 0)
    other = lax.broadcasted_iota(jnp.int32, (count, count), 1)
    same = lax.shift_right_logical(one, 2) == lax.shift_right_logical(other, 2)
    offset = mm(jnp.where(same & (other < one), 1.0, 0.0).astype(BF16), beyond)
    table = earlier + 1024.0 * jnp.concatenate([offset] * (ROWS // 128), axis=1)
    slots, names, most = [], [], jnp.zeros((1, ROWS), jnp.int32)
    for k in range(NAMED):
        mine = group[k : k + 1, :]
        found = jnp.sum(jnp.where(hits[k], table, 0.0), axis=0, keepdims=True).astype(jnp.int32)
        rank = jnp.bitwise_and(found, 1023)
        for previous in range(k):
            rank = rank + jnp.where(group[previous : previous + 1, :] == mine, 1, 0)
        target = lax.shift_right_logical(mine, 2)
        place = (jnp.bitwise_and(target, PAIRS - 1) * 2 + lax.shift_right_logical(target, 4)) * MAIN
        main = place + jnp.bitwise_and(mine, QUARTERS - 1) * SHARE + rank
        extra = lax.shift_right_logical(found, 10) + rank - SHARE
        late = jnp.where(extra < EXTRA, MAIN_SLOTS + target * EXTRA + extra, -1)
        slots.append(jnp.where(rank < SHARE, main, late))
        names.append((local[k : k + 1, :] + 1).astype(F32).astype(BF16))
        most = jnp.maximum(most, jnp.where(rank < SHARE, 0, extra))
    over = jnp.where(jnp.max(most, axis=1, keepdims=True) >= EXTRA, 1.0, 0.0)
    shifted = (act_ref[...].astype(F32) - bias_column(bias_ref)).astype(BF16)

    for k in range(NAMED):
        slots_ref[k : k + 1, :] = slots[k]
    slots_ref[NAMED:, :] = jnp.zeros((8 - NAMED, ROWS), jnp.int32)
    slots = [slot.astype(jnp.int16) for slot in slots]
    named, place = placed(slots, names, MAIN_SLOTS, EXTRA_SLOTS)
    padded = jnp.concatenate([shifted, jnp.zeros((96, ROWS), BF16)], axis=0)
    values = mm_nt(place, padded)
    store_extra(send_ref, values)
    lane = lax.broadcasted_iota(jnp.int32, (EXTRA_SLOTS, 128), 1)
    ids = mm(named, jnp.ones((ROWS, 128), BF16))
    line = jnp.bitwise_and(lax.broadcasted_iota(jnp.int32, (EXTRA_SLOTS, 128), 0), EXTRA - 1)
    last = jnp.where(lane == 32, ids, values[:, 256:])
    last = jnp.where((lane >= MAIN) & (line == 1), jnp.broadcast_to(over, last.shape), last).astype(BF16)
    row = lax.broadcasted_iota(jnp.int16, (EXTRA, 128), 0)
    place_ids = row * jnp.int16(128) + lax.broadcasted_iota(jnp.int16, (EXTRA, 128), 1)
    named_here = (place_ids >= jnp.int16(MAIN)) & (place_ids < jnp.int16(128))
    for double in range(PAIRS // 2):
        named, place = placed(slots, names, double * 256, 256)
        values = mm_nt(shifted, place)
        ids = mm_nt(jnp.ones((EXTRA, ROWS), BF16), named).astype(BF16)
        for side in range(2):
            pair = 2 * double + side
            store_pair(send_ref, pair, values[:, side * 128 : (side + 1) * 128])
            for half in range(2):
                device = pair + half * PAIRS
                mine = ids[:, side * 128 : (side + 1) * 128]
                mine = mine if half else pltpu.roll(mine, MAIN, 1)
                tile = last[device * EXTRA : (device + 1) * EXTRA]
                send_ref[device, HALF + 2 * EXTRA :, :] = jnp.where(named_here, mine, tile)
        start_stage(send_ref, out_ref, sems, 2 * double + 2)
    wait_stages(send_ref, out_ref, sems)


def encode_kernel(recv_ref, enc_ref, rest_ref, out_ref, ids_ref, over_ref, full_ref):
    last, turned = unpack_grouped(recv_ref, full_ref)
    pick = lax.broadcasted_iota(jnp.int32, (2 * GROUPS, EXTRA_SLOTS), 0)
    column = lax.broadcasted_iota(jnp.int32, (2 * GROUPS, EXTRA_SLOTS), 1)
    wanted = jnp.where(pick < GROUPS, pick * EXTRA, (pick - GROUPS) * EXTRA + 1)
    rows = mm(jnp.where(column == wanted, 1.0, 0.0).astype(BF16), last)
    first, second = rows[:PAIRS], rows[PAIRS:GROUPS]
    low = lax.broadcasted_iota(jnp.int32, (PAIRS, 128), 1) < MAIN
    named = jnp.where(low, pltpu.roll(first, MAIN, 1), second)
    picked = [[named[4 * quad + j : 4 * quad + j + 1] for quad in range(4)] for j in range(4)]
    tiles = regroup([jnp.concatenate(some, axis=0) for some in picked])
    for quarter in range(QUARTERS):
        ids_ref[4 * quarter : 4 * quarter + 4, :] = tiles[quarter]
    for part in range(EXTRA_SLOTS // 128):
        ids_ref[PAIRS + part : PAIRS + part + 1, :] = turned[32:33, part * 128 : (part + 1) * 128]
    ids_ref[LANE_TILES:, :] = jnp.zeros((24 - LANE_TILES, 128), F32)
    flags = jnp.where(lax.broadcasted_iota(jnp.int32, (GROUPS, 128), 1) == MAIN, rows[GROUPS:], 0.0)
    flag = jnp.max(jnp.max(flags, axis=1, keepdims=True), axis=0, keepdims=True)
    over_ref[0, 0] = jnp.max(flag).astype(jnp.int32)

    for tile in range(LANE_TILES // 2):
        lanes = slice(tile * 256, (tile + 1) * 256)
        ids = jnp.concatenate([ids_ref[2 * tile : 2 * tile + 1, :], ids_ref[2 * tile + 1 : 2 * tile + 2, :]], axis=1)
        code = ids.astype(jnp.int32) - 1
        main = tile < PAIRS // 2
        quarter = tile // 2 if main else 0
        first, held = (8 * quarter, 8) if main else (0, LOCAL)
        part = mm(enc_ref[first * BLOCK : (first + held) * BLOCK, 0:256], full_ref[0:256, lanes])
        total = jnp.zeros((BLOCK, 256), F32)
        for b in range(held):
            total = jnp.where(code == first + b, part[b * BLOCK : (b + 1) * BLOCK], total)
        rest = full_ref[256:, lanes]
        member = jnp.broadcast_to(jnp.bitwise_and(code, 7), (32, 256))
        spread = jnp.concatenate([jnp.where(member == m, rest, BF16(0)) for m in range(8)], axis=0)
        if main:
            more = mm(rest_ref[quarter * BLOCK : (quarter + 1) * BLOCK, :], spread)
        else:
            part = mm(rest_ref[...], spread)
            more = jnp.zeros((BLOCK, 256), F32)
            for g in range(QUARTERS):
                wanted = lax.shift_right_arithmetic(code, 3) == g
                more = jnp.where(wanted, part[g * BLOCK : (g + 1) * BLOCK], more)
        total = total + more
        for half in range(2):
            lane_tile = 2 * tile + half
            slot_row = (lane_tile % CHUNK_TILES) * 16
            for quarter in range(4):
                piece = total[quarter * 16 : (quarter + 1) * 16, half * 128 : (half + 1) * 128]
                out_ref[quarter + 4 * (lane_tile // CHUNK_TILES), slot_row : slot_row + 16, :] = piece.astype(BF16)


def load_codes(codes_ref, full_ref):
    for tile in range(LANE_TILES):
        for quarter in range(4):
            full_ref[quarter * 16 : (quarter + 1) * 16, tile * 128 : (tile + 1) * 128] = codes_ref[
                quarter + 4 * (tile // CHUNK_TILES),
                (tile % CHUNK_TILES) * 16 : (tile % CHUNK_TILES + 1) * 16,
                :,
            ]


def decode_kernel(codes_ref, ids_ref, weights_ref, send_ref, full_ref, extra_ref, dec_ref, sems):
    fetches = []
    for quarter in range(QUARTERS):
        lanes = pl.ds(quarter * 8 * BLOCK, 8 * BLOCK)
        fetches.append(
            pltpu.make_async_copy(weights_ref.at[:, lanes], dec_ref.at[:, lanes], sems.at[quarter])
        )
        fetches[-1].start()
    load_codes(codes_ref, full_ref)

    def contribution(tile):
        codes = full_ref[:, tile * 256 : (tile + 1) * 256]
        ids = jnp.concatenate([ids_ref[2 * tile : 2 * tile + 1, :], ids_ref[2 * tile + 1 : 2 * tile + 2, :]], axis=1)
        ids = jnp.broadcast_to(ids, (BLOCK, 256)).astype(BF16)
        main = tile < PAIRS // 2
        first, held = (8 * (tile // 2), 8) if main else (0, LOCAL)
        spread = [jnp.where(ids == BF16(b + 1), codes, BF16(0)) for b in range(first, first + held)]
        weights = dec_ref[:, first * BLOCK : (first + held) * BLOCK]
        return mm(weights, jnp.concatenate(spread, axis=0)).astype(BF16)

    for double in range(2):
        values = []
        for quarter in range(QUARTERS):
            if double == 0:
                fetches[quarter].wait()
            values.append(contribution(2 * quarter + double))
        for side in range(2):
            lanes = slice(side * 128, (side + 1) * 128)
            tops = ungroup([value[:HALF, lanes] for value in values])
            bottoms = ungroup([value[HALF:, lanes] for value in values])
            for j in range(4):
                pair = 8 * double + 4 * side + j
                first, second = exchange(tops[j], bottoms[j], MAIN)
                send_ref[pair, 0:HALF, :] = first
                send_ref[pair + PAIRS, 0:HALF, :] = second
    extra_ref[FEATURES:, :] = jnp.zeros((384 - FEATURES, EXTRA_SLOTS), BF16)
    for tile in range(PAIRS // 2, LANE_TILES // 2):
        start = tile * 256 - MAIN_SLOTS
        extra_ref[0:FEATURES, start : start + 256] = contribution(tile)
    store_extra(send_ref, mm_nt(identity(EXTRA_SLOTS), extra_ref[...]))


def combine_kernel(
    recv_ref, slots_ref, act_ref, bias_ref, out_ref, loss_ref, full_ref, place_ref, send_ref, sems
):
    slots = [slots_ref[k : k + 1, :].astype(jnp.int16) for k in range(NAMED)]
    ones = [jnp.ones((1, ROWS), BF16)] * NAMED
    for start in range(0, SLOTS, 256):
        place_ref[start : start + 256, :] = placed(slots, ones, start, 256)[0]
    unpack(recv_ref, full_ref)
    error = mm(full_ref[...], place_ref[...]) + bias_column(bias_ref) - act_ref[...].astype(F32)
    sent = error.astype(BF16)
    padded = jnp.concatenate([sent, jnp.zeros((96, ROWS), BF16)], axis=0)
    store_extra(send_ref, mm_nt(place_ref[MAIN_SLOTS:, :], padded))
    for double in range(PAIRS // 2):
        values = mm_nt(sent, place_ref[double * 256 : (double + 1) * 256, :])
        store_pair(send_ref, 2 * double, values[:, :128])
        store_pair(send_ref, 2 * double + 1, values[:, 128:])
        start_stage(send_ref, out_ref, sems, 2 * double + 2)
    loss = jnp.sum(error * error, axis=0, keepdims=True)
    for part in range(ROWS // 128):
        loss_ref[part : part + 1, :] = loss[:, part * 128 : (part + 1) * 128]
    wait_stages(send_ref, out_ref, sems)


def gradient_kernel(
    recv_ref, codes_ref, ids_ref, loss_ref, out_ref, out_loss_ref, full_ref, code_ref, grad_ref, sems
):
    out_loss_ref[...] = loss_ref[...]
    unpack_grouped(recv_ref, full_ref)
    load_codes(codes_ref, code_ref)
    ids = jnp.concatenate([ids_ref[tile : tile + 1, :] for tile in range(LANE_TILES)], axis=1)
    ids = jnp.broadcast_to(ids, (BLOCK, SLOTS)).astype(BF16)
    copies, begin = [], 0
    for start in range(0, LOCAL * BLOCK, 256):
        stop = start + 256
        width = MAIN_SLOTS // QUARTERS
        lanes = slice(start // 512 * width, (start // 512 + 1) * width)

        def both(values):
            return jnp.concatenate([values[:, lanes], values[:, MAIN_SLOTS:]], axis=1)

        near, codes = both(ids), both(code_ref)
        spread = [jnp.where(near == BF16(b + 1), codes, BF16(0)) for b in range(start // BLOCK, stop // BLOCK)]
        grad_ref[:, start:stop] = mm_nt(both(full_ref), jnp.concatenate(spread, axis=0)).astype(BF16)
        if stop in (LOCAL * BLOCK * 3 // 4, LOCAL * BLOCK):
            lanes = pl.ds(begin, stop - begin)
            copy = pltpu.make_async_copy(grad_ref.at[:, lanes], out_ref.at[:, lanes], sems.at[len(copies)])
            copy.start()
            copies.append(copy)
            begin = stop
    for copy in copies:
        copy.wait()


def call(kernel, out_shape, scratch, flops, name, megabytes, **specs):
    return pl.pallas_call(
        kernel,
        out_shape=out_shape,
        scratch_shapes=scratch,
        name=name,
        **specs,
        compiler_params=pltpu.CompilerParams(vmem_limit_bytes=megabytes * 1024 * 1024),
        cost_estimate=pl.CostEstimate(flops=flops, bytes_accessed=6_000_000, transcendentals=0),
    )


def shape(dims, dtype=BF16):
    return jax.ShapeDtypeStruct(dims, dtype)


def in_hbm(dims, dtype=BF16):
    return pltpu.HBM(dims, dtype)


def route(buffer):
    return lax.all_to_all(buffer, PLANE, split_axis=0, concat_axis=0, tiled=True)


def sum_codes(partial):
    shares = partial.reshape(4, SHARDS // 4 * CHUNK_ROWS, 128)
    received = lax.all_to_all(shares, INNER, split_axis=0, concat_axis=0, tiled=True)
    total = lax.psum(jnp.sum(received.astype(F32), axis=0), OUTER)
    codes = jnp.maximum(total, 0.0).astype(BF16)
    copies = jnp.broadcast_to(codes[None], shares.shape)
    return lax.all_to_all(copies, INNER, split_axis=0, concat_axis=0, tiled=True).reshape(partial.shape)


def sum_loss(part):
    return lax.psum(lax.psum(part, OUTER), INNER)


def padded_plan(activations, bias_dec, encoder, decoder, active_blocks):
    row_count, shard_width = activations.shape
    per_row = active_blocks.shape[1]
    groups = lax.axis_size(PLANE)
    local_blocks = encoder.shape[1] // BLOCK
    total_blocks = local_blocks * groups
    capacity = max(2, 2 * row_count * per_row // total_blocks)
    slot_count = total_blocks * capacity
    pair_blocks = active_blocks.reshape(-1)
    pair_iota = jnp.arange(pair_blocks.shape[0], dtype=jnp.int32)
    same_block = pair_blocks[:, None] == pair_blocks[None, :]
    earlier = pair_iota[None, :] < pair_iota[:, None]
    block_rank = jnp.sum((same_block & earlier).astype(jnp.int32), axis=1)
    slot_index = (pair_blocks * capacity + block_rank).reshape(row_count, per_row)
    slot_iota = jnp.arange(slot_count, dtype=jnp.int32)
    placement = jnp.zeros((slot_count, row_count), BF16)
    for which in range(per_row):
        placement = placement + (slot_index[:, which][None, :] == slot_iota[:, None]).astype(BF16)
    slot_shape = (groups, local_blocks, capacity, shard_width)

    def scatter_rows(values):
        filled = jnp.dot(placement, values, preferred_element_type=F32).astype(values.dtype)
        return filled.reshape(slot_shape)

    bias_wide = bias_dec.astype(F32)[None, :]
    shifted = (activations.astype(F32) - bias_wide).astype(BF16)
    received = route(scatter_rows(shifted))
    enc_local = encoder.reshape(shard_width, local_blocks, BLOCK)
    partial_pre = jnp.einsum("sbkd,dbl->sbkl", received, enc_local, preferred_element_type=F32)
    pre_total = lax.psum(partial_pre, DP)
    latent_codes = jnp.maximum(pre_total, 0.0).astype(BF16)
    dec_local = decoder.reshape(local_blocks, BLOCK, shard_width)
    contrib = jnp.einsum("sbkl,bld->sbkd", latent_codes, dec_local, preferred_element_type=F32).astype(BF16)
    returned = route(contrib).reshape(slot_count, shard_width)
    summed_rows = jnp.einsum("sr,sd->rd", placement, returned, preferred_element_type=F32)
    error = summed_rows + bias_wide - activations.astype(F32)
    row_loss = lax.psum(jnp.sum(error * error, axis=1), DP)
    error_sent = route(scatter_rows(error.astype(BF16)))
    gradient = jnp.einsum("sbkl,sbkd->bld", latent_codes, error_sent, preferred_element_type=F32)
    return gradient.reshape(local_blocks * BLOCK, shard_width).astype(BF16), row_loss


def on_device(activations, bias_dec, encoder, decoder, active_blocks):
    act = activations.T
    bias = bias_dec
    packed = in_hbm((GROUPS, PACKED, 128))
    full = pltpu.VMEM((FEATURES, SLOTS), BF16)
    sending = [pltpu.VMEM((GROUPS, PACKED, 128), BF16), pltpu.SemaphoreType.DMA((2 * PAIRS // STAGE,))]
    vmem, hbm = pl.BlockSpec(memory_space=pltpu.VMEM), pl.BlockSpec(memory_space=pltpu.HBM)
    spread_flops = 2 * FEATURES * SLOTS * LOCAL * BLOCK
    sent, slots = call(
        prepare_kernel,
        (packed, shape((8, ROWS), jnp.int32)),
        sending,
        2 * FEATURES * SLOTS * ROWS,
        "prepare",
        20,
        out_specs=(hbm, vmem),
    )(act, bias, active_blocks.T)
    received = route(sent)
    turned = encoder.T
    rest = turned[:, 256:].reshape(4, 8, BLOCK, 32).transpose(0, 2, 1, 3).reshape(4 * BLOCK, 256)
    partial, ids, over = call(
        encode_kernel,
        (shape((SHARDS, CHUNK_ROWS, 128)), shape((24, 128), F32), shape((1, 1), jnp.int32)),
        [full],
        spread_flops,
        "encode",
        20,
        out_specs=(vmem, vmem, pl.BlockSpec(memory_space=pltpu.SMEM)),
    )(received, turned, rest)
    codes = sum_codes(partial)
    sent = call(
        decode_kernel,
        shape((GROUPS, PACKED, 128)),
        [
            pltpu.VMEM((BLOCK, SLOTS), BF16),
            pltpu.VMEM((384, EXTRA_SLOTS), BF16),
            pltpu.VMEM((FEATURES, LOCAL * BLOCK), BF16),
            pltpu.SemaphoreType.DMA((QUARTERS,)),
        ],
        spread_flops,
        "decode",
        20,
        in_specs=(vmem, vmem, hbm),
    )(codes, ids, decoder.T)
    received = route(sent)
    sent, loss = call(
        combine_kernel,
        (packed, shape((ROWS // 128, 128), F32)),
        [full, pltpu.VMEM((SLOTS, ROWS), BF16)] + sending,
        4 * FEATURES * SLOTS * ROWS,
        "combine",
        20,
        out_specs=(hbm, vmem),
    )(received, slots, act, bias)
    received = route(sent)
    loss = sum_loss(loss)

    def packed_plan():
        gradient, row_loss = call(
            gradient_kernel,
            (in_hbm((FEATURES, LOCAL * BLOCK)), in_hbm((ROWS // 128, 128), F32)),
            [
                full,
                pltpu.VMEM((BLOCK, SLOTS), BF16),
                pltpu.VMEM((FEATURES, LOCAL * BLOCK), BF16),
                pltpu.SemaphoreType.DMA((2,)),
            ],
            spread_flops,
            "gradient",
            24,
            out_specs=(hbm, vmem),
        )(pltpu.with_memory_space_constraint(received, pltpu.VMEM), codes, ids, loss)
        return gradient.T, row_loss.reshape(ROWS)

    return lax.cond(
        over[0, 0] > 0,
        lambda: padded_plan(activations, bias_dec, encoder, decoder, active_blocks),
        packed_plan,
    )


def solution(mesh):
    split = jax.sharding.Mesh(mesh.devices.reshape(4, 4, 8, 4), (OUTER, INNER) + PLANE)
    placed = (
        P(PLANE, DP),
        P(DP),
        P(DP, PLANE),
        P(PLANE, DP),
        P(PLANE, None),
    )
    return jax.shard_map(
        on_device,
        mesh=split,
        in_specs=placed,
        out_specs=(P(PLANE, DP), P(PLANE)),
        check_vma=False,
    )
```
